32 devices in a mesh: wave: 4 (over y, core), tm: 8 (over z, x).
Axes of the slice: x: 2, y: 2, z: 4, core: 2. Of those that a mesh axis runs over, the one named last changes fastest.
Arguments:
- field: float32 [4, 128, 2, 2, 8192], P(None, 'wave', None, None, 'tm'), may hold values from -3 to 3
- lit_count: int32 [4], replicated, may hold values from 32 to 128
- route_fibre: int32 [4, 64], replicated, may hold values from 0 to 3, as said below
- route_slot: int32 [4, 64], replicated, may hold values from 0 to 63, as said below
- dispersion: float32 [2, 4], replicated, may hold values from 20 to 42
- nonlinearity: float32 [2, 4], replicated, may hold values from 0.25 to 2.5
Outputs:
- received: float32 [4, 128, 2, 2, 8192], P(None, 'wave', None, None, 'tm')
The draws below stay inside these ranges and needn't reach their ends.
Inputs may be any that keep to these rules, and one draw needn't show every extreme that they name: `route_fibre`: together with route_slot it names every block of every fibre exactly once. `route_slot`: blocks 16 g .. 16 g + 15 of all fibres form channel group g. Of the 64 blocks of one group, at most 32 land in any one group, and every draw has pairs of groups with exactly 32.
All inputs are finite; a program needn't handle non-finite values.
Results may differ from the reference program's by a relative error of at most 0.0003.
Values sent between devices are 32-bit elements; how exact they have to be, the bound alone decides.
No kernel may reach another device: no remote copies, remote signals or barrier semaphores. Data moves between devices by JAX's collectives and lax.ppermute only.
A program may use at most 64 MiB of HBM per device.

```python
import math
import jax
import jax.numpy as jnp
from jax import lax

CH = 128
FIB = 4
BLK = 2
HALF = 2
NFFT = 2048
MARGIN = 512
VALID = 1024
TIME = 8192
NBLK = 64
WAVES = 4
GROUP_BLOCKS = 16
SENDS = 64
SLOTS = 32


def roadm_plan(key):
    base_key = jax.random.fold_in(key, 41)
    key_full, key_offset, key_order, key_place = jax.random.split(base_key, 4)
    half_slots = SLOTS // 2
    full_groups = jax.random.randint(key_full, (), 1, SENDS // SLOTS + 1)
    position = jnp.arange(SENDS)
    group_index = jnp.where(position < full_groups * SLOTS, position // SLOTS, full_groups + (position - full_groups * SLOTS) // half_slots)
    offsets = jax.random.permutation(key_offset, WAVES)
    target = (jnp.arange(WAVES)[:, None] + offsets[group_index][None, :]) % WAVES
    orders = jax.vmap(lambda subkey: jax.random.permutation(subkey, SENDS))(jax.random.split(key_order, WAVES))
    places = jax.vmap(lambda subkey: jax.random.permutation(subkey, SENDS))(jax.random.split(key_place, WAVES))
    target_flat = target.reshape(-1)
    serial = jnp.arange(WAVES * SENDS)
    earlier = (target_flat[None, :] == target_flat[:, None]) & (serial[None, :] < serial[:, None])
    arrival = jnp.sum(earlier.astype(jnp.int32), axis=1)
    landing = places[target_flat, arrival]
    source = orders.reshape(-1)
    source_group = serial // SENDS
    src_fibre = source // GROUP_BLOCKS
    src_block = source_group * GROUP_BLOCKS + source % GROUP_BLOCKS
    dst_fibre = (landing // GROUP_BLOCKS).astype(jnp.int32)
    dst_block = (target_flat * GROUP_BLOCKS + landing % GROUP_BLOCKS).astype(jnp.int32)
    fibre_map = jnp.zeros((FIB, NBLK), jnp.int32).at[src_fibre, src_block].set(dst_fibre)
    block_map = jnp.zeros((FIB, NBLK), jnp.int32).at[src_fibre, src_block].set(dst_block)
    return (fibre_map, block_map)


def draw_route_fibre(key, part):
    return roadm_plan(key)[0]


def draw_route_slot(key, part):
    return roadm_plan(key)[1]


def plant(entries, own_key, low, high):
    longest = entries.shape.index(max(entries.shape))
    spots = []
    for shift in (0, 1):
        where = [jax.random.randint(jax.random.fold_in(own_key, axis), (), 0, length) for axis, length in enumerate(entries.shape)]
        where[longest] = (where[longest] + shift) % entries.shape[longest]
        spots.append(tuple(where))
    return entries.at[spots[0]].set(low).at[spots[1]].set(high)


def levels(key, shape, cuts, least, top_value):
    loudness, own = 1.0, jax.random.fold_in(key, 6)
    for axis_at, blocks in cuts:
        steps = jnp.exp(jax.random.uniform(jax.random.fold_in(own, axis_at), (blocks,), jnp.float32, least / len(cuts), top_value / len(cuts)))
        loudness = loudness * jnp.repeat(steps, shape[axis_at] // blocks).reshape([-1 if axis == axis_at else 1 for axis in range(len(shape))])
    return loudness


def normal_values(stream_key, extent, scale, most, cuts=(), dtype=jnp.bfloat16):
    values = scale * jax.random.normal(stream_key, extent, jnp.float32)
    if cuts:
        values = values * levels(stream_key, extent, cuts, -0.22, 0.18)
    return jnp.clip(values, -most, most).astype(dtype)


def setup_inputs(seed: int = 0) -> dict:
    seeds = jax.random.split(jax.random.key(seed), 7)
    field = normal_values(seeds[0], (FIB, CH, 2, 2, TIME), 0.5, 3.0, ((1, 4), (4, 8)), jnp.float32)
    lit_count = plant(jax.random.randint(seeds[1], (FIB,), CH // 4, CH + 1), jax.random.fold_in(seeds[1], 1), CH // 4, CH).astype(jnp.int32)
    route_fibre = draw_route_fibre(jax.random.fold_in(seeds[6], 71), 0)
    route_slot = draw_route_slot(jax.random.fold_in(seeds[6], 71), 0)
    dispersion = jnp.clip(jax.random.uniform(seeds[4], (2, FIB), jnp.float32, 20.0, 42.0), 20.0, 42.0)
    nonlinearity = jnp.clip(jnp.exp(jax.random.uniform(seeds[5], (2, FIB), jnp.float32, math.log(0.25), math.log(2.5))), 0.25, 2.5)
    return dict(field=field, lit_count=lit_count, route_fibre=route_fibre, route_slot=route_slot, dispersion=dispersion, nonlinearity=nonlinearity)


def frequency_grid():
    index = jnp.arange(NFFT)
    signed = jnp.where(index < NFFT // 2, index, index - NFFT).astype(jnp.float32)
    return signed * (2.0 * jnp.pi / NFFT)


def fibre_step(arrays):
    waveform, spread, strength = arrays
    padded = jnp.concatenate([waveform[..., -MARGIN:], waveform, waveform[..., :MARGIN]], axis=-1)
    pieces = padded.reshape(CH, 2, 2, TIME // VALID + 1, VALID)
    blocks = jnp.concatenate([pieces[..., :-1, :], pieces[..., 1:, :]], axis=-1)
    complex_in = blocks[:, :, 0] + 1j * blocks[:, :, 1]
    spectrum = jnp.fft.fft(complex_in, axis=-1)
    omega = frequency_grid()
    channel = jnp.arange(CH).astype(jnp.float32)
    offsets = (jnp.pi / 2.0) * (2.0 * channel + 1.0 - CH) / CH
    theta = spread * (omega[None, :] ** 2 + 2.0 * omega[None, :] * offsets[:, None])
    spectrum = spectrum * jnp.exp(1j * theta)[:, None, None, :]
    inverse = jnp.fft.ifft(spectrum, axis=-1)[..., MARGIN:MARGIN + VALID].reshape(CH, 2, TIME)
    real_part = inverse.real
    imag_part = inverse.imag
    power = jnp.sum(real_part * real_part + imag_part * imag_part, axis=1)
    fibre_total = jnp.sum(power, axis=0)
    phase = strength * (2.0 * fibre_total[None, :] - power) / CH
    cosine = jnp.cos(phase)[:, None, :]
    sine = jnp.sin(phase)[:, None, :]
    return jnp.stack([real_part * cosine - imag_part * sine, real_part * sine + imag_part * cosine], axis=2)


def switch(waveform, route_fibre, route_slot):
    blocks = waveform.reshape(FIB * NBLK, BLK, 2, 2, TIME)
    target = (route_fibre * NBLK + route_slot).reshape(-1)
    moved = jnp.zeros_like(blocks).at[target].set(blocks)
    return moved.reshape(FIB, CH, 2, 2, TIME)


def reference(field, lit_count, route_fibre, route_slot, dispersion, nonlinearity):
    channel = jnp.arange(CH)
    lit_mask = channel[None, :] < lit_count[:, None]
    waveform = jnp.where(lit_mask[:, :, None, None, None], field, jnp.zeros_like(field))
    for span_index in range(2):
        if span_index == 1:
            waveform = switch(waveform, route_fibre, route_slot)
        for step_index in range(HALF):
            waveform = lax.map(fibre_step, (waveform, dispersion[span_index], nonlinearity[span_index]))
    return waveform
```

```python
import functools
import math

import jax
import jax.numpy as jnp
import numpy as np
from jax import lax
from jax.experimental import pallas as pl
from jax.experimental.pallas import tpu as pltpu
from jax.sharding import PartitionSpec as P

BLK = 2
FA = 16
FB = 128
NFFT = FA * FB
HALF = 2
MARGIN = 512
VALID = 1024
LEAD = MARGIN // FB
STEP = VALID // FB
SUB = 8
VMEM_BYTES = 40 * 1024 * 1024


def split_bf16(values):
    high = values.astype(jnp.bfloat16)
    low = (values - high.astype(np.float64)).astype(jnp.bfloat16)
    return high, low


def matrix_tables():
    index = np.arange(FB)
    angle = 2.0 * np.pi * (np.outer(index, index) % FB) / FB
    cos, sin = np.cos(angle), np.sin(angle)
    forward = np.block([[cos, -sin], [sin, cos]])
    inverse = np.block([[cos, sin], [-sin, cos]])
    tables = []
    for matrix in (forward, inverse):
        high, low = split_bf16(matrix)
        tables.append(np.concatenate([high, low, high], axis=0))
    return tables


def twist_table():
    angle = 2.0 * np.pi * np.outer(np.arange(FA), np.arange(FB)) / NFFT
    table = np.stack([np.cos(angle), np.sin(angle)]).astype(np.float32)
    return np.ascontiguousarray(np.broadcast_to(table[:, :, None, :], (2, FA, SUB, FB)))


def filter_tables(spread, channel, channels_total):
    index = np.arange(FA)[:, None] + FA * np.arange(FB)[None, :]
    signed = np.where(index < NFFT // 2, index, index - NFFT).astype(np.float32)
    omega = jnp.asarray(signed) * (2.0 * math.pi / NFFT)
    offsets = (math.pi / 2.0) * (2.0 * channel.astype(jnp.float32) + 1.0 - channels_total)
    offsets = offsets / channels_total
    theta = spread[None, :, None] * (
        omega[:, None, :] ** 2 + 2.0 * omega[:, None, :] * offsets[None, :, None]
    )
    scale = 1.0 / NFFT
    return jnp.cos(theta) * scale, jnp.sin(theta) * scale


def cadd(a, b):
    return (a[0] + b[0], a[1] + b[1])


def csub(a, b):
    return (a[0] - b[0], a[1] - b[1])


def cturn(a, sign):
    return (-a[1], a[0]) if sign > 0 else (a[1], -a[0])


def croot(a, m, sign):
    m %= FA
    if m == 0:
        return a
    if m == 4:
        return cturn(a, sign)
    if m in (2, 6):
        h = np.float32(math.sqrt(0.5))
        c = h if m == 2 else -h
        s = h * sign
        if m == 2:
            if sign > 0:
                return ((a[0] - a[1]) * h, (a[0] + a[1]) * h)
            return ((a[0] + a[1]) * h, (a[1] - a[0]) * h)
        if sign > 0:
            return ((a[0] + a[1]) * (-h), (a[0] - a[1]) * h)
        return ((a[1] - a[0]) * h, (a[0] + a[1]) * (-h))
    c = np.float32(math.cos(2.0 * math.pi * m / FA))
    s = np.float32(sign * math.sin(2.0 * math.pi * m / FA))
    return (a[0] * c - a[1] * s, a[0] * s + a[1] * c)


def dft4(z, sign, keep=(0, 1, 2, 3)):
    even, odd = cadd(z[0], z[2]), cadd(z[1], z[3])
    out = {}
    if 0 in keep:
        out[0] = cadd(even, odd)
    if 2 in keep:
        out[2] = csub(even, odd)
    if 1 in keep or 3 in keep:
        base, turn = csub(z[0], z[2]), cturn(csub(z[1], z[3]), sign)
        if 1 in keep:
            out[1] = cadd(base, turn)
        if 3 in keep:
            out[3] = csub(base, turn)
    return out


def dft16(z, sign, keep=(0, 1, 2, 3)):
    inner = [dft4([z[4 * n1 + n2] for n1 in range(4)], sign) for n2 in range(4)]
    out = {}
    for k1 in range(4):
        column = [croot(inner[n2][k1], n2 * k1, sign) for n2 in range(4)]
        for k2, value in dft4(column, sign, keep).items():
            out[k1 + 4 * k2] = value
    return out


def sincos(x):
    n = jnp.round(x * np.float32(2.0 / math.pi))
    r = x - n * np.float32(1.5703125)
    r = r - n * np.float32(4.837512969970703125e-4)
    r = r - n * np.float32(7.54978995489188216e-8)
    q = n.astype(jnp.int32)
    r2 = r * r
    s = np.float32(-1.9515295891e-4) * r2 + np.float32(8.3321608736e-3)
    s = s * r2 + np.float32(-1.6666654611e-1)
    s = s * r2 * r + r
    c = np.float32(2.443315711809948e-5) * r2 + np.float32(-1.388731625493765e-3)
    c = c * r2 + np.float32(4.166664568298827e-2)
    c = c * r2 * r2 - np.float32(0.5) * r2 + np.float32(1.0)
    odd = (q & 1) == 1
    sine = jnp.where(odd, c, s)
    cosine = jnp.where(odd, s, c)
    sine = jnp.where((q & 2) == 2, -sine, sine)
    cosine = jnp.where(((q + 1) & 2) == 2, -cosine, cosine)
    return sine, cosine


def rotate_chunk(x_ref, q_ref, sel_ref, strength, tt, channels_total, fibres, slots, write):
    real, imag = x_ref[tt, 0], x_ref[tt, 1]
    power = real * real + imag * imag
    power = power[:slots] + power[slots:]
    if fibres == 1:
        total = q_ref[0, pl.ds(tt, 1), :]
    else:
        total = sel_ref[0] * q_ref[0, pl.ds(tt, 1), :]
        for f in range(1, fibres):
            total = total + sel_ref[f] * q_ref[f, pl.ds(tt, 1), :]
    phase = strength * (2.0 * total - power) * np.float32(1.0 / channels_total)
    sine, cosine = sincos(phase)
    sine = jnp.concatenate([sine, sine], axis=0)
    cosine = jnp.concatenate([cosine, cosine], axis=0)
    write(real * cosine - imag * sine, real * sine + imag * cosine)


def final_kernel(x_ref, q_ref, sel_ref, strength_ref, o_ref, *, channels_total, fibres, slots):
    def body(tt, carry):
        def write(real, imag):
            o_ref[tt, 0] = real
            o_ref[tt, 1] = imag

        rotate_chunk(
            x_ref, q_ref, sel_ref, strength_ref[...], tt, channels_total, fibres, slots, write
        )
        return carry

    lax.fori_loop(0, x_ref.shape[0], body, 0)


def split_store(a_ref, base, column, value):
    high = value.astype(jnp.bfloat16)
    low = (value - high.astype(jnp.float32)).astype(jnp.bfloat16)
    rows = value.shape[0]
    a_ref[base : base + rows, column : column + FB] = high
    a_ref[base : base + rows, 2 * FB + column : 3 * FB + column] = high
    a_ref[base : base + rows, 4 * FB + column : 5 * FB + column] = low


def step_kernel(
    *refs, rotate, channels_total, fibres_in, fibres_out, slots
):
    if rotate:
        (x_ref, q_ref, selin_ref, strength_ref, selout_ref, fc_ref, fs_ref, tw_ref, wf_ref, wi_ref,
         u_ref, p_ref, xs_ref, a_ref, z_ref) = refs
    else:
        (x_ref, selout_ref, fc_ref, fs_ref, tw_ref, wf_ref, wi_ref,
         u_ref, p_ref, a_ref, z_ref) = refs
        xs_ref = x_ref
    chunks = x_ref.shape[0]
    groups = 2 * slots // SUB
    half = groups // 2

    if rotate:

        def turn(tt, carry):
            def write(real, imag):
                xs_ref[tt, 0] = real
                xs_ref[tt, 1] = imag

            rotate_chunk(
                x_ref, q_ref, selin_ref, strength_ref[...], tt, channels_total, fibres_in, slots,
                write,
            )
            return carry

        lax.fori_loop(0, chunks, turn, 0)

    def block(j, carry):
        places = []
        for a in range(FA):
            at = j * STEP + (a - LEAD)
            at = jnp.where(at < 0, at + chunks, at)
            places.append(jnp.where(at >= chunks, at - chunks, at))
        for g in range(groups):
            rows = slice(g * SUB, (g + 1) * SUB)
            z = [(xs_ref[at, 0, rows, :], xs_ref[at, 1, rows, :]) for at in places]
            y = dft16(z, -1)
            for i in range(FA // 2):
                pair = []
                for k in (2 * i, 2 * i + 1):
                    real, imag = y[k]
                    if k:
                        c, s = tw_ref[0, k], tw_ref[1, k]
                        real, imag = real * c + imag * s, imag * c - real * s
                    pair.append((real, imag))
                base = (g * FA + 2 * i) * SUB
                for part in range(2):
                    value = jnp.concatenate([pair[0][part], pair[1][part]], axis=0)
                    split_store(a_ref, base, part * FB, value)
        z_ref[...] = jnp.dot(a_ref[...], wf_ref[...], preferred_element_type=jnp.float32)
        for g in range(groups):
            rows = slice((g % half) * SUB, (g % half + 1) * SUB)
            for i in range(FA // 2):
                pair = []
                for k in (2 * i, 2 * i + 1):
                    at = (g * FA + k) * SUB
                    real, imag = z_ref[at : at + SUB, :FB], z_ref[at : at + SUB, FB:]
                    c, s = fc_ref[k, rows, :], fs_ref[k, rows, :]
                    pair.append((real * c - imag * s, real * s + imag * c))
                base = (g * FA + 2 * i) * SUB
                for part in range(2):
                    value = jnp.concatenate([pair[0][part], pair[1][part]], axis=0)
                    split_store(a_ref, base, part * FB, value)
        z_ref[...] = jnp.dot(a_ref[...], wi_ref[...], preferred_element_type=jnp.float32)
        for g in range(groups):
            rows = slice(g * SUB, (g + 1) * SUB)
            z = []
            for k in range(FA):
                at = (g * FA + k) * SUB
                real, imag = z_ref[at : at + SUB, :FB], z_ref[at : at + SUB, FB:]
                if k:
                    c, s = tw_ref[0, k], tw_ref[1, k]
                    real, imag = real * c - imag * s, real * s + imag * c
                z.append((real, imag))
            y = dft16(z, 1, keep=(1, 2))
            for k in range(STEP):
                u_ref[j * STEP + k, 0, rows, :] = y[LEAD + k][0]
                u_ref[j * STEP + k, 1, rows, :] = y[LEAD + k][1]
        for k in range(STEP):
            tt = j * STEP + k
            real, imag = u_ref[tt, 0], u_ref[tt, 1]
            power = real * real + imag * imag
            power = power[:slots] + power[slots:]
            for f in range(fibres_out):
                mine = power if fibres_out == 1 else power * selout_ref[f]
                p_ref[f, pl.ds(tt, 1), :] = jnp.sum(mine, axis=0, keepdims=True)
        return carry

    lax.fori_loop(0, chunks // STEP, block, 0)


def pack_kernel(lit_ref, x_ref, o_ref, *, units, slots):
    rows = 2 * slots
    span = 2 * STEP
    for g in range(o_ref.shape[0]):
        if units < slots:
            o_ref[g] = jnp.zeros(o_ref.shape[1:], jnp.float32)
        for u in range(units):
            lit = lit_ref[g * units + u] > 0
            for p in range(2):
                at = ((g * units + u) * 2 + p) * span
                value = jnp.where(lit, x_ref[at : at + span, :], 0.0)
                o_ref[g, pl.ds(p * slots + u, span, stride=rows), :] = value


def send_kernel(item_ref, x_ref, o_ref, *, units, slots):
    rows = 2 * slots
    span = 2 * STEP

    def body(n, carry):
        for c in range(BLK):
            channel = item_ref[n] * BLK + c
            g = channel // units
            u = channel - g * units
            for p in range(2):
                at = (c * 2 + p) * span
                o_ref[n, at : at + span, :] = x_ref[g, pl.ds(p * slots + u, span, stride=rows), :]
        return carry

    lax.fori_loop(0, o_ref.shape[0], body, 0)


def place_kernel(from_ref, x_ref, o_ref):
    def body(n, carry):
        o_ref[n] = x_ref[from_ref[n]]
        return carry

    lax.fori_loop(0, o_ref.shape[0], body, 0)


def params():
    return pltpu.CompilerParams(vmem_limit_bytes=VMEM_BYTES)


def in_vmem():
    return pl.BlockSpec(memory_space=pltpu.VMEM)


def in_smem():
    return pl.BlockSpec(memory_space=pltpu.SMEM)


def summed(values, rounds):
    for axis, bit in rounds:
        pairs = [(i, i ^ bit) for i in range(lax.axis_size(axis))]
        values = values + lax.ppermute(values, axis, pairs)
    return values


def route_tables(route_fibre, route_slot, groups, my_group, capacity):
    fibres = route_slot.shape[0]
    group_blocks = route_slot.shape[1] // groups
    sends = fibres * group_blocks

    def by_group(table):
        return table.reshape(fibres, groups, group_blocks).transpose(1, 0, 2).reshape(groups, sends)

    slot_all, fibre_all = by_group(route_slot), by_group(route_fibre)
    target_all = slot_all // group_blocks
    landing_all = fibre_all * group_blocks + slot_all % group_blocks
    position = jnp.arange(sends)
    earlier = (target_all[:, :, None] == target_all[:, None, :]) & (
        position[None, None, :] < position[None, :, None]
    )
    arrival_all = jnp.sum(earlier.astype(jnp.int32), axis=2)
    my_target = lax.dynamic_index_in_dim(target_all, my_group, 0, keepdims=False)
    my_arrival = lax.dynamic_index_in_dim(arrival_all, my_group, 0, keepdims=False)
    slot_index = my_target * capacity + my_arrival
    matches = slot_index[None, :] == jnp.arange(groups * capacity)[:, None]
    source_item = jnp.sum(jnp.where(matches, position[None, :], 0), axis=1)
    mine = target_all == my_group
    receive_slot = jnp.arange(groups)[:, None] * capacity + arrival_all
    hits = mine[:, :, None] & (landing_all[:, :, None] == position[None, None, :])
    take_from = jnp.sum(jnp.where(hits, receive_slot[:, :, None], 0), axis=(0, 1))
    return source_item.astype(jnp.int32), take_from.astype(jnp.int32)


def local(field, lit_count, route_fibre, route_slot, dispersion, nonlinearity):
    fibres, channels, samples = field.shape[0], field.shape[1], field.shape[-1]
    groups, times = lax.axis_size("wave"), lax.axis_size("tm")
    my_group, my_time = lax.axis_index("wave"), lax.axis_index("tm")
    channels_total = groups * channels
    units = fibres * channels // times
    slots = -(-units // SUB) * SUB
    rows = 2 * slots
    near = samples // FB
    chunks = times * near
    same_fibre = channels % units == 0
    group_blocks = channels // BLK
    sends = fibres * group_blocks
    capacity = 2 * sends // groups

    unit = my_time * units + jnp.minimum(jnp.arange(slots), units - 1)
    in_fibre = unit // channels
    in_channel = my_group * channels + unit % channels
    in_block = in_channel // BLK
    out_fibre = route_fibre[in_fibre, in_block]
    out_channel = route_slot[in_fibre, in_block] * BLK + in_channel % BLK
    real_slot = jnp.arange(slots) < units

    def wide(values):
        return jnp.broadcast_to(values.astype(jnp.float32)[..., None], values.shape + (FB,))

    def selection(fibre):
        chosen = (fibre[None, :] == jnp.arange(fibres)[:, None]) & real_slot[None, :]
        return wide(chosen)

    spans = []
    for span, (fibre, channel) in enumerate(((in_fibre, in_channel), (out_fibre, out_channel))):
        spread, strength = dispersion[span][fibre], nonlinearity[span][fibre]
        fc, fs = filter_tables(spread, channel, channels_total)
        spans.append((fc, fs, wide(strength), selection(fibre)))
    source_item, take_from = route_tables(route_fibre, route_slot, groups, my_group, capacity)

    wave_rounds = [("wave", 1 << b) for b in range(groups.bit_length() - 1)]
    time_rounds = [("tm", 1 << b) for b in range(times.bit_length() - 1)]
    shared = channels // units if same_fibre else 0
    fibre_rounds = [("tm", 1 << b) for b in range(shared.bit_length() - 1)]

    lit_mask = (my_group * channels + jnp.arange(channels))[None, :] < lit_count[:, None]
    lit = lit_mask.reshape(-1).astype(jnp.int32)

    def natural_rows(values):
        split = values.reshape(fibres, channels, 2, 2, near, FB)
        return split.transpose(0, 1, 2, 4, 3, 5).reshape(-1, FB)

    packed = pl.pallas_call(
        functools.partial(pack_kernel, units=units, slots=slots),
        out_shape=jax.ShapeDtypeStruct((times, 2 * near * rows, FB), jnp.float32),
        in_specs=[in_smem(), in_vmem()],
        out_specs=in_vmem(),
        compiler_params=params(),
        name="pack",
    )(lit, natural_rows(field))
    wave_form = lax.all_to_all(packed, "tm", split_axis=0, concat_axis=0, tiled=True)
    wave_form = wave_form.reshape(chunks, 2, rows, FB)

    twist = jnp.asarray(twist_table())
    forward, inverse = (jnp.asarray(table) for table in matrix_tables())
    total, q_fibres, q_spec = None, 0, None
    for step in range(2 * HALF):
        span = step // HALF
        fc, fs, strength, select = spans[span]
        fibres_out = 1 if (span == 0 and same_fibre) else fibres
        rotate = step > 0
        operands = [wave_form]
        if rotate:
            operands += [total, spans[(step - 1) // HALF][3], spans[(step - 1) // HALF][2]]
        operands += [select, fc, fs, twist, forward, inverse]
        scratch = [
            pltpu.VMEM((FA * rows, 6 * FB), jnp.bfloat16),
            pltpu.VMEM((FA * rows, 2 * FB), jnp.float32),
        ]
        if rotate:
            scratch = [pltpu.VMEM(wave_form.shape, jnp.float32)] + scratch
        wave_form, partial = pl.pallas_call(
            functools.partial(
                step_kernel, rotate=rotate, channels_total=channels_total, fibres_in=q_fibres,
                fibres_out=fibres_out, slots=slots,
            ),
            out_shape=(
                jax.ShapeDtypeStruct(wave_form.shape, jnp.float32),
                jax.ShapeDtypeStruct((fibres_out, chunks, FB), jnp.float32),
            ),
            in_specs=[in_vmem()] * len(operands),
            out_specs=(in_vmem(), in_vmem()),
            scratch_shapes=scratch,
            compiler_params=params(),
            name="step",
        )(*operands)
        rounds = fibre_rounds if fibres_out == 1 else time_rounds
        total, q_fibres = summed(partial, wave_rounds + rounds), fibres_out

    _, _, strength, select = spans[1]
    finished = pl.pallas_call(
        functools.partial(
            final_kernel, channels_total=channels_total, fibres=q_fibres, slots=slots
        ),
        out_shape=jax.ShapeDtypeStruct(wave_form.shape, jnp.float32),
        in_specs=[in_vmem()] * 4,
        out_specs=in_vmem(),
        compiler_params=params(),
        name="final",
    )(wave_form, total, select, strength)

    finished = finished.reshape(times, 2 * near * rows, FB)
    gathered = lax.all_to_all(finished, "tm", split_axis=0, concat_axis=0, tiled=True)
    outgoing = pl.pallas_call(
        functools.partial(send_kernel, units=units, slots=slots),
        out_shape=jax.ShapeDtypeStruct((groups * capacity, BLK * 4 * near, FB), jnp.float32),
        in_specs=[in_smem(), in_vmem()],
        out_specs=in_vmem(),
        compiler_params=params(),
        name="send",
    )(source_item, gathered)
    incoming = lax.all_to_all(outgoing, "wave", split_axis=0, concat_axis=0, tiled=True)
    placed = pl.pallas_call(
        place_kernel,
        out_shape=jax.ShapeDtypeStruct((sends, BLK * 4 * near, FB), jnp.float32),
        in_specs=[in_smem(), in_vmem()],
        out_specs=in_vmem(),
        compiler_params=params(),
        name="place",
    )(take_from, incoming)
    result = placed.reshape(fibres, channels, 2, near, 2, FB).transpose(0, 1, 2, 4, 3, 5)
    return result.reshape(fibres, channels, 2, 2, samples)


def solution(mesh):
    return jax.shard_map(
        local,
        mesh=mesh,
        in_specs=(P(None, "wave", None, None, "tm"), P(), P(), P(), P(), P()),
        out_specs=P(None, "wave", None, None, "tm"),
        check_vma=False,
    )
```

```python
import functools
import math

import jax
import jax.numpy as jnp
import numpy as np
from jax import lax
from jax.experimental import pallas as pl
from jax.experimental.pallas import tpu as pltpu
from jax.sharding import PartitionSpec as P

BLK = 2
FA = 16
FB = 128
NFFT = FA * FB
HALF = 2
MARGIN = 512
VALID = 1024
LEAD = MARGIN // FB
STEP = VALID // FB
SUB = 8
VMEM_BYTES = 40 * 1024 * 1024


def split_bf16(values):
    high = values.astype(jnp.bfloat16)
    low = (values - high.astype(np.float64)).astype(jnp.bfloat16)
    return high, low


def matrix_tables():
    index = np.arange(FB)
    angle = 2.0 * np.pi * (np.outer(index, index) % FB) / FB
    cos, sin = np.cos(angle), np.sin(angle)
    forward = np.block([[cos, -sin], [sin, cos]])
    inverse = np.block([[cos, sin], [-sin, cos]])
    tables = []
    for matrix in (forward, inverse):
        high, low = split_bf16(matrix)
        tables.append(np.concatenate([high, low, high], axis=0))
    return tables


def twist_table():
    angle = 2.0 * np.pi * np.outer(np.arange(FA), np.arange(FB)) / NFFT
    table = np.stack([np.cos(angle), np.sin(angle)]).astype(np.float32)
    return np.ascontiguousarray(np.broadcast_to(table[:, :, None, :], (2, FA, SUB, FB)))


def filter_tables(spread, channel, channels_total):
    index = np.arange(FA)[:, None] + FA * np.arange(FB)[None, :]
    signed = np.where(index < NFFT // 2, index, index - NFFT).astype(np.float32)
    omega = jnp.asarray(signed) * (2.0 * math.pi / NFFT)
    offsets = (math.pi / 2.0) * (2.0 * channel.astype(jnp.float32) + 1.0 - channels_total)
    offsets = offsets / channels_total
    theta = spread[None, :, None] * (
        omega[:, None, :] ** 2 + 2.0 * omega[:, None, :] * offsets[None, :, None]
    )
    scale = 1.0 / NFFT
    return jnp.cos(theta) * scale, jnp.sin(theta) * scale


def cadd(a, b):
    return (a[0] + b[0], a[1] + b[1])


def csub(a, b):
    return (a[0] - b[0], a[1] - b[1])


def cturn(a, sign):
    return (-a[1], a[0]) if sign > 0 else (a[1], -a[0])


def croot(a, m, sign):
    m %= FA
    if m == 0:
        return a
    if m == 4:
        return cturn(a, sign)
    if m in (2, 6):
        h = np.float32(math.sqrt(0.5))
        c = h if m == 2 else -h
        s = h * sign
        if m == 2:
            if sign > 0:
                return ((a[0] - a[1]) * h, (a[0] + a[1]) * h)
            return ((a[0] + a[1]) * h, (a[1] - a[0]) * h)
        if sign > 0:
            return ((a[0] + a[1]) * (-h), (a[0] - a[1]) * h)
        return ((a[1] - a[0]) * h, (a[0] + a[1]) * (-h))
    c = np.float32(math.cos(2.0 * math.pi * m / FA))
    s = np.float32(sign * math.sin(2.0 * math.pi * m / FA))
    return (a[0] * c - a[1] * s, a[0] * s + a[1] * c)


def dft4(z, sign, keep=(0, 1, 2, 3)):
    even, odd = cadd(z[0], z[2]), cadd(z[1], z[3])
    out = {}
    if 0 in keep:
        out[0] = cadd(even, odd)
    if 2 in keep:
        out[2] = csub(even, odd)
    if 1 in keep or 3 in keep:
        base, turn = csub(z[0], z[2]), cturn(csub(z[1], z[3]), sign)
        if 1 in keep:
            out[1] = cadd(base, turn)
        if 3 in keep:
            out[3] = csub(base, turn)
    return out


def dft16(z, sign, keep=(0, 1, 2, 3)):
    inner = [dft4([z[4 * n1 + n2] for n1 in range(4)], sign) for n2 in range(4)]
    out = {}
    for k1 in range(4):
        column = [croot(inner[n2][k1], n2 * k1, sign) for n2 in range(4)]
        for k2, value in dft4(column, sign, keep).items():
            out[k1 + 4 * k2] = value
    return out


def sincos(x):
    n = jnp.round(x * np.float32(2.0 / math.pi))
    r = x - n * np.float32(1.5703125)
    r = r - n * np.float32(4.837512969970703125e-4)
    r = r - n * np.float32(7.54978995489188216e-8)
    q = n.astype(jnp.int32)
    r2 = r * r
    s = np.float32(-1.9515295891e-4) * r2 + np.float32(8.3321608736e-3)
    s = s * r2 + np.float32(-1.6666654611e-1)
    s = s * r2 * r + r
    c = np.float32(2.443315711809948e-5) * r2 + np.float32(-1.388731625493765e-3)
    c = c * r2 + np.float32(4.166664568298827e-2)
    c = c * r2 * r2 - np.float32(0.5) * r2 + np.float32(1.0)
    odd = (q & 1) == 1
    sine = jnp.where(odd, c, s)
    cosine = jnp.where(odd, s, c)
    sine = jnp.where((q & 2) == 2, -sine, sine)
    cosine = jnp.where(((q + 1) & 2) == 2, -cosine, cosine)
    return sine, cosine


def rotate_chunk(x_ref, q_ref, sel_ref, strength, tt, channels_total, fibres, slots, write):
    real, imag = x_ref[tt, 0], x_ref[tt, 1]
    power = real * real + imag * imag
    power = power[:slots] + power[slots:]
    if fibres == 1:
        total = q_ref[0, pl.ds(tt, 1), :]
    else:
        total = sel_ref[0] * q_ref[0, pl.ds(tt, 1), :]
        for f in range(1, fibres):
            total = total + sel_ref[f] * q_ref[f, pl.ds(tt, 1), :]
    phase = strength * (2.0 * total - power) * np.float32(1.0 / channels_total)
    sine, cosine = sincos(phase)
    sine = jnp.concatenate([sine, sine], axis=0)
    cosine = jnp.concatenate([cosine, cosine], axis=0)
    write(real * cosine - imag * sine, real * sine + imag * cosine)


def split_store(a_ref, base, column, value):
    high = value.astype(jnp.bfloat16)
    low = (value - high.astype(jnp.float32)).astype(jnp.bfloat16)
    rows = value.shape[0]
    a_ref[base : base + rows, column : column + FB] = high
    a_ref[base : base + rows, 2 * FB + column : 3 * FB + column] = high
    a_ref[base : base + rows, 4 * FB + column : 5 * FB + column] = low


def step_kernel(
    *refs, rotate, hold, channels_total, fibres_in, fibres_out, slots
):
    refs = list(refs)
    x_ref = refs.pop(0)
    if rotate:
        q_ref, selin_ref, strength_ref = refs[:3]
        refs = refs[3:]
    selout_ref, fc_ref, fs_ref, tw_ref, wf_ref, wi_ref, u_ref, p_ref = refs[:8]
    refs = refs[8:]
    rest_ref = refs.pop(0) if hold else None
    xs_ref = refs.pop(0) if rotate else x_ref
    a_ref, z_ref = refs
    chunks = x_ref.shape[0]
    held = xs_ref.shape[2]
    groups = held // SUB
    half = slots // SUB

    if rotate:

        def turn(tt, carry):
            def write(real, imag):
                xs_ref[tt, 0] = real[:held]
                xs_ref[tt, 1] = imag[:held]
                if hold:
                    rest_ref[tt, 0] = real[held:]
                    rest_ref[tt, 1] = imag[held:]

            rotate_chunk(
                x_ref, q_ref, selin_ref, strength_ref[...], tt, channels_total, fibres_in, slots,
                write,
            )
            return carry

        lax.fori_loop(0, chunks, turn, 0)

    def block(j, carry):
        places = []
        for a in range(FA):
            at = j * STEP + (a - LEAD)
            at = jnp.where(at < 0, at + chunks, at)
            places.append(jnp.where(at >= chunks, at - chunks, at))
        for g in range(groups):
            rows = slice(g * SUB, (g + 1) * SUB)
            z = [(xs_ref[at, 0, rows, :], xs_ref[at, 1, rows, :]) for at in places]
            y = dft16(z, -1)
            for i in range(FA // 2):
                pair = []
                for k in (2 * i, 2 * i + 1):
                    real, imag = y[k]
                    if k:
                        c, s = tw_ref[0, k], tw_ref[1, k]
                        real, imag = real * c + imag * s, imag * c - real * s
                    pair.append((real, imag))
                base = (g * FA + 2 * i) * SUB
                for part in range(2):
                    value = jnp.concatenate([pair[0][part], pair[1][part]], axis=0)
                    split_store(a_ref, base, part * FB, value)
        z_ref[...] = jnp.dot(a_ref[...], wf_ref[...], preferred_element_type=jnp.float32)
        for g in range(groups):
            rows = slice((g % half) * SUB, (g % half + 1) * SUB)
            for i in range(FA // 2):
                pair = []
                for k in (2 * i, 2 * i + 1):
                    at = (g * FA + k) * SUB
                    real, imag = z_ref[at : at + SUB, :FB], z_ref[at : at + SUB, FB:]
                    c, s = fc_ref[k, rows, :], fs_ref[k, rows, :]
                    pair.append((real * c - imag * s, real * s + imag * c))
                base = (g * FA + 2 * i) * SUB
                for part in range(2):
                    value = jnp.concatenate([pair[0][part], pair[1][part]], axis=0)
                    split_store(a_ref, base, part * FB, value)
        z_ref[...] = jnp.dot(a_ref[...], wi_ref[...], preferred_element_type=jnp.float32)
        for g in range(groups):
            rows = slice(g * SUB, (g + 1) * SUB)
            z = []
            for k in range(FA):
                at = (g * FA + k) * SUB
                real, imag = z_ref[at : at + SUB, :FB], z_ref[at : at + SUB, FB:]
                if k:
                    c, s = tw_ref[0, k], tw_ref[1, k]
                    real, imag = real * c - imag * s, real * s + imag * c
                z.append((real, imag))
            y = dft16(z, 1, keep=(1, 2))
            for k in range(STEP):
                u_ref[j * STEP + k, 0, rows, :] = y[LEAD + k][0]
                u_ref[j * STEP + k, 1, rows, :] = y[LEAD + k][1]
        for k in range(STEP):
            tt = j * STEP + k
            real, imag = u_ref[tt, 0], u_ref[tt, 1]
            power = real * real + imag * imag
            if held > slots:
                power = power[:slots] + power[slots:]
            for f in range(fibres_out):
                mine = power if fibres_out == 1 else power * selout_ref[f]
                p_ref[f, pl.ds(tt, 1), :] = jnp.sum(mine, axis=0, keepdims=True)
        return carry

    lax.fori_loop(0, chunks // STEP, block, 0)


def pack_kernel(lit_ref, x_ref, o_ref, *, units, slots):
    rows = 2 * slots
    span = 2 * STEP
    for g in range(o_ref.shape[0]):
        if units < slots:
            o_ref[g] = jnp.zeros(o_ref.shape[1:], jnp.float32)
        for u in range(units):
            lit = lit_ref[g * units + u] > 0
            for p in range(2):
                at = ((g * units + u) * 2 + p) * span
                value = jnp.where(lit, x_ref[at : at + span, :], 0.0)
                o_ref[g, pl.ds(p * slots + u, span, stride=rows), :] = value


def send_kernel(item_ref, count_ref, x_ref, *o_refs, units, slots):
    capacity, near = o_refs[0].shape[0], o_refs[0].shape[1] // (2 * BLK)
    for s, o_ref in enumerate(o_refs):

        def body(n, carry, s=s, o_ref=o_ref):
            for c in range(BLK):
                channel = item_ref[s * capacity + n] * BLK + c
                g = channel // units
                u = channel - g * units
                for part in range(2):
                    at = (c * 2 + part) * near
                    o_ref[n, at : at + near, :] = x_ref[
                        g, pl.ds(part * slots + u, near, stride=2 * slots), :
                    ]
            return carry

        lax.fori_loop(0, count_ref[s], body, 0)


def place_kernel(from_ref, strength_ref, q_ref, *refs, channels_total, sources):
    in_refs, (o_ref, held_ref, sems) = refs[: 2 * sources], refs[2 * sources :]
    capacity, near = in_refs[0].shape[0], in_refs[0].shape[1] // (2 * BLK)
    copies = []
    for p in range(2):
        for s in range(sources):
            copies.append(
                pltpu.make_async_copy(
                    in_refs[p * sources + s],
                    held_ref.at[p, pl.ds(s * capacity, capacity)],
                    sems.at[p, s],
                )
            )
    for copy in copies:
        copy.start()
    for copy in copies:
        copy.wait()
    fibres = q_ref.shape[0]
    group_blocks = o_ref.shape[0] // fibres
    for f in range(fibres):
        total = 2.0 * q_ref[f]
        strength = strength_ref[f]

        def body(b, carry, f=f, total=total, strength=strength):
            n = f * group_blocks + b
            source = from_ref[n]
            for c in range(BLK):
                parts = []
                power = None
                for p in range(2):
                    at = c * 2 * near
                    real = held_ref[p, source, at : at + near, :]
                    imag = held_ref[p, source, at + near : at + 2 * near, :]
                    parts.append((real, imag))
                    mine = real * real + imag * imag
                    power = mine if power is None else power + mine
                phase = strength * (total - power) * np.float32(1.0 / channels_total)
                sine, cosine = sincos(phase)
                for p, (real, imag) in enumerate(parts):
                    at = (c * 2 + p) * 2 * near
                    o_ref[n, pl.ds(at, near, stride=2), :] = real * cosine - imag * sine
                    o_ref[n, pl.ds(at + 1, near, stride=2), :] = real * sine + imag * cosine
            return carry

        lax.fori_loop(0, group_blocks, body, 0)


def params():
    return pltpu.CompilerParams(vmem_limit_bytes=VMEM_BYTES)


def in_vmem():
    return pl.BlockSpec(memory_space=pltpu.VMEM)


def in_smem():
    return pl.BlockSpec(memory_space=pltpu.SMEM)


def summed(values, rounds):
    for axis, bit in rounds:
        pairs = [(i, i ^ bit) for i in range(lax.axis_size(axis))]
        values = values + lax.ppermute(values, axis, pairs)
    return values


def route_tables(route_fibre, route_slot, groups, my_group, capacity):
    fibres = route_slot.shape[0]
    group_blocks = route_slot.shape[1] // groups
    sends = fibres * group_blocks

    def by_group(table):
        return table.reshape(fibres, groups, group_blocks).transpose(1, 0, 2).reshape(groups, sends)

    slot_all, fibre_all = by_group(route_slot), by_group(route_fibre)
    target_all = slot_all // group_blocks
    landing_all = fibre_all * group_blocks + slot_all % group_blocks
    position = jnp.arange(sends)
    earlier = (target_all[:, :, None] == target_all[:, None, :]) & (
        position[None, None, :] < position[None, :, None]
    )
    arrival_all = jnp.sum(earlier.astype(jnp.int32), axis=2)
    my_target = lax.dynamic_index_in_dim(target_all, my_group, 0, keepdims=False)
    my_arrival = lax.dynamic_index_in_dim(arrival_all, my_group, 0, keepdims=False)
    partner = my_target ^ my_group
    slot_index = partner * capacity + my_arrival
    matches = slot_index[None, :] == jnp.arange(groups * capacity)[:, None]
    source_item = jnp.sum(jnp.where(matches, position[None, :], 0), axis=1)
    counts = jnp.sum((partner[None, :] == jnp.arange(groups)[:, None]).astype(jnp.int32), axis=1)
    mine = target_all == my_group
    receive_slot = (jnp.arange(groups) ^ my_group)[:, None] * capacity + arrival_all
    hits = mine[:, :, None] & (landing_all[:, :, None] == position[None, None, :])
    take_from = jnp.sum(jnp.where(hits, receive_slot[:, :, None], 0), axis=(0, 1))
    return source_item.astype(jnp.int32), counts, take_from.astype(jnp.int32)


def local_total(values, times, my_time, wave_rounds):
    bit = times // 2
    while bit:
        halves = values.reshape(values.shape[0], 2, -1, FB)
        high = (my_time // bit) % 2
        keep = lax.dynamic_index_in_dim(halves, high, 1, keepdims=False)
        give = lax.dynamic_index_in_dim(halves, 1 - high, 1, keepdims=False)
        pairs = [(i, i ^ bit) for i in range(times)]
        values = keep + lax.ppermute(give, "tm", pairs)
        bit //= 2
    return summed(values, wave_rounds)


def local(field, lit_count, route_fibre, route_slot, dispersion, nonlinearity):
    fibres, channels, samples = field.shape[0], field.shape[1], field.shape[-1]
    groups, times = lax.axis_size("wave"), lax.axis_size("tm")
    my_group, my_time = lax.axis_index("wave"), lax.axis_index("tm")
    channels_total = groups * channels
    units = fibres * channels // times
    slots = -(-units // SUB) * SUB
    rows = 2 * slots
    near = samples // FB
    chunks = times * near
    same_fibre = channels % units == 0
    group_blocks = channels // BLK
    sends = fibres * group_blocks
    capacity = 2 * sends // groups

    unit = my_time * units + jnp.minimum(jnp.arange(slots), units - 1)
    in_fibre = unit // channels
    in_channel = my_group * channels + unit % channels
    in_block = in_channel // BLK
    out_fibre = route_fibre[in_fibre, in_block]
    out_channel = route_slot[in_fibre, in_block] * BLK + in_channel % BLK
    real_slot = jnp.arange(slots) < units

    def wide(values):
        return jnp.broadcast_to(values.astype(jnp.float32)[..., None], values.shape + (FB,))

    def selection(fibre):
        chosen = (fibre[None, :] == jnp.arange(fibres)[:, None]) & real_slot[None, :]
        return wide(chosen)

    spans = []
    for span, (fibre, channel) in enumerate(((in_fibre, in_channel), (out_fibre, out_channel))):
        spread, strength = dispersion[span][fibre], nonlinearity[span][fibre]
        fc, fs = filter_tables(spread, channel, channels_total)
        spans.append((fc, fs, wide(strength), selection(fibre)))
    source_item, counts, take_from = route_tables(route_fibre, route_slot, groups, my_group, capacity)

    wave_rounds = [("wave", 1 << b) for b in range(groups.bit_length() - 1)]
    time_rounds = [("tm", 1 << b) for b in range(times.bit_length() - 1)]
    shared = channels // units if same_fibre else 0
    fibre_rounds = [("tm", 1 << b) for b in range(shared.bit_length() - 1)]

    lit_mask = (my_group * channels + jnp.arange(channels))[None, :] < lit_count[:, None]
    lit = lit_mask.reshape(-1).astype(jnp.int32)

    def natural_rows(values):
        split = values.reshape(fibres, channels, 2, 2, near, FB)
        return split.transpose(0, 1, 2, 4, 3, 5).reshape(-1, FB)

    packed = pl.pallas_call(
        functools.partial(pack_kernel, units=units, slots=slots),
        out_shape=jax.ShapeDtypeStruct((times, 2 * near * rows, FB), jnp.float32),
        in_specs=[in_smem(), in_vmem()],
        out_specs=in_vmem(),
        compiler_params=params(),
        name="pack",
    )(lit, natural_rows(field))
    wave_form = lax.all_to_all(packed, "tm", split_axis=0, concat_axis=0, tiled=True)
    wave_form = wave_form.reshape(chunks, 2, rows, FB)

    twist = jnp.asarray(twist_table())
    forward, inverse = (jnp.asarray(table) for table in matrix_tables())
    def dispersed(x, step, total, q_fibres, fibres_out, hold):
        fc, fs, _, select = spans[step // HALF]
        rotate = total is not None
        operands = [x]
        if rotate:
            operands += [total, spans[(step - 1) // HALF][3], spans[(step - 1) // HALF][2]]
        operands += [select, fc, fs, twist, forward, inverse]
        held = slots if hold else x.shape[2]
        part = jax.ShapeDtypeStruct((chunks, 2, held, FB), jnp.float32)
        outs = [part, jax.ShapeDtypeStruct((fibres_out, chunks, FB), jnp.float32)]
        outs += [part] if hold else []
        scratch = [pltpu.VMEM(part.shape, jnp.float32)] if rotate else []
        scratch += [
            pltpu.VMEM((FA * held, 6 * FB), jnp.bfloat16),
            pltpu.VMEM((FA * held, 2 * FB), jnp.float32),
        ]
        return pl.pallas_call(
            functools.partial(
                step_kernel, rotate=rotate, hold=hold, channels_total=channels_total,
                fibres_in=q_fibres, fibres_out=fibres_out, slots=slots,
            ),
            out_shape=tuple(outs),
            in_specs=[in_vmem()] * len(operands),
            out_specs=tuple([in_vmem()] * len(outs)),
            scratch_shapes=scratch,
            compiler_params=params(),
            name="step",
        )(*operands)

    total, q_fibres = None, 0
    for step in range(2 * HALF - 1):
        fibres_out = 1 if (step < HALF and same_fibre) else fibres
        wave_form, partial = dispersed(wave_form, step, total, q_fibres, fibres_out, False)
        rounds = fibre_rounds if fibres_out == 1 else time_rounds
        total, q_fibres = summed(partial, wave_rounds + rounds), fibres_out

    last = 2 * HALF - 1

    def to_times(values):
        values = values.reshape(times, 2 * near * slots, FB)
        return lax.all_to_all(values, "tm", split_axis=0, concat_axis=0, tiled=True)

    def to_groups(values):
        block = jax.ShapeDtypeStruct((capacity, BLK * 2 * near, FB), jnp.float32)
        outgoing = pl.pallas_call(
            functools.partial(send_kernel, units=units, slots=slots),
            out_shape=(block,) * groups,
            in_specs=[in_smem(), in_smem(), in_vmem()],
            out_specs=(in_vmem(),) * groups,
            compiler_params=params(),
            name="send",
        )(source_item, counts, values)
        moved = [outgoing[0]]
        for s in range(1, groups):
            moved.append(lax.ppermute(outgoing[s], "wave", [(i, i ^ s) for i in range(groups)]))
        return moved

    first, partial, rest = dispersed(wave_form, last, total, q_fibres, fibres, True)
    first = to_times(first)
    second, more = dispersed(rest, last, None, 0, fibres, False)
    second = to_times(second)
    own_total = local_total(partial + more, times, my_time, wave_rounds)
    blocks = to_groups(first) + to_groups(second)
    strength = jnp.broadcast_to(nonlinearity[1][:, None, None], (fibres, near, FB))
    placed = pl.pallas_call(
        functools.partial(place_kernel, channels_total=channels_total, sources=groups),
        out_shape=jax.ShapeDtypeStruct((sends, BLK * 4 * near, FB), jnp.float32),
        in_specs=[in_smem(), in_vmem(), in_vmem()]
        + [pl.BlockSpec(memory_space=pl.ANY)] * (2 * groups),
        out_specs=in_vmem(),
        scratch_shapes=[
            pltpu.VMEM((2, groups * capacity, BLK * 2 * near, FB), jnp.float32),
            pltpu.SemaphoreType.DMA((2, groups)),
        ],
        compiler_params=params(),
        name="place",
    )(take_from, strength, own_total, *blocks)
    result = placed.reshape(fibres, channels, 2, near, 2, FB).transpose(0, 1, 2, 4, 3, 5)
    return result.reshape(fibres, channels, 2, 2, samples)


def solution(mesh):
    return jax.shard_map(
        local,
        mesh=mesh,
        in_specs=(P(None, "wave", None, None, "tm"), P(), P(), P(), P(), P()),
        out_specs=P(None, "wave", None, None, "tm"),
        check_vma=False,
    )
```

```python
import functools
import math

import jax
import jax.numpy as jnp
import numpy as np
from jax import lax
from jax.experimental import pallas as pl
from jax.experimental.pallas import tpu as pltpu
from jax.sharding import PartitionSpec as P

BLK = 2
FA = 16
FB = 128
NFFT = FA * FB
HALF = 2
MARGIN = 512
VALID = 1024
LEAD = MARGIN // FB
STEP = VALID // FB
SUB = 8
VMEM_BYTES = 40 * 1024 * 1024


def split_bf16(values):
    high = values.astype(jnp.bfloat16)
    low = (values - high.astype(np.float64)).astype(jnp.bfloat16)
    return high, low


def matrix_tables():
    index = np.arange(FB)
    angle = 2.0 * np.pi * (np.outer(index, index) % FB) / FB
    cos, sin = np.cos(angle), np.sin(angle)
    forward = np.block([[cos, -sin], [sin, cos]])
    inverse = np.block([[cos, sin], [-sin, cos]])
    tables = []
    for matrix in (forward, inverse):
        high, low = split_bf16(matrix)
        tables.append(np.concatenate([high, low, high], axis=0))
    return tables


def twist_table():
    angle = 2.0 * np.pi * np.outer(np.arange(FA), np.arange(FB)) / NFFT
    table = np.stack([np.cos(angle), np.sin(angle)]).astype(np.float32)
    return np.ascontiguousarray(np.broadcast_to(table[:, :, None, :], (2, FA, SUB, FB)))


def filter_tables(spread, channel, channels_total):
    index = np.arange(FA)[:, None] + FA * np.arange(FB)[None, :]
    signed = np.where(index < NFFT // 2, index, index - NFFT).astype(np.float32)
    omega = jnp.asarray(signed) * (2.0 * math.pi / NFFT)
    offsets = (math.pi / 2.0) * (2.0 * channel.astype(jnp.float32) + 1.0 - channels_total)
    offsets = offsets / channels_total
    theta = spread[None, :, None] * (
        omega[:, None, :] ** 2 + 2.0 * omega[:, None, :] * offsets[None, :, None]
    )
    scale = 1.0 / NFFT
    return jnp.cos(theta) * scale, jnp.sin(theta) * scale


def cadd(a, b):
    return (a[0] + b[0], a[1] + b[1])


def csub(a, b):
    return (a[0] - b[0], a[1] - b[1])


def cturn(a, sign):
    return (-a[1], a[0]) if sign > 0 else (a[1], -a[0])


def croot(a, m, sign):
    m %= FA
    if m == 0:
        return a
    if m == 4:
        return cturn(a, sign)
    if m in (2, 6):
        h = np.float32(math.sqrt(0.5))
        c = h if m == 2 else -h
        s = h * sign
        if m == 2:
            if sign > 0:
                return ((a[0] - a[1]) * h, (a[0] + a[1]) * h)
            return ((a[0] + a[1]) * h, (a[1] - a[0]) * h)
        if sign > 0:
            return ((a[0] + a[1]) * (-h), (a[0] - a[1]) * h)
        return ((a[1] - a[0]) * h, (a[0] + a[1]) * (-h))
    c = np.float32(math.cos(2.0 * math.pi * m / FA))
    s = np.float32(sign * math.sin(2.0 * math.pi * m / FA))
    return (a[0] * c - a[1] * s, a[0] * s + a[1] * c)


def dft4(z, sign, keep=(0, 1, 2, 3)):
    even, odd = cadd(z[0], z[2]), cadd(z[1], z[3])
    out = {}
    if 0 in keep:
        out[0] = cadd(even, odd)
    if 2 in keep:
        out[2] = csub(even, odd)
    if 1 in keep or 3 in keep:
        base, turn = csub(z[0], z[2]), cturn(csub(z[1], z[3]), sign)
        if 1 in keep:
            out[1] = cadd(base, turn)
        if 3 in keep:
            out[3] = csub(base, turn)
    return out


def dft16(z, sign, keep=(0, 1, 2, 3)):
    inner = [dft4([z[4 * n1 + n2] for n1 in range(4)], sign) for n2 in range(4)]
    out = {}
    for k1 in range(4):
        column = [croot(inner[n2][k1], n2 * k1, sign) for n2 in range(4)]
        for k2, value in dft4(column, sign, keep).items():
            out[k1 + 4 * k2] = value
    return out


def sincos(x):
    n = jnp.round(x * np.float32(2.0 / math.pi))
    r = x - n * np.float32(1.5703125)
    r = r - n * np.float32(4.837512969970703125e-4)
    r = r - n * np.float32(7.54978995489188216e-8)
    q = n.astype(jnp.int32)
    r2 = r * r
    s = np.float32(-1.9515295891e-4) * r2 + np.float32(8.3321608736e-3)
    s = s * r2 + np.float32(-1.6666654611e-1)
    s = s * r2 * r + r
    c = np.float32(2.443315711809948e-5) * r2 + np.float32(-1.388731625493765e-3)
    c = c * r2 + np.float32(4.166664568298827e-2)
    c = c * r2 * r2 - np.float32(0.5) * r2 + np.float32(1.0)
    odd = (q & 1) == 1
    sine = jnp.where(odd, c, s)
    cosine = jnp.where(odd, s, c)
    sine = jnp.where((q & 2) == 2, -sine, sine)
    cosine = jnp.where(((q + 1) & 2) == 2, -cosine, cosine)
    return sine, cosine


def rotate_chunk(x_ref, q_ref, sel_ref, strength, tt, channels_total, fibres, slots, write):
    real, imag = x_ref[tt, 0], x_ref[tt, 1]
    power = real * real + imag * imag
    power = power[:slots] + power[slots:]
    if fibres == 1:
        total = q_ref[0, pl.ds(tt, 1), :]
    else:
        total = sel_ref[0] * q_ref[0, pl.ds(tt, 1), :]
        for f in range(1, fibres):
            total = total + sel_ref[f] * q_ref[f, pl.ds(tt, 1), :]
    phase = strength * (2.0 * total - power) * np.float32(1.0 / channels_total)
    sine, cosine = sincos(phase)
    sine = jnp.concatenate([sine, sine], axis=0)
    cosine = jnp.concatenate([cosine, cosine], axis=0)
    write(real * cosine - imag * sine, real * sine + imag * cosine)


def split_store(a_ref, base, column, value):
    high = value.astype(jnp.bfloat16)
    low = (value - high.astype(jnp.float32)).astype(jnp.bfloat16)
    rows = value.shape[0]
    a_ref[base : base + rows, column : column + FB] = high
    a_ref[base : base + rows, 2 * FB + column : 3 * FB + column] = high
    a_ref[base : base + rows, 4 * FB + column : 5 * FB + column] = low


def step_kernel(
    *refs, rotate, apart, channels_total, fibres_in, fibres_out, slots
):
    refs = list(refs)
    x_ref = refs.pop(0)
    if rotate:
        q_ref, selin_ref, strength_ref = refs[:3]
        refs = refs[3:]
    selout_ref, fc_ref, fs_ref, tw_ref, wf_ref, wi_ref, u_ref = refs[:7]
    refs = refs[7:]
    u_refs = [u_ref, refs.pop(0)] if apart else [u_ref]
    p_ref = refs.pop(0)
    xs_ref = refs.pop(0) if rotate else x_ref
    a_ref, z_ref = refs
    chunks = x_ref.shape[0]
    groups = 2 * slots // SUB
    half = groups // 2

    if rotate:

        def turn(tt, carry):
            def write(real, imag):
                xs_ref[tt, 0] = real
                xs_ref[tt, 1] = imag

            rotate_chunk(
                x_ref, q_ref, selin_ref, strength_ref[...], tt, channels_total, fibres_in, slots,
                write,
            )
            return carry

        lax.fori_loop(0, chunks, turn, 0)

    def block(j, carry):
        places = []
        for a in range(FA):
            at = j * STEP + (a - LEAD)
            at = jnp.where(at < 0, at + chunks, at)
            places.append(jnp.where(at >= chunks, at - chunks, at))
        for g in range(groups):
            rows = slice(g * SUB, (g + 1) * SUB)
            z = [(xs_ref[at, 0, rows, :], xs_ref[at, 1, rows, :]) for at in places]
            y = dft16(z, -1)
            for i in range(FA // 2):
                pair = []
                for k in (2 * i, 2 * i + 1):
                    real, imag = y[k]
                    if k:
                        c, s = tw_ref[0, k], tw_ref[1, k]
                        real, imag = real * c + imag * s, imag * c - real * s
                    pair.append((real, imag))
                base = (g * FA + 2 * i) * SUB
                for part in range(2):
                    value = jnp.concatenate([pair[0][part], pair[1][part]], axis=0)
                    split_store(a_ref, base, part * FB, value)
        z_ref[...] = jnp.dot(a_ref[...], wf_ref[...], preferred_element_type=jnp.float32)
        for g in range(groups):
            rows = slice((g % half) * SUB, (g % half + 1) * SUB)
            for i in range(FA // 2):
                pair = []
                for k in (2 * i, 2 * i + 1):
                    at = (g * FA + k) * SUB
                    real, imag = z_ref[at : at + SUB, :FB], z_ref[at : at + SUB, FB:]
                    c, s = fc_ref[k, rows, :], fs_ref[k, rows, :]
                    pair.append((real * c - imag * s, real * s + imag * c))
                base = (g * FA + 2 * i) * SUB
                for part in range(2):
                    value = jnp.concatenate([pair[0][part], pair[1][part]], axis=0)
                    split_store(a_ref, base, part * FB, value)
        z_ref[...] = jnp.dot(a_ref[...], wi_ref[...], preferred_element_type=jnp.float32)
        for g in range(groups):
            to_ref = u_refs[g // half] if apart else u_ref
            place = g % half if apart else g
            rows = slice(place * SUB, (place + 1) * SUB)
            z = []
            for k in range(FA):
                at = (g * FA + k) * SUB
                real, imag = z_ref[at : at + SUB, :FB], z_ref[at : at + SUB, FB:]
                if k:
                    c, s = tw_ref[0, k], tw_ref[1, k]
                    real, imag = real * c - imag * s, real * s + imag * c
                z.append((real, imag))
            y = dft16(z, 1, keep=(1, 2))
            for k in range(STEP):
                to_ref[j * STEP + k, 0, rows, :] = y[LEAD + k][0]
                to_ref[j * STEP + k, 1, rows, :] = y[LEAD + k][1]
        for k in range(STEP):
            tt = j * STEP + k
            power = None
            for p in range(2):
                if apart:
                    real, imag = u_refs[p][tt, 0], u_refs[p][tt, 1]
                else:
                    rows = slice(p * slots, (p + 1) * slots)
                    real, imag = u_ref[tt, 0, rows, :], u_ref[tt, 1, rows, :]
                mine = real * real + imag * imag
                power = mine if power is None else power + mine
            for f in range(fibres_out):
                mine = power if fibres_out == 1 else power * selout_ref[f]
                p_ref[f, pl.ds(tt, 1), :] = jnp.sum(mine, axis=0, keepdims=True)
        return carry

    lax.fori_loop(0, chunks // STEP, block, 0)


def pack_kernel(lit_ref, x_ref, o_ref, *, units, slots):
    rows = 2 * slots
    span = 2 * STEP
    for g in range(o_ref.shape[0]):
        if units < slots:
            o_ref[g] = jnp.zeros(o_ref.shape[1:], jnp.float32)
        for u in range(units):
            lit = lit_ref[g * units + u] > 0
            for p in range(2):
                at = ((g * units + u) * 2 + p) * span
                value = jnp.where(lit, x_ref[at : at + span, :], 0.0)
                o_ref[g, pl.ds(p * slots + u, span, stride=rows), :] = value


def send_kernel(item_ref, count_ref, x_ref, *o_refs, units, slots):
    capacity, near = o_refs[0].shape[0], o_refs[0].shape[1] // (2 * BLK)
    for s, o_ref in enumerate(o_refs):

        def body(n, carry, s=s, o_ref=o_ref):
            for c in range(BLK):
                channel = item_ref[s * capacity + n] * BLK + c
                g = channel // units
                u = channel - g * units
                for part in range(2):
                    at = (c * 2 + part) * near
                    o_ref[n, at : at + near, :] = x_ref[
                        g, pl.ds(part * slots + u, near, stride=2 * slots), :
                    ]
            return carry

        lax.fori_loop(0, count_ref[s], body, 0)


def place_kernel(from_ref, strength_ref, q_ref, *refs, channels_total, sources):
    in_refs, (o_ref, held_ref, sems) = refs[: 2 * sources], refs[2 * sources :]
    capacity, near = in_refs[0].shape[0], in_refs[0].shape[1] // (2 * BLK)
    copies = []
    for p in range(2):
        for s in range(sources):
            copies.append(
                pltpu.make_async_copy(
                    in_refs[p * sources + s],
                    held_ref.at[p, pl.ds(s * capacity, capacity)],
                    sems.at[p, s],
                )
            )
    for copy in copies:
        copy.start()
    for copy in copies:
        copy.wait()
    fibres = q_ref.shape[0]
    group_blocks = o_ref.shape[0] // fibres
    for f in range(fibres):
        total = 2.0 * q_ref[f]
        strength = strength_ref[f]

        def body(b, carry, f=f, total=total, strength=strength):
            n = f * group_blocks + b
            source = from_ref[n]
            for c in range(BLK):
                parts = []
                power = None
                for p in range(2):
                    at = c * 2 * near
                    real = held_ref[p, source, at : at + near, :]
                    imag = held_ref[p, source, at + near : at + 2 * near, :]
                    parts.append((real, imag))
                    mine = real * real + imag * imag
                    power = mine if power is None else power + mine
                phase = strength * (total - power) * np.float32(1.0 / channels_total)
                sine, cosine = sincos(phase)
                for p, (real, imag) in enumerate(parts):
                    at = (c * 2 + p) * 2 * near
                    o_ref[n, pl.ds(at, near, stride=2), :] = real * cosine - imag * sine
                    o_ref[n, pl.ds(at + 1, near, stride=2), :] = real * sine + imag * cosine
            return carry

        lax.fori_loop(0, group_blocks, body, 0)


def params():
    return pltpu.CompilerParams(vmem_limit_bytes=VMEM_BYTES)


def cost(flops, moved):
    return pl.CostEstimate(flops=int(flops), bytes_accessed=int(moved), transcendentals=0)


def in_vmem():
    return pl.BlockSpec(memory_space=pltpu.VMEM)


def in_smem():
    return pl.BlockSpec(memory_space=pltpu.SMEM)


def summed(values, rounds):
    for axis, bit in rounds:
        pairs = [(i, i ^ bit) for i in range(lax.axis_size(axis))]
        values = values + lax.ppermute(values, axis, pairs)
    return values


def route_tables(route_fibre, route_slot, groups, my_group, capacity):
    fibres = route_slot.shape[0]
    group_blocks = route_slot.shape[1] // groups
    sends = fibres * group_blocks

    def by_group(table):
        return table.reshape(fibres, groups, group_blocks).transpose(1, 0, 2).reshape(groups, sends)

    slot_all, fibre_all = by_group(route_slot), by_group(route_fibre)
    target_all = slot_all // group_blocks
    landing_all = fibre_all * group_blocks + slot_all % group_blocks
    position = jnp.arange(sends)
    earlier = (target_all[:, :, None] == target_all[:, None, :]) & (
        position[None, None, :] < position[None, :, None]
    )
    arrival_all = jnp.sum(earlier.astype(jnp.int32), axis=2)
    my_target = lax.dynamic_index_in_dim(target_all, my_group, 0, keepdims=False)
    my_arrival = lax.dynamic_index_in_dim(arrival_all, my_group, 0, keepdims=False)
    partner = my_target ^ my_group
    slot_index = partner * capacity + my_arrival
    matches = slot_index[None, :] == jnp.arange(groups * capacity)[:, None]
    source_item = jnp.sum(jnp.where(matches, position[None, :], 0), axis=1)
    counts = jnp.sum((partner[None, :] == jnp.arange(groups)[:, None]).astype(jnp.int32), axis=1)
    mine = target_all == my_group
    receive_slot = (jnp.arange(groups) ^ my_group)[:, None] * capacity + arrival_all
    hits = mine[:, :, None] & (landing_all[:, :, None] == position[None, None, :])
    take_from = jnp.sum(jnp.where(hits, receive_slot[:, :, None], 0), axis=(0, 1))
    return source_item.astype(jnp.int32), counts, take_from.astype(jnp.int32)


def time_halves(values, bits):
    times = lax.axis_size("tm")
    count = times.bit_length() - 1
    for b in bits:
        side = (lax.axis_index("tm") >> b) & 1
        dim = count - b
        keep = lax.dynamic_index_in_dim(values, side, dim)
        give = lax.dynamic_index_in_dim(values, 1 - side, dim)
        values = keep + lax.ppermute(give, "tm", [(i, i ^ (1 << b)) for i in range(times)])
    return values


def local(field, lit_count, route_fibre, route_slot, dispersion, nonlinearity):
    fibres, channels, samples = field.shape[0], field.shape[1], field.shape[-1]
    groups, times = lax.axis_size("wave"), lax.axis_size("tm")
    my_group, my_time = lax.axis_index("wave"), lax.axis_index("tm")
    channels_total = groups * channels
    units = fibres * channels // times
    slots = -(-units // SUB) * SUB
    rows = 2 * slots
    near = samples // FB
    chunks = times * near
    same_fibre = channels % units == 0
    group_blocks = channels // BLK
    sends = fibres * group_blocks
    capacity = 2 * sends // groups

    unit = my_time * units + jnp.minimum(jnp.arange(slots), units - 1)
    in_fibre = unit // channels
    in_channel = my_group * channels + unit % channels
    in_block = in_channel // BLK
    out_fibre = route_fibre[in_fibre, in_block]
    out_channel = route_slot[in_fibre, in_block] * BLK + in_channel % BLK
    real_slot = jnp.arange(slots) < units

    def wide(values):
        return jnp.broadcast_to(values.astype(jnp.float32)[..., None], values.shape + (FB,))

    def selection(fibre):
        chosen = (fibre[None, :] == jnp.arange(fibres)[:, None]) & real_slot[None, :]
        return wide(chosen)

    spans = []
    for span, (fibre, channel) in enumerate(((in_fibre, in_channel), (out_fibre, out_channel))):
        spread, strength = dispersion[span][fibre], nonlinearity[span][fibre]
        fc, fs = filter_tables(spread, channel, channels_total)
        spans.append((fc, fs, wide(strength), selection(fibre)))
    source_item, counts, take_from = route_tables(route_fibre, route_slot, groups, my_group, capacity)

    wave_rounds = [("wave", 1 << b) for b in range(groups.bit_length() - 1)]
    time_rounds = [("tm", 1 << b) for b in range(times.bit_length() - 1)]
    shared = channels // units if same_fibre else 0
    fibre_rounds = [("tm", 1 << b) for b in range(shared.bit_length() - 1)]

    lit_mask = (my_group * channels + jnp.arange(channels))[None, :] < lit_count[:, None]
    lit = lit_mask.reshape(-1).astype(jnp.int32)

    def natural_rows(values):
        split = values.reshape(fibres, channels, 2, 2, near, FB)
        return split.transpose(0, 1, 2, 4, 3, 5).reshape(-1, FB)

    packed = pl.pallas_call(
        functools.partial(pack_kernel, units=units, slots=slots),
        out_shape=jax.ShapeDtypeStruct((times, 2 * near * rows, FB), jnp.float32),
        in_specs=[in_smem(), in_vmem()],
        out_specs=in_vmem(),
        compiler_params=params(),
        name="pack",
    )(lit, natural_rows(field))
    wave_form = lax.all_to_all(packed, "tm", split_axis=0, concat_axis=0, tiled=True)
    wave_form = wave_form.reshape(chunks, 2, rows, FB)

    twist = jnp.asarray(twist_table())
    forward, inverse = (jnp.asarray(table) for table in matrix_tables())
    def dispersed(x, step, total, q_fibres, fibres_out, part):
        fc, fs, _, select = spans[step // HALF]
        rotate = total is not None
        operands = [x]
        if rotate:
            operands += [total, spans[(step - 1) // HALF][3], spans[(step - 1) // HALF][2]]
        operands += [select, fc, fs, twist, forward, inverse]
        shape = (chunks, 2, slots if part else rows, FB)
        outs = [jax.ShapeDtypeStruct(shape, jnp.float32)] * (2 if part else 1)
        outs += [jax.ShapeDtypeStruct((fibres_out, chunks, FB), jnp.float32)]
        scratch = [pltpu.VMEM(x.shape, jnp.float32)] if rotate else []
        scratch += [
            pltpu.VMEM((FA * rows, 6 * FB), jnp.bfloat16),
            pltpu.VMEM((FA * rows, 2 * FB), jnp.float32),
        ]
        return pl.pallas_call(
            functools.partial(
                step_kernel, rotate=rotate, apart=part, channels_total=channels_total,
                fibres_in=q_fibres, fibres_out=fibres_out, slots=slots,
            ),
            out_shape=tuple(outs),
            in_specs=[in_vmem()] * len(operands),
            out_specs=tuple([in_vmem()] * len(outs)),
            scratch_shapes=scratch,
            compiler_params=params(),
            cost_estimate=cost(chunks * rows * FB * 6400, 4 * x.size * 4),
            name="step",
        )(*operands)

    total, q_fibres = None, 0
    for step in range(2 * HALF - 1):
        fibres_out = 1 if (step < HALF and same_fibre) else fibres
        wave_form, partial = dispersed(wave_form, step, total, q_fibres, fibres_out, False)
        rounds = fibre_rounds if fibres_out == 1 else time_rounds
        total, q_fibres = summed(partial, wave_rounds + rounds), fibres_out

    last = 2 * HALF - 1

    def to_times(values):
        values = values.reshape(times, 2 * near * slots, FB)
        return lax.all_to_all(values, "tm", split_axis=0, concat_axis=0, tiled=True)

    def prepared(values):
        block = jax.ShapeDtypeStruct((capacity, BLK * 2 * near, FB), jnp.float32)
        return pl.pallas_call(
            functools.partial(send_kernel, units=units, slots=slots),
            out_shape=(block,) * groups,
            in_specs=[in_smem(), in_smem(), in_vmem()],
            out_specs=(in_vmem(),) * groups,
            compiler_params=params(),
            cost_estimate=cost(0, 4 * 4 * values.size),
            name="send",
        )(source_item, counts, values)

    def to_groups(outgoing):
        moved = [outgoing[0]]
        for s in range(1, groups):
            moved.append(lax.ppermute(outgoing[s], "wave", [(i, i ^ s) for i in range(groups)]))
        return moved

    first, second, partial = dispersed(wave_form, last, total, q_fibres, fibres, True)
    bits = list(range(times.bit_length() - 1))
    partial = summed(partial, wave_rounds).reshape([fibres] + [2] * len(bits) + [near, FB])
    first, partial = lax.optimization_barrier((to_times(first), partial))
    first = prepared(first)
    first, second = lax.optimization_barrier((first, second))
    partial = time_halves(partial, bits[:1] + bits[2:])
    second, partial, *first = lax.optimization_barrier((to_times(second), partial, *to_groups(first)))
    blocks = first + to_groups(prepared(second))
    own_total = time_halves(partial, bits[1:2]).reshape(fibres, near, FB)
    strength = jnp.broadcast_to(nonlinearity[1][:, None, None], (fibres, near, FB))
    placed = pl.pallas_call(
        functools.partial(place_kernel, channels_total=channels_total, sources=groups),
        out_shape=jax.ShapeDtypeStruct((sends, BLK * 4 * near, FB), jnp.float32),
        in_specs=[in_smem(), in_vmem(), in_vmem()]
        + [pl.BlockSpec(memory_space=pl.ANY)] * (2 * groups),
        out_specs=in_vmem(),
        scratch_shapes=[
            pltpu.VMEM((2, groups * capacity, BLK * 2 * near, FB), jnp.float32),
            pltpu.SemaphoreType.DMA((2, groups)),
        ],
        compiler_params=params(),
        cost_estimate=cost(0, 4 * 4 * field.size),
        name="place",
    )(take_from, strength, own_total, *blocks)
    result = placed.reshape(fibres, channels, 2, near, 2, FB).transpose(0, 1, 2, 4, 3, 5)
    return result.reshape(fibres, channels, 2, 2, samples)


def solution(mesh):
    return jax.shard_map(
        local,
        mesh=mesh,
        in_specs=(P(None, "wave", None, None, "tm"), P(), P(), P(), P(), P()),
        out_specs=P(None, "wave", None, None, "tm"),
        check_vma=False,
    )
```

```python
import functools
import math

import jax
import jax.numpy as jnp
import numpy as np
from jax import lax
from jax.experimental import pallas as pl
from jax.experimental.pallas import tpu as pltpu
from jax.sharding import PartitionSpec as P

BLK = 2
FA = 16
FB = 128
NFFT = FA * FB
HALF = 2
MARGIN = 512
VALID = 1024
LEAD = MARGIN // FB
STEP = VALID // FB
SUB = 8
UNROLL = 4
LAG = 1
VMEM_BYTES = 40 * 1024 * 1024


def split_bf16(values):
    high = values.astype(jnp.bfloat16)
    low = (values - high.astype(np.float64)).astype(jnp.bfloat16)
    return high, low


def matrix_tables():
    index = np.arange(FB)
    angle = 2.0 * np.pi * (np.outer(index, index) % FB) / FB
    cos, sin = np.cos(angle), np.sin(angle)
    forward = np.block([[cos, -sin], [sin, cos]])
    inverse = np.block([[cos, sin], [-sin, cos]])
    tables = []
    for matrix in (forward, inverse):
        high, low = split_bf16(matrix)
        tables.append(np.concatenate([high, low], axis=0))
    return tables


def twist_table():
    angle = 2.0 * np.pi * np.outer(np.arange(FA), np.arange(FB)) / NFFT
    table = np.stack([np.cos(angle), np.sin(angle)]).astype(np.float32)
    return np.ascontiguousarray(np.broadcast_to(table[:, :, None, :], (2, FA, SUB, FB)))


def filter_tables(spread, channel, channels_total):
    index = np.arange(FA)[:, None] + FA * np.arange(FB)[None, :]
    signed = np.where(index < NFFT // 2, index, index - NFFT).astype(np.float32)
    omega = jnp.asarray(signed) * (2.0 * math.pi / NFFT)
    offsets = (math.pi / 2.0) * (2.0 * channel.astype(jnp.float32) + 1.0 - channels_total)
    offsets = offsets / channels_total
    theta = spread[None, :, None] * (
        omega[:, None, :] ** 2 + 2.0 * omega[:, None, :] * offsets[None, :, None]
    )
    scale = 1.0 / NFFT
    return jnp.cos(theta) * scale, jnp.sin(theta) * scale


def cadd(a, b):
    return (a[0] + b[0], a[1] + b[1])


def csub(a, b):
    return (a[0] - b[0], a[1] - b[1])


def cturn(a, sign):
    return (-a[1], a[0]) if sign > 0 else (a[1], -a[0])


def croot(a, m, sign):
    m %= FA
    if m == 0:
        return a
    if m == 4:
        return cturn(a, sign)
    if m in (2, 6):
        h = np.float32(math.sqrt(0.5))
        c = h if m == 2 else -h
        s = h * sign
        if m == 2:
            if sign > 0:
                return ((a[0] - a[1]) * h, (a[0] + a[1]) * h)
            return ((a[0] + a[1]) * h, (a[1] - a[0]) * h)
        if sign > 0:
            return ((a[0] + a[1]) * (-h), (a[0] - a[1]) * h)
        return ((a[1] - a[0]) * h, (a[0] + a[1]) * (-h))
    c = np.float32(math.cos(2.0 * math.pi * m / FA))
    s = np.float32(sign * math.sin(2.0 * math.pi * m / FA))
    return (a[0] * c - a[1] * s, a[0] * s + a[1] * c)


def dft4(z, sign, keep=(0, 1, 2, 3)):
    even, odd = cadd(z[0], z[2]), cadd(z[1], z[3])
    out = {}
    if 0 in keep:
        out[0] = cadd(even, odd)
    if 2 in keep:
        out[2] = csub(even, odd)
    if 1 in keep or 3 in keep:
        base, turn = csub(z[0], z[2]), cturn(csub(z[1], z[3]), sign)
        if 1 in keep:
            out[1] = cadd(base, turn)
        if 3 in keep:
            out[3] = csub(base, turn)
    return out


def dft16(z, sign, keep=(0, 1, 2, 3)):
    inner = [dft4([z[4 * n1 + n2] for n1 in range(4)], sign) for n2 in range(4)]
    out = {}
    for k1 in range(4):
        column = [croot(inner[n2][k1], n2 * k1, sign) for n2 in range(4)]
        for k2, value in dft4(column, sign, keep).items():
            out[k1 + 4 * k2] = value
    return out


def sincos(x):
    n = jnp.round(x * np.float32(2.0 / math.pi))
    r = x - n * np.float32(1.5703125)
    r = r - n * np.float32(4.837512969970703125e-4)
    r = r - n * np.float32(7.54978995489188216e-8)
    q = n.astype(jnp.int32)
    r2 = r * r
    s = np.float32(-1.9515295891e-4) * r2 + np.float32(8.3321608736e-3)
    s = s * r2 + np.float32(-1.6666654611e-1)
    s = s * r2 * r + r
    c = np.float32(2.443315711809948e-5) * r2 + np.float32(-1.388731625493765e-3)
    c = c * r2 + np.float32(4.166664568298827e-2)
    c = c * r2 * r2 - np.float32(0.5) * r2 + np.float32(1.0)
    odd = (q & 1) == 1
    sine = jnp.where(odd, c, s)
    cosine = jnp.where(odd, s, c)
    sine = jnp.where((q & 2) == 2, -sine, sine)
    cosine = jnp.where(((q + 1) & 2) == 2, -cosine, cosine)
    return sine, cosine


def rotate_chunk(x_ref, q_ref, sel_ref, strength, tt, channels_total, fibres, slots, write):
    real, imag = x_ref[tt, 0], x_ref[tt, 1]
    power = real * real + imag * imag
    power = power[:slots] + power[slots:]
    if fibres == 1:
        total = q_ref[0, pl.ds(tt, 1), :]
    else:
        total = sel_ref[0] * q_ref[0, pl.ds(tt, 1), :]
        for f in range(1, fibres):
            total = total + sel_ref[f] * q_ref[f, pl.ds(tt, 1), :]
    phase = strength * (2.0 * total - power) * np.float32(1.0 / channels_total)
    sine, cosine = sincos(phase)
    sine = jnp.concatenate([sine, sine], axis=0)
    cosine = jnp.concatenate([cosine, cosine], axis=0)
    write(real * cosine - imag * sine, real * sine + imag * cosine)


def split_store(a_ref, base, column, value):
    high = value.astype(jnp.bfloat16)
    low = (value - high.astype(jnp.float32)).astype(jnp.bfloat16)
    rows = value.shape[0]
    a_ref[base : base + rows, column : column + FB] = high
    a_ref[base : base + rows, 2 * FB + column : 3 * FB + column] = low


def step_kernel(
    *refs, rotate, apart, channels_total, fibres_in, fibres_out, slots
):
    refs = list(refs)
    x_ref = refs.pop(0)
    if rotate:
        q_ref, selin_ref, strength_ref = refs[:3]
        refs = refs[3:]
    selout_ref, fc_ref, fs_ref, tw_ref, wf_ref, wi_ref, u_ref = refs[:7]
    refs = refs[7:]
    u_refs = [u_ref, refs.pop(0)] if apart else [u_ref]
    p_ref = refs.pop(0)
    xs_ref = refs.pop(0) if rotate else x_ref
    lanes = refs
    chunks = x_ref.shape[0]
    groups = 2 * slots // SUB
    half = groups // 2

    if rotate:

        def turn(tt, carry):
            def write(real, imag):
                xs_ref[tt, 0] = real
                xs_ref[tt, 1] = imag

            rotate_chunk(
                x_ref, q_ref, selin_ref, strength_ref[...], tt, channels_total, fibres_in, slots,
                write,
            )
            return carry

        lax.fori_loop(0, chunks, turn, 0, unroll=STEP)

    def gather(j, a_ref, g):
        places = []
        for a in range(FA):
            at = j * STEP + (a - LEAD)
            at = jnp.where(at < 0, at + chunks, at)
            places.append(jnp.where(at >= chunks, at - chunks, at))
        rows = slice(g * SUB, (g + 1) * SUB)
        z = [(xs_ref[at, 0, rows, :], xs_ref[at, 1, rows, :]) for at in places]
        y = dft16(z, -1)
        for i in range(FA // 2):
            pair = []
            for k in (2 * i, 2 * i + 1):
                real, imag = y[k]
                if k:
                    c, s = tw_ref[0, k], tw_ref[1, k]
                    real, imag = real * c + imag * s, imag * c - real * s
                pair.append((real, imag))
            store_pair(a_ref, (g * FA + 2 * i) * SUB, pair)

    def shape(a_ref, z_ref, g):
        rows = slice((g % half) * SUB, (g % half + 1) * SUB)
        for i in range(FA // 2):
            pair = []
            for k in (2 * i, 2 * i + 1):
                at = (g * FA + k) * SUB
                real, imag = z_ref[at : at + SUB, :FB], z_ref[at : at + SUB, FB:]
                c, s = fc_ref[k, rows, :], fs_ref[k, rows, :]
                pair.append((real * c - imag * s, real * s + imag * c))
            store_pair(a_ref, (g * FA + 2 * i) * SUB, pair)

    def spread(j, z_ref, g):
        to_ref = u_refs[g // half] if apart else u_ref
        place = g % half if apart else g
        rows = slice(place * SUB, (place + 1) * SUB)
        z = []
        for k in range(FA):
            at = (g * FA + k) * SUB
            real, imag = z_ref[at : at + SUB, :FB], z_ref[at : at + SUB, FB:]
            if k:
                c, s = tw_ref[0, k], tw_ref[1, k]
                real, imag = real * c - imag * s, real * s + imag * c
            z.append((real, imag))
        y = dft16(z, 1, keep=(1, 2))
        for k in range(STEP):
            real, imag = y[LEAD + k]
            to_ref[j * STEP + k, 0, rows, :] = real
            to_ref[j * STEP + k, 1, rows, :] = imag

    def add_up(j):
        for k in range(STEP):
            tt = j * STEP + k
            power = None
            for p in range(2):
                if apart:
                    real, imag = u_refs[p][tt, 0], u_refs[p][tt, 1]
                else:
                    rows = slice(p * slots, (p + 1) * slots)
                    real, imag = u_ref[tt, 0, rows, :], u_ref[tt, 1, rows, :]
                mine = real * real + imag * imag
                power = mine if power is None else power + mine
            for f in range(fibres_out):
                mine = power if fibres_out == 1 else power * selout_ref[f]
                p_ref[f, pl.ds(tt, 1), :] = jnp.sum(mine, axis=0, keepdims=True)

    count = len(lanes) // 4
    size = FA * SUB

    def blocks(n, carry):
        stage = [lanes[4 * i : 4 * i + 4] for i in range(count)]

        def times(a_ref, w_ref, z_ref, g):
            at = slice(g * size, (g + 1) * size)
            z_ref[at, :] = product(a_ref[at, :], w_ref)

        units = [(i, g) for i in range(count) for g in range(groups)]

        def unit(turn, stages_back):
            at = turn - stages_back * LAG
            return units[at] if 0 <= at < len(units) else None

        for turn in range(len(units) + 4 * LAG):
            if now := unit(turn, 4):
                i, g = now
                spread(n * count + i, stage[i][3], g)
                if g == groups - 1:
                    add_up(n * count + i)
            if now := unit(turn, 3):
                i, g = now
                times(stage[i][2], wi_ref, stage[i][3], g)
            if now := unit(turn, 2):
                i, g = now
                shape(stage[i][2], stage[i][1], g)
            if now := unit(turn, 1):
                i, g = now
                times(stage[i][0], wf_ref, stage[i][1], g)
            if now := unit(turn, 0):
                i, g = now
                gather(n * count + i, stage[i][0], g)
        return carry

    lax.fori_loop(0, chunks // STEP // count, blocks, 0)


def product(operand, w_ref):
    width = 2 * FB
    high, low = operand[:, :width], operand[:, width:]
    matrix_high, matrix_low = w_ref[:width, :], w_ref[width:, :]
    return (
        jnp.dot(high, matrix_high, preferred_element_type=jnp.float32)
        + jnp.dot(high, matrix_low, preferred_element_type=jnp.float32)
        + jnp.dot(low, matrix_high, preferred_element_type=jnp.float32)
    )


def store_pair(a_ref, base, pair):
    for part in range(2):
        split_store(a_ref, base, part * FB, jnp.concatenate([pair[0][part], pair[1][part]], axis=0))


def step_scratch(rows, count):
    operand = pltpu.VMEM((FA * rows, 4 * FB), jnp.bfloat16)
    product = pltpu.VMEM((FA * rows, 2 * FB), jnp.float32)
    return [operand, product, operand, product] * count


def pack_kernel(lit_ref, x_ref, o_ref, *, units, slots):
    rows = 2 * slots
    span = 2 * STEP
    for g in range(o_ref.shape[0]):
        if units < slots:
            o_ref[g] = jnp.zeros(o_ref.shape[1:], jnp.float32)
        for u in range(units):
            lit = lit_ref[g * units + u] > 0
            for p in range(2):
                at = ((g * units + u) * 2 + p) * span
                value = jnp.where(lit, x_ref[at : at + span, :], 0.0)
                o_ref[g, pl.ds(p * slots + u, span, stride=rows), :] = value


def send_kernel(item_ref, count_ref, x_ref, *o_refs, units, slots):
    capacity, near = o_refs[0].shape[0], o_refs[0].shape[1] // (2 * BLK)
    for s, o_ref in enumerate(o_refs):

        def body(n, carry, s=s, o_ref=o_ref):
            for c in range(BLK):
                channel = item_ref[s * capacity + n] * BLK + c
                g = channel // units
                u = channel - g * units
                for part in range(2):
                    at = (c * 2 + part) * near
                    o_ref[n, at : at + near, :] = x_ref[
                        g, pl.ds(part * slots + u, near, stride=2 * slots), :
                    ]
            return carry

        lax.fori_loop(0, count_ref[s], body, 0)


def place_kernel(from_ref, strength_ref, q_ref, *refs, channels_total, sources):
    in_refs, (o_ref, held_ref, sems) = refs[: 2 * sources], refs[2 * sources :]
    capacity, near = in_refs[0].shape[0], in_refs[0].shape[1] // (2 * BLK)
    copies = []
    for p in range(2):
        for s in range(sources):
            copies.append(
                pltpu.make_async_copy(
                    in_refs[p * sources + s],
                    held_ref.at[p, pl.ds(s * capacity, capacity)],
                    sems.at[p, s],
                )
            )
    for copy in copies:
        copy.start()
    for copy in copies:
        copy.wait()
    fibres = q_ref.shape[0]
    group_blocks = o_ref.shape[0] // fibres
    for f in range(fibres):
        total = 2.0 * q_ref[f]
        strength = strength_ref[f]

        def body(b, carry, f=f, total=total, strength=strength):
            n = f * group_blocks + b
            source = from_ref[n]
            for c in range(BLK):
                parts = []
                power = None
                for p in range(2):
                    at = c * 2 * near
                    real = held_ref[p, source, at : at + near, :]
                    imag = held_ref[p, source, at + near : at + 2 * near, :]
                    parts.append((real, imag))
                    mine = real * real + imag * imag
                    power = mine if power is None else power + mine
                phase = strength * (total - power) * np.float32(1.0 / channels_total)
                sine, cosine = sincos(phase)
                for p, (real, imag) in enumerate(parts):
                    at = (c * 2 + p) * 2 * near
                    o_ref[n, pl.ds(at, near, stride=2), :] = real * cosine - imag * sine
                    o_ref[n, pl.ds(at + 1, near, stride=2), :] = real * sine + imag * cosine
            return carry

        lax.fori_loop(0, group_blocks, body, 0, unroll=4)


def params():
    return pltpu.CompilerParams(vmem_limit_bytes=VMEM_BYTES)


def cost(flops, moved):
    return pl.CostEstimate(flops=int(flops), bytes_accessed=int(moved), transcendentals=0)


def in_vmem():
    return pl.BlockSpec(memory_space=pltpu.VMEM)


def in_smem():
    return pl.BlockSpec(memory_space=pltpu.SMEM)


def summed(values, rounds):
    for axis, bit in rounds:
        pairs = [(i, i ^ bit) for i in range(lax.axis_size(axis))]
        values = values + lax.ppermute(values, axis, pairs)
    return values


def route_tables(route_fibre, route_slot, groups, my_group, capacity):
    fibres = route_slot.shape[0]
    group_blocks = route_slot.shape[1] // groups
    sends = fibres * group_blocks

    def by_group(table):
        return table.reshape(fibres, groups, group_blocks).transpose(1, 0, 2).reshape(groups, sends)

    slot_all, fibre_all = by_group(route_slot), by_group(route_fibre)
    target_all = slot_all // group_blocks
    landing_all = fibre_all * group_blocks + slot_all % group_blocks
    position = jnp.arange(sends)
    earlier = (target_all[:, :, None] == target_all[:, None, :]) & (
        position[None, None, :] < position[None, :, None]
    )
    arrival_all = jnp.sum(earlier.astype(jnp.int32), axis=2)
    my_target = lax.dynamic_index_in_dim(target_all, my_group, 0, keepdims=False)
    my_arrival = lax.dynamic_index_in_dim(arrival_all, my_group, 0, keepdims=False)
    partner = my_target ^ my_group
    slot_index = partner * capacity + my_arrival
    matches = slot_index[None, :] == jnp.arange(groups * capacity)[:, None]
    source_item = jnp.sum(jnp.where(matches, position[None, :], 0), axis=1)
    counts = jnp.sum((partner[None, :] == jnp.arange(groups)[:, None]).astype(jnp.int32), axis=1)
    mine = target_all == my_group
    receive_slot = (jnp.arange(groups) ^ my_group)[:, None] * capacity + arrival_all
    hits = mine[:, :, None] & (landing_all[:, :, None] == position[None, None, :])
    take_from = jnp.sum(jnp.where(hits, receive_slot[:, :, None], 0), axis=(0, 1))
    return source_item.astype(jnp.int32), counts, take_from.astype(jnp.int32)


def time_halves(values, bits):
    times = lax.axis_size("tm")
    count = times.bit_length() - 1
    for b in bits:
        side = (lax.axis_index("tm") >> b) & 1
        dim = count - b
        keep = lax.dynamic_index_in_dim(values, side, dim)
        give = lax.dynamic_index_in_dim(values, 1 - side, dim)
        values = keep + lax.ppermute(give, "tm", [(i, i ^ (1 << b)) for i in range(times)])
    return values


def local(field, lit_count, route_fibre, route_slot, dispersion, nonlinearity):
    fibres, channels, samples = field.shape[0], field.shape[1], field.shape[-1]
    groups, times = lax.axis_size("wave"), lax.axis_size("tm")
    my_group, my_time = lax.axis_index("wave"), lax.axis_index("tm")
    channels_total = groups * channels
    units = fibres * channels // times
    slots = -(-units // SUB) * SUB
    rows = 2 * slots
    near = samples // FB
    chunks = times * near
    same_fibre = channels % units == 0
    group_blocks = channels // BLK
    sends = fibres * group_blocks
    capacity = 2 * sends // groups

    unit = my_time * units + jnp.minimum(jnp.arange(slots), units - 1)
    in_fibre = unit // channels
    in_channel = my_group * channels + unit % channels
    in_block = in_channel // BLK
    out_fibre = route_fibre[in_fibre, in_block]
    out_channel = route_slot[in_fibre, in_block] * BLK + in_channel % BLK
    real_slot = jnp.arange(slots) < units

    def wide(values):
        return jnp.broadcast_to(values.astype(jnp.float32)[..., None], values.shape + (FB,))

    def selection(fibre):
        chosen = (fibre[None, :] == jnp.arange(fibres)[:, None]) & real_slot[None, :]
        return wide(chosen)

    spans = []
    for span, (fibre, channel) in enumerate(((in_fibre, in_channel), (out_fibre, out_channel))):
        spread, strength = dispersion[span][fibre], nonlinearity[span][fibre]
        fc, fs = filter_tables(spread, channel, channels_total)
        spans.append((fc, fs, wide(strength), selection(fibre)))
    source_item, counts, take_from = route_tables(route_fibre, route_slot, groups, my_group, capacity)

    wave_rounds = [("wave", 1 << b) for b in range(groups.bit_length() - 1)]
    time_rounds = [("tm", 1 << b) for b in range(times.bit_length() - 1)]
    shared = channels // units if same_fibre else 0
    fibre_rounds = [("tm", 1 << b) for b in range(shared.bit_length() - 1)]

    lit_mask = (my_group * channels + jnp.arange(channels))[None, :] < lit_count[:, None]
    lit = lit_mask.reshape(-1).astype(jnp.int32)

    def natural_rows(values):
        split = values.reshape(fibres, channels, 2, 2, near, FB)
        return split.transpose(0, 1, 2, 4, 3, 5).reshape(-1, FB)

    packed = pl.pallas_call(
        functools.partial(pack_kernel, units=units, slots=slots),
        out_shape=jax.ShapeDtypeStruct((times, 2 * near * rows, FB), jnp.float32),
        in_specs=[in_smem(), in_vmem()],
        out_specs=in_vmem(),
        compiler_params=params(),
        name="pack",
    )(lit, natural_rows(field))
    wave_form = lax.all_to_all(packed, "tm", split_axis=0, concat_axis=0, tiled=True)
    wave_form = wave_form.reshape(chunks, 2, rows, FB)

    twist = jnp.asarray(twist_table())
    forward, inverse = (jnp.asarray(table) for table in matrix_tables())
    def dispersed(x, step, total, q_fibres, fibres_out, part):
        fc, fs, _, select = spans[step // HALF]
        rotate = total is not None
        operands = [x]
        if rotate:
            operands += [total, spans[(step - 1) // HALF][3], spans[(step - 1) // HALF][2]]
        operands += [select, fc, fs, twist, forward, inverse]
        shape = (chunks, 2, slots if part else rows, FB)
        outs = [jax.ShapeDtypeStruct(shape, jnp.float32)] * (2 if part else 1)
        outs += [jax.ShapeDtypeStruct((fibres_out, chunks, FB), jnp.float32)]
        scratch = [pltpu.VMEM(x.shape, jnp.float32)] if rotate else []
        scratch += step_scratch(rows, math.gcd(UNROLL, chunks // STEP))
        return pl.pallas_call(
            functools.partial(
                step_kernel, rotate=rotate, apart=part, channels_total=channels_total,
                fibres_in=q_fibres, fibres_out=fibres_out, slots=slots,
            ),
            out_shape=tuple(outs),
            in_specs=[in_vmem()] * len(operands),
            out_specs=tuple([in_vmem()] * len(outs)),
            scratch_shapes=scratch,
            compiler_params=params(),
            cost_estimate=cost(chunks * rows * FB * 6400, 4 * x.size * 4),
            name="step",
        )(*operands)

    total, q_fibres = None, 0
    for step in range(2 * HALF - 1):
        fibres_out = 1 if (step < HALF and same_fibre) else fibres
        wave_form, partial = dispersed(wave_form, step, total, q_fibres, fibres_out, False)
        rounds = fibre_rounds if fibres_out == 1 else time_rounds
        total, q_fibres = summed(partial, wave_rounds + rounds), fibres_out

    last = 2 * HALF - 1

    def to_times(values):
        values = values.reshape(times, 2 * near * slots, FB)
        return lax.all_to_all(values, "tm", split_axis=0, concat_axis=0, tiled=True)

    def prepared(values):
        block = jax.ShapeDtypeStruct((capacity, BLK * 2 * near, FB), jnp.float32)
        return pl.pallas_call(
            functools.partial(send_kernel, units=units, slots=slots),
            out_shape=(block,) * groups,
            in_specs=[in_smem(), in_smem(), in_vmem()],
            out_specs=(in_vmem(),) * groups,
            compiler_params=params(),
            cost_estimate=cost(0, 4 * 4 * values.size),
            name="send",
        )(source_item, counts, values)

    def to_groups(outgoing):
        moved = [outgoing[0]]
        for s in range(1, groups):
            moved.append(lax.ppermute(outgoing[s], "wave", [(i, i ^ s) for i in range(groups)]))
        return moved

    first, second, partial = dispersed(wave_form, last, total, q_fibres, fibres, True)
    bits = list(range(times.bit_length() - 1))
    partial = summed(partial, wave_rounds).reshape([fibres] + [2] * len(bits) + [near, FB])
    first, partial = lax.optimization_barrier((to_times(first), partial))
    first = prepared(first)
    first, second = lax.optimization_barrier((first, second))
    partial = time_halves(partial, bits[:1] + bits[2:])
    second, partial, *first = lax.optimization_barrier((to_times(second), partial, *to_groups(first)))
    blocks = first + to_groups(prepared(second))
    own_total = time_halves(partial, bits[1:2]).reshape(fibres, near, FB)
    strength = jnp.broadcast_to(nonlinearity[1][:, None, None], (fibres, near, FB))
    placed = pl.pallas_call(
        functools.partial(place_kernel, channels_total=channels_total, sources=groups),
        out_shape=jax.ShapeDtypeStruct((sends, BLK * 4 * near, FB), jnp.float32),
        in_specs=[in_smem(), in_vmem(), in_vmem()]
        + [pl.BlockSpec(memory_space=pl.ANY)] * (2 * groups),
        out_specs=in_vmem(),
        scratch_shapes=[
            pltpu.VMEM((2, groups * capacity, BLK * 2 * near, FB), jnp.float32),
            pltpu.SemaphoreType.DMA((2, groups)),
        ],
        compiler_params=params(),
        cost_estimate=cost(0, 4 * 4 * field.size),
        name="place",
    )(take_from, strength, own_total, *blocks)
    result = placed.reshape(fibres, channels, 2, near, 2, FB).transpose(0, 1, 2, 4, 3, 5)
    return result.reshape(fibres, channels, 2, 2, samples)


def solution(mesh):
    return jax.shard_map(
        local,
        mesh=mesh,
        in_specs=(P(None, "wave", None, None, "tm"), P(), P(), P(), P(), P()),
        out_specs=P(None, "wave", None, None, "tm"),
        check_vma=False,
    )
```

```python
import functools
import math

import jax
import jax.numpy as jnp
import numpy as np
from jax import lax
from jax.experimental import pallas as pl
from jax.experimental.pallas import tpu as pltpu
from jax.sharding import PartitionSpec as P

BLK = 2
FA = 16
FB = 128
NFFT = FA * FB
HALF = 2
MARGIN = 512
VALID = 1024
LEAD = MARGIN // FB
STEP = VALID // FB
SUB = 8
UNROLL = 4
LAG = 1
SPARE = 6 * 1024 * 1024


def split_bf16(values):
    high = values.astype(jnp.bfloat16)
    low = (values - high.astype(np.float64)).astype(jnp.bfloat16)
    return high, low


def matrix_tables():
    index = np.arange(FB)
    angle = 2.0 * np.pi * (np.outer(index, index) % FB) / FB
    cos, sin = np.cos(angle), np.sin(angle)
    forward = np.block([[cos, -sin], [sin, cos]])
    inverse = np.block([[cos, sin], [-sin, cos]])
    tables = []
    for matrix in (forward, inverse):
        high, low = split_bf16(matrix)
        tables.append(np.concatenate([high, low], axis=0))
    return tables


def twist_table():
    angle = 2.0 * np.pi * np.outer(np.arange(FA), np.arange(FB)) / NFFT
    table = np.stack([np.cos(angle), np.sin(angle)]).astype(np.float32)
    return np.ascontiguousarray(np.broadcast_to(table[:, :, None, :], (2, FA, SUB, FB)))


def filter_tables(spread, channel, channels_total):
    index = np.arange(FA)[:, None] + FA * np.arange(FB)[None, :]
    signed = np.where(index < NFFT // 2, index, index - NFFT).astype(np.float32)
    omega = jnp.asarray(signed) * (2.0 * math.pi / NFFT)
    offsets = (math.pi / 2.0) * (2.0 * channel.astype(jnp.float32) + 1.0 - channels_total)
    offsets = offsets / channels_total
    theta = spread[None, :, None] * (
        omega[:, None, :] ** 2 + 2.0 * omega[:, None, :] * offsets[None, :, None]
    )
    scale = 1.0 / NFFT
    return jnp.cos(theta) * scale, jnp.sin(theta) * scale


def cadd(a, b):
    return (a[0] + b[0], a[1] + b[1])


def csub(a, b):
    return (a[0] - b[0], a[1] - b[1])


def cturn(a, sign):
    return (-a[1], a[0]) if sign > 0 else (a[1], -a[0])


def croot(a, m, sign):
    m %= FA
    if m == 0:
        return a
    if m == 4:
        return cturn(a, sign)
    if m in (2, 6):
        h = np.float32(math.sqrt(0.5))
        c = h if m == 2 else -h
        s = h * sign
        if m == 2:
            if sign > 0:
                return ((a[0] - a[1]) * h, (a[0] + a[1]) * h)
            return ((a[0] + a[1]) * h, (a[1] - a[0]) * h)
        if sign > 0:
            return ((a[0] + a[1]) * (-h), (a[0] - a[1]) * h)
        return ((a[1] - a[0]) * h, (a[0] + a[1]) * (-h))
    c = np.float32(math.cos(2.0 * math.pi * m / FA))
    s = np.float32(sign * math.sin(2.0 * math.pi * m / FA))
    return (a[0] * c - a[1] * s, a[0] * s + a[1] * c)


def dft4(z, sign, keep=(0, 1, 2, 3)):
    even, odd = cadd(z[0], z[2]), cadd(z[1], z[3])
    out = {}
    if 0 in keep:
        out[0] = cadd(even, odd)
    if 2 in keep:
        out[2] = csub(even, odd)
    if 1 in keep or 3 in keep:
        base, turn = csub(z[0], z[2]), cturn(csub(z[1], z[3]), sign)
        if 1 in keep:
            out[1] = cadd(base, turn)
        if 3 in keep:
            out[3] = csub(base, turn)
    return out


def dft16(z, sign, keep=(0, 1, 2, 3)):
    inner = [dft4([z[4 * n1 + n2] for n1 in range(4)], sign) for n2 in range(4)]
    out = {}
    for k1 in range(4):
        column = [croot(inner[n2][k1], n2 * k1, sign) for n2 in range(4)]
        for k2, value in dft4(column, sign, keep).items():
            out[k1 + 4 * k2] = value
    return out


def sincos(x):
    n = jnp.round(x * np.float32(2.0 / math.pi))
    r = x - n * np.float32(1.5703125)
    r = r - n * np.float32(4.837512969970703125e-4)
    r = r - n * np.float32(7.54978995489188216e-8)
    q = n.astype(jnp.int32)
    r2 = r * r
    s = np.float32(-1.9515295891e-4) * r2 + np.float32(8.3321608736e-3)
    s = s * r2 + np.float32(-1.6666654611e-1)
    s = s * r2 * r + r
    c = np.float32(2.443315711809948e-5) * r2 + np.float32(-1.388731625493765e-3)
    c = c * r2 + np.float32(4.166664568298827e-2)
    c = c * r2 * r2 - np.float32(0.5) * r2 + np.float32(1.0)
    odd = (q & 1) == 1
    sine = jnp.where(odd, c, s)
    cosine = jnp.where(odd, s, c)
    sine = jnp.where((q & 2) == 2, -sine, sine)
    cosine = jnp.where(((q + 1) & 2) == 2, -cosine, cosine)
    return sine, cosine


def rotate_chunk(x_ref, q_ref, sel_ref, strength, tt, channels_total, fibres, slots, write):
    real, imag = x_ref[tt, 0], x_ref[tt, 1]
    power = real * real + imag * imag
    power = power[:slots] + power[slots:]
    if fibres == 1:
        total = q_ref[0, pl.ds(tt, 1), :]
    else:
        total = sel_ref[0] * q_ref[0, pl.ds(tt, 1), :]
        for f in range(1, fibres):
            total = total + sel_ref[f] * q_ref[f, pl.ds(tt, 1), :]
    phase = strength * (2.0 * total - power) * np.float32(1.0 / channels_total)
    sine, cosine = sincos(phase)
    sine = jnp.concatenate([sine, sine], axis=0)
    cosine = jnp.concatenate([cosine, cosine], axis=0)
    write(real * cosine - imag * sine, real * sine + imag * cosine)


def split_store(a_ref, base, column, value):
    high = value.astype(jnp.bfloat16)
    low = (value - high.astype(jnp.float32)).astype(jnp.bfloat16)
    rows = value.shape[0]
    a_ref[base : base + rows, column : column + FB] = high
    a_ref[base : base + rows, 2 * FB + column : 3 * FB + column] = low


def step_kernel(
    *refs, rotate, hold, fetch, leave, channels_total, fibres_in, fibres_out, slots
):
    refs = list(refs)
    x_ref = refs.pop(0)
    if rotate:
        q_ref, selin_ref, strength_ref = refs[:3]
        refs = refs[3:]
    selout_ref, fc_ref, fs_ref, tw_ref, wf_ref, wi_ref, u_out = refs[:7]
    refs = refs[7:]
    p_ref = refs.pop(0)
    rest_ref = refs.pop(0) if hold else None
    xs_ref = refs.pop(0) if rotate else x_ref
    u_ref, out_sems = (refs.pop(0), refs.pop(0)) if leave else (u_out, None)
    from_ref, in_sems = x_ref, None
    if fetch:
        x_ref, in_sems = refs.pop(0), refs.pop(0)
    lanes = refs
    chunks = x_ref.shape[0]
    held = u_ref.shape[2]
    groups = held // SUB
    half = slots // SUB

    if rotate:

        def turn(tt, carry):
            def write(real, imag):
                xs_ref[tt, 0] = real[:held]
                xs_ref[tt, 1] = imag[:held]
                if hold:
                    rest_ref[tt, 0] = real[held:]
                    rest_ref[tt, 1] = imag[held:]

            rotate_chunk(
                x_ref, q_ref, selin_ref, strength_ref[...], tt, channels_total, fibres_in, slots,
                write,
            )
            return carry

        if fetch:
            copies = []
            pieces = in_sems.shape[0]
            length = chunks // pieces
            for i in range(pieces):
                at = pl.ds(i * length, length)
                copies.append(
                    pltpu.make_async_copy(from_ref.at[at], x_ref.at[at], in_sems.at[i])
                )
                copies[-1].start()
            for i, copy in enumerate(copies):
                copy.wait()
                lax.fori_loop(i * length, (i + 1) * length, turn, 0, unroll=STEP)
        else:
            lax.fori_loop(0, chunks, turn, 0, unroll=STEP)

    def gather(j, a_ref, g):
        places = []
        for a in range(FA):
            at = j * STEP + (a - LEAD)
            at = jnp.where(at < 0, at + chunks, at)
            places.append(jnp.where(at >= chunks, at - chunks, at))
        rows = slice(g * SUB, (g + 1) * SUB)
        z = [(xs_ref[at, 0, rows, :], xs_ref[at, 1, rows, :]) for at in places]
        y = dft16(z, -1)
        for i in range(FA // 2):
            pair = []
            for k in (2 * i, 2 * i + 1):
                real, imag = y[k]
                if k:
                    c, s = tw_ref[0, k], tw_ref[1, k]
                    real, imag = real * c + imag * s, imag * c - real * s
                pair.append((real, imag))
            store_pair(a_ref, (g * FA + 2 * i) * SUB, pair)

    def shape(a_ref, z_ref, g):
        rows = slice((g % half) * SUB, (g % half + 1) * SUB)
        for i in range(FA // 2):
            pair = []
            for k in (2 * i, 2 * i + 1):
                at = (g * FA + k) * SUB
                real, imag = z_ref[at : at + SUB, :FB], z_ref[at : at + SUB, FB:]
                c, s = fc_ref[k, rows, :], fs_ref[k, rows, :]
                pair.append((real * c - imag * s, real * s + imag * c))
            store_pair(a_ref, (g * FA + 2 * i) * SUB, pair)

    def spread(j, z_ref, g):
        rows = slice(g * SUB, (g + 1) * SUB)
        z = []
        for k in range(FA):
            at = (g * FA + k) * SUB
            real, imag = z_ref[at : at + SUB, :FB], z_ref[at : at + SUB, FB:]
            if k:
                c, s = tw_ref[0, k], tw_ref[1, k]
                real, imag = real * c - imag * s, real * s + imag * c
            z.append((real, imag))
        y = dft16(z, 1, keep=(1, 2))
        for k in range(STEP):
            real, imag = y[LEAD + k]
            u_ref[j * STEP + k, 0, rows, :] = real
            u_ref[j * STEP + k, 1, rows, :] = imag

    def add_up(j):
        for k in range(STEP):
            tt = j * STEP + k
            power = None
            for p in range(held // slots):
                rows = slice(p * slots, (p + 1) * slots)
                real, imag = u_ref[tt, 0, rows, :], u_ref[tt, 1, rows, :]
                mine = real * real + imag * imag
                power = mine if power is None else power + mine
            for f in range(fibres_out):
                mine = power if fibres_out == 1 else power * selout_ref[f]
                p_ref[f, pl.ds(tt, 1), :] = jnp.sum(mine, axis=0, keepdims=True)

    count = len(lanes) // 4
    size = FA * SUB

    def blocks(n, carry):
        stage = [lanes[4 * i : 4 * i + 4] for i in range(count)]

        def times(a_ref, w_ref, z_ref, g):
            at = slice(g * size, (g + 1) * size)
            z_ref[at, :] = product(a_ref[at, :], w_ref)

        units = [(i, g) for i in range(count) for g in range(groups)]

        def unit(turn, stages_back):
            at = turn - stages_back * LAG
            return units[at] if 0 <= at < len(units) else None

        for turn in range(len(units) + 4 * LAG):
            if now := unit(turn, 4):
                i, g = now
                spread(n * count + i, stage[i][3], g)
                if g == groups - 1:
                    add_up(n * count + i)
            if now := unit(turn, 3):
                i, g = now
                times(stage[i][2], wi_ref, stage[i][3], g)
            if now := unit(turn, 2):
                i, g = now
                shape(stage[i][2], stage[i][1], g)
            if now := unit(turn, 1):
                i, g = now
                times(stage[i][0], wf_ref, stage[i][1], g)
            if now := unit(turn, 0):
                i, g = now
                gather(n * count + i, stage[i][0], g)
        return carry

    turns = chunks // STEP // count

    def leaving(n):
        at = pl.ds(n * count * STEP, count * STEP)
        return pltpu.make_async_copy(u_ref.at[at], u_out.at[at], out_sems.at[n])

    def blocks_out(n, carry):
        blocks(n, carry)
        leaving(n).start()
        return carry

    if leave:
        lax.fori_loop(0, turns, blocks_out, 0)
        for n in range(turns):
            leaving(n).wait()
    else:
        lax.fori_loop(0, turns, blocks, 0)


def product(operand, w_ref):
    width = 2 * FB
    high, low = operand[:, :width], operand[:, width:]
    matrix_high, matrix_low = w_ref[:width, :], w_ref[width:, :]
    return (
        jnp.dot(high, matrix_high, preferred_element_type=jnp.float32)
        + jnp.dot(high, matrix_low, preferred_element_type=jnp.float32)
        + jnp.dot(low, matrix_high, preferred_element_type=jnp.float32)
    )


def store_pair(a_ref, base, pair):
    for part in range(2):
        split_store(a_ref, base, part * FB, jnp.concatenate([pair[0][part], pair[1][part]], axis=0))


def step_scratch(rows, count):
    operand = pltpu.VMEM((FA * rows, 4 * FB), jnp.bfloat16)
    product = pltpu.VMEM((FA * rows, 2 * FB), jnp.float32)
    return [operand, product, operand, product] * count


def pack_kernel(lit_ref, x_ref, o_ref, *, units, slots):
    rows = 2 * slots
    span = o_ref.shape[1] // rows
    first = pl.program_id(0) * o_ref.shape[0] * units
    for g in range(o_ref.shape[0]):
        if units < slots:
            o_ref[g] = jnp.zeros(o_ref.shape[1:], jnp.float32)
        for u in range(units):
            channel = g * units + u
            lit = lit_ref[first + channel] > 0
            for p in range(2):
                at = (channel * 2 + p) * span
                value = jnp.where(lit, x_ref[at : at + span, :], 0.0)
                o_ref[g, pl.ds(p * slots + u, span, stride=rows), :] = value


def send_kernel(item_ref, count_ref, x_ref, *refs, units, slots):
    *out_refs, held_ref, sems = refs
    capacity, near = held_ref.shape[1], held_ref.shape[2] // (2 * BLK)
    several = math.gcd(capacity, 4)
    copies = []
    for s, out_ref in enumerate(out_refs):
        o_ref = held_ref.at[s]

        def body(m, carry, s=s, o_ref=o_ref):
            for k in range(several):
                n = m * several + k
                for c in range(BLK):
                    channel = item_ref[s * capacity + n] * BLK + c
                    g = channel // units
                    u = channel - g * units
                    for part in range(2):
                        at = (c * 2 + part) * near
                        o_ref[n, at : at + near, :] = x_ref[
                            g, pl.ds(part * slots + u, near, stride=2 * slots), :
                        ]
            return carry

        lax.fori_loop(0, (count_ref[s] + several - 1) // several, body, 0)
        copies.append(pltpu.make_async_copy(o_ref, out_ref, sems.at[s]))
        copies[-1].start()
    for copy in copies:
        copy.wait()


def place_kernel(from_ref, strength_ref, q_ref, *refs, channels_total, sources):
    in_refs, (o_ref, held_ref, sems) = refs[: 2 * sources], refs[2 * sources :]
    capacity, near = in_refs[0].shape[0], in_refs[0].shape[1] // (2 * BLK)
    copies = []
    for p in range(2):
        for s in range(sources):
            copies.append(
                pltpu.make_async_copy(
                    in_refs[p * sources + s],
                    held_ref.at[p, pl.ds(s * capacity, capacity)],
                    sems.at[p, s],
                )
            )
    for copy in copies:
        copy.start()
    for copy in copies:
        copy.wait()
    fibres = q_ref.shape[0]
    group_blocks = o_ref.shape[0] // fibres
    for f in range(fibres):
        total = 2.0 * q_ref[f]
        strength = strength_ref[f]

        def body(b, carry, f=f, total=total, strength=strength):
            n = f * group_blocks + b
            source = from_ref[n]
            for c in range(BLK):
                parts = []
                power = None
                for p in range(2):
                    at = c * 2 * near
                    real = held_ref[p, source, at : at + near, :]
                    imag = held_ref[p, source, at + near : at + 2 * near, :]
                    parts.append((real, imag))
                    mine = real * real + imag * imag
                    power = mine if power is None else power + mine
                phase = strength * (total - power) * np.float32(1.0 / channels_total)
                sine, cosine = sincos(phase)
                for p, (real, imag) in enumerate(parts):
                    at = (c * 2 + p) * 2 * near
                    o_ref[n, pl.ds(at, near, stride=2), :] = real * cosine - imag * sine
                    o_ref[n, pl.ds(at + 1, near, stride=2), :] = real * sine + imag * cosine
            return carry

        lax.fori_loop(0, group_blocks, body, 0, unroll=4)


def params(*shapes):
    return pltpu.CompilerParams(
        vmem_limit_bytes=SPARE + sum(4 * math.prod(shape) for shape in shapes)
    )


def cost(flops, moved):
    return pl.CostEstimate(flops=int(flops), bytes_accessed=int(moved), transcendentals=0)


def in_vmem():
    return pl.BlockSpec(memory_space=pltpu.VMEM)


def in_smem():
    return pl.BlockSpec(memory_space=pltpu.SMEM)


def summed(values, rounds):
    size = lax.axis_size("wave") * lax.axis_size("tm")
    for bits in rounds:
        masks = [0]
        for bit in bits:
            masks += [mask | bit for mask in masks]
        others = [
            lax.ppermute(values, ("wave", "tm"), [(i, i ^ mask) for i in range(size)])
            for mask in masks[1:]
        ]
        for other in others:
            values = values + other
    return values


def route_tables(route_fibre, route_slot, groups, my_group, capacity):
    fibres = route_slot.shape[0]
    group_blocks = route_slot.shape[1] // groups
    sends = fibres * group_blocks

    def by_group(table):
        return table.reshape(fibres, groups, group_blocks).transpose(1, 0, 2).reshape(groups, sends)

    slot_all, fibre_all = by_group(route_slot), by_group(route_fibre)
    target_all = slot_all // group_blocks
    landing_all = fibre_all * group_blocks + slot_all % group_blocks
    position = jnp.arange(sends)
    earlier = (target_all[:, :, None] == target_all[:, None, :]) & (
        position[None, None, :] < position[None, :, None]
    )
    arrival_all = jnp.sum(earlier.astype(jnp.int32), axis=2)
    my_target = lax.dynamic_index_in_dim(target_all, my_group, 0, keepdims=False)
    my_arrival = lax.dynamic_index_in_dim(arrival_all, my_group, 0, keepdims=False)
    partner = my_target ^ my_group
    slot_index = partner * capacity + my_arrival
    matches = slot_index[None, :] == jnp.arange(groups * capacity)[:, None]
    source_item = jnp.sum(jnp.where(matches, position[None, :], 0), axis=1)
    counts = jnp.sum((partner[None, :] == jnp.arange(groups)[:, None]).astype(jnp.int32), axis=1)
    mine = target_all == my_group
    receive_slot = (jnp.arange(groups) ^ my_group)[:, None] * capacity + arrival_all
    hits = mine[:, :, None] & (landing_all[:, :, None] == position[None, None, :])
    take_from = jnp.sum(jnp.where(hits, receive_slot[:, :, None], 0), axis=(0, 1))
    return source_item.astype(jnp.int32), counts, take_from.astype(jnp.int32)


def time_parts(values, bits):
    times = lax.axis_size("tm")
    count = times.bit_length() - 1
    masks = [0]
    for b in bits:
        masks += [mask | (1 << b) for mask in masks]
    kept = None
    for mask in masks:
        part = values
        for b in bits:
            side = ((lax.axis_index("tm") ^ mask) >> b) & 1
            part = lax.dynamic_index_in_dim(part, side, count - b)
        if mask:
            part = lax.ppermute(part, "tm", [(i, i ^ mask) for i in range(times)])
        kept = part if kept is None else kept + part
    return kept


def local(field, lit_count, route_fibre, route_slot, dispersion, nonlinearity):
    fibres, channels, samples = field.shape[0], field.shape[1], field.shape[-1]
    groups, times = lax.axis_size("wave"), lax.axis_size("tm")
    my_group, my_time = lax.axis_index("wave"), lax.axis_index("tm")
    channels_total = groups * channels
    units = fibres * channels // times
    slots = -(-units // SUB) * SUB
    rows = 2 * slots
    near = samples // FB
    chunks = times * near
    same_fibre = channels % units == 0
    group_blocks = channels // BLK
    sends = fibres * group_blocks
    capacity = 2 * sends // groups

    unit = my_time * units + jnp.minimum(jnp.arange(slots), units - 1)
    in_fibre = unit // channels
    in_channel = my_group * channels + unit % channels
    in_block = in_channel // BLK
    out_fibre = route_fibre[in_fibre, in_block]
    out_channel = route_slot[in_fibre, in_block] * BLK + in_channel % BLK
    real_slot = jnp.arange(slots) < units

    def wide(values):
        return jnp.broadcast_to(values.astype(jnp.float32)[..., None], values.shape + (FB,))

    def selection(fibre):
        chosen = (fibre[None, :] == jnp.arange(fibres)[:, None]) & real_slot[None, :]
        return wide(chosen)

    spans = []
    for span, (fibre, channel) in enumerate(((in_fibre, in_channel), (out_fibre, out_channel))):
        spread, strength = dispersion[span][fibre], nonlinearity[span][fibre]
        fc, fs = filter_tables(spread, channel, channels_total)
        spans.append((fc, fs, wide(strength), selection(fibre)))
    source_item, counts, take_from = route_tables(route_fibre, route_slot, groups, my_group, capacity)

    wave_bits = [times << b for b in range(groups.bit_length() - 1)]
    time_bits = [1 << b for b in range(times.bit_length() - 1)]
    wave_rounds = [(bit,) for bit in wave_bits]
    all_rounds = wave_rounds + [(bit,) for bit in time_bits]
    shared = channels // units if same_fibre else 0
    fibre_bits = wave_bits + time_bits[: max(shared.bit_length() - 1, 0)]
    fibre_rounds = [tuple(fibre_bits[:1])]
    fibre_rounds += [tuple(fibre_bits[i : i + 2]) for i in range(1, len(fibre_bits), 2)]

    lit_mask = (my_group * channels + jnp.arange(channels))[None, :] < lit_count[:, None]
    lit = lit_mask.reshape(-1).astype(jnp.int32)

    def natural_rows(values):
        split = values.reshape(fibres, channels, 2, 2, near, FB)
        return split.transpose(0, 1, 2, 4, 3, 5).reshape(-1, FB)

    strips = math.gcd(times, 4)
    block = (times // strips, 2 * near * rows, FB)
    natural = pltpu.with_memory_space_constraint(natural_rows(field), pltpu.HBM)
    packed = pl.pallas_call(
        functools.partial(pack_kernel, units=units, slots=slots),
        out_shape=pltpu.HBM((times,) + block[1:], jnp.float32),
        grid=(strips,),
        in_specs=[in_smem(), pl.BlockSpec((natural.shape[0] // strips, FB), lambda i: (i, 0))],
        out_specs=pl.BlockSpec(block, lambda i: (i, 0, 0)),
        compiler_params=params(field.shape, block, block),
        name="pack",
    )(lit, natural)
    wave_form = lax.all_to_all(packed, "tm", split_axis=0, concat_axis=0, tiled=True)
    wave_form = wave_form.reshape(chunks, 2, rows, FB)

    twist = jnp.asarray(twist_table())
    forward, inverse = (jnp.asarray(table) for table in matrix_tables())
    def dispersed(x, step, total, q_fibres, fibres_out, hold):
        fc, fs, _, select = spans[step // HALF]
        rotate = total is not None
        operands = [x]
        if rotate:
            operands += [total, spans[(step - 1) // HALF][3], spans[(step - 1) // HALF][2]]
        operands += [select, fc, fs, twist, forward, inverse]
        held = slots if hold else x.shape[2]
        shape = (chunks, 2, held, FB)
        leave, fetch = not rotate or hold, step == 1
        wave = (pltpu.HBM if leave else jax.ShapeDtypeStruct)(shape, jnp.float32)
        outs = [wave, jax.ShapeDtypeStruct((fibres_out, chunks, FB), jnp.float32)]
        outs += [pltpu.HBM(shape, jnp.float32)] if hold else []
        specs_in = [in_vmem()] * len(operands)
        specs_out = [in_vmem()] * len(outs)
        unroll = math.gcd(UNROLL, chunks // STEP)
        scratch = [pltpu.VMEM(shape, jnp.float32)] if rotate else []
        if leave:
            specs_out[0] = pl.BlockSpec(memory_space=pltpu.HBM)
            turns = chunks // STEP // unroll
            scratch += [pltpu.VMEM(shape, jnp.float32), pltpu.SemaphoreType.DMA((turns,))]
        if fetch:
            specs_in[0] = pl.BlockSpec(memory_space=pltpu.HBM)
            operands[0] = pltpu.with_memory_space_constraint(x, pltpu.HBM)
            scratch += [
                pltpu.VMEM(x.shape, jnp.float32),
                pltpu.SemaphoreType.DMA((math.gcd(4, chunks // STEP),)),
            ]
        scratch += step_scratch(held, unroll)
        return pl.pallas_call(
            functools.partial(
                step_kernel, rotate=rotate, hold=hold, fetch=fetch, leave=leave,
                channels_total=channels_total, fibres_in=q_fibres, fibres_out=fibres_out,
                slots=slots,
            ),
            out_shape=tuple(outs),
            in_specs=specs_in,
            out_specs=tuple(specs_out),
            scratch_shapes=scratch,
            compiler_params=params(*[x.shape] * 5, *[ref.shape for ref in scratch]),
            cost_estimate=cost(chunks * held * FB * 6400, 4 * x.size * 4),
            name="step",
        )(*operands)

    total, q_fibres = None, 0
    for step in range(2 * HALF - 1):
        fibres_out = 1 if (step < HALF and same_fibre) else fibres
        wave_form, partial = dispersed(wave_form, step, total, q_fibres, fibres_out, False)
        rounds = fibre_rounds if fibres_out == 1 else all_rounds
        total, q_fibres = summed(partial, rounds), fibres_out

    last = 2 * HALF - 1

    def to_times(values):
        values = values.reshape(times, 2 * near * slots, FB)
        return lax.all_to_all(values, "tm", split_axis=0, concat_axis=0, tiled=True)

    def prepared(values):
        block = pltpu.HBM((capacity, BLK * 2 * near, FB), jnp.float32)
        return pl.pallas_call(
            functools.partial(send_kernel, units=units, slots=slots),
            out_shape=(block,) * groups,
            in_specs=[in_smem(), in_smem(), in_vmem()],
            out_specs=(pl.BlockSpec(memory_space=pltpu.HBM),) * groups,
            scratch_shapes=[
                pltpu.VMEM((groups,) + block.shape, jnp.float32),
                pltpu.SemaphoreType.DMA((groups,)),
            ],
            compiler_params=params(values.shape, (groups,) + block.shape),
            cost_estimate=cost(0, 4 * 4 * values.size),
            name="send",
        )(source_item, counts, values)

    def to_groups(outgoing):
        moved = [pltpu.with_memory_space_constraint(outgoing[0], pltpu.HBM)]
        for s in range(1, groups):
            moved.append(lax.ppermute(outgoing[s], "wave", [(i, i ^ s) for i in range(groups)]))
        return moved

    first, partial, rest = dispersed(wave_form, last, total, q_fibres, fibres, True)
    second, more = dispersed(rest, last, None, 0, fibres, False)
    bits = list(range(times.bit_length() - 1))
    partial = summed(partial + more, wave_rounds)
    partial = partial.reshape([fibres] + [2] * len(bits) + [near, FB])
    partial = time_parts(partial, bits[:1])
    first, partial = lax.optimization_barrier((to_times(first), partial))
    first = prepared(first)
    first, second = lax.optimization_barrier((first, second))
    second, *first = lax.optimization_barrier((to_times(second), *to_groups(first)))
    blocks = first + to_groups(prepared(second))
    for i in range(1, len(bits), 2):
        partial = time_parts(partial, bits[i : i + 2])
    own_total = partial.reshape(fibres, near, FB)
    strength = jnp.broadcast_to(nonlinearity[1][:, None, None], (fibres, near, FB))
    placed = pl.pallas_call(
        functools.partial(place_kernel, channels_total=channels_total, sources=groups),
        out_shape=jax.ShapeDtypeStruct((sends, BLK * 4 * near, FB), jnp.float32),
        in_specs=[in_smem(), in_vmem(), in_vmem()]
        + [pl.BlockSpec(memory_space=pl.ANY)] * (2 * groups),
        out_specs=in_vmem(),
        scratch_shapes=[
            pltpu.VMEM((2, groups * capacity, BLK * 2 * near, FB), jnp.float32),
            pltpu.SemaphoreType.DMA((2, groups)),
        ],
        compiler_params=params(field.shape, (2, groups * capacity, BLK * 2 * near, FB)),
        cost_estimate=cost(0, 4 * 4 * field.size),
        name="place",
    )(take_from, strength, own_total, *blocks)
    result = placed.reshape(fibres, channels, 2, near, 2, FB).transpose(0, 1, 2, 4, 3, 5)
    return result.reshape(fibres, channels, 2, 2, samples)


def solution(mesh):
    return jax.shard_map(
        local,
        mesh=mesh,
        in_specs=(P(None, "wave", None, None, "tm"), P(), P(), P(), P(), P()),
        out_specs=P(None, "wave", None, None, "tm"),
        check_vma=False,
    )
```

```python
import functools
import math

import jax
import jax.numpy as jnp
import numpy as np
from jax import lax
from jax.experimental import pallas as pl
from jax.experimental.pallas import tpu as pltpu
from jax.sharding import PartitionSpec as P

BLK = 2
FA = 16
FB = 128
NFFT = FA * FB
HALF = 2
MARGIN = 512
VALID = 1024
LEAD = MARGIN // FB
STEP = VALID // FB
SUB = 8
UNROLL = 4
LAG = 1
SPARE = 6 * 1024 * 1024


def split_bf16(values):
    high = values.astype(jnp.bfloat16)
    low = (values - high.astype(np.float64)).astype(jnp.bfloat16)
    return high, low


def matrix_tables():
    index = np.arange(FB)
    angle = 2.0 * np.pi * (np.outer(index, index) % FB) / FB
    cos, sin = np.cos(angle), np.sin(angle)
    forward = np.block([[cos, -sin], [sin, cos]])
    inverse = np.block([[cos, sin], [-sin, cos]])
    tables = []
    for matrix in (forward, inverse):
        high, low = split_bf16(matrix)
        tables.append(np.concatenate([high, low], axis=0))
    return tables


def twist_table():
    angle = 2.0 * np.pi * np.outer(np.arange(FA), np.arange(FB)) / NFFT
    table = np.stack([np.cos(angle), np.sin(angle)]).astype(np.float32)
    return np.ascontiguousarray(np.broadcast_to(table[:, :, None, :], (2, FA, SUB, FB)))


def filter_tables(spread, channel, channels_total):
    index = np.arange(FA)[:, None] + FA * np.arange(FB)[None, :]
    signed = np.where(index < NFFT // 2, index, index - NFFT).astype(np.float32)
    omega = jnp.asarray(signed) * (2.0 * math.pi / NFFT)
    offsets = (math.pi / 2.0) * (2.0 * channel.astype(jnp.float32) + 1.0 - channels_total)
    offsets = offsets / channels_total
    theta = spread[None, :, None] * (
        omega[:, None, :] ** 2 + 2.0 * omega[:, None, :] * offsets[None, :, None]
    )
    scale = 1.0 / NFFT
    return jnp.cos(theta) * scale, jnp.sin(theta) * scale


def cadd(a, b):
    return (a[0] + b[0], a[1] + b[1])


def csub(a, b):
    return (a[0] - b[0], a[1] - b[1])


def cturn(a, sign):
    return (-a[1], a[0]) if sign > 0 else (a[1], -a[0])


def croot(a, m, sign):
    m %= FA
    if m == 0:
        return a
    if m == 4:
        return cturn(a, sign)
    if m in (2, 6):
        h = np.float32(math.sqrt(0.5))
        c = h if m == 2 else -h
        s = h * sign
        if m == 2:
            if sign > 0:
                return ((a[0] - a[1]) * h, (a[0] + a[1]) * h)
            return ((a[0] + a[1]) * h, (a[1] - a[0]) * h)
        if sign > 0:
            return ((a[0] + a[1]) * (-h), (a[0] - a[1]) * h)
        return ((a[1] - a[0]) * h, (a[0] + a[1]) * (-h))
    c = np.float32(math.cos(2.0 * math.pi * m / FA))
    s = np.float32(sign * math.sin(2.0 * math.pi * m / FA))
    return (a[0] * c - a[1] * s, a[0] * s + a[1] * c)


def dft4(z, sign, keep=(0, 1, 2, 3)):
    even, odd = cadd(z[0], z[2]), cadd(z[1], z[3])
    out = {}
    if 0 in keep:
        out[0] = cadd(even, odd)
    if 2 in keep:
        out[2] = csub(even, odd)
    if 1 in keep or 3 in keep:
        base, turn = csub(z[0], z[2]), cturn(csub(z[1], z[3]), sign)
        if 1 in keep:
            out[1] = cadd(base, turn)
        if 3 in keep:
            out[3] = csub(base, turn)
    return out


def dft16(z, sign, keep=(0, 1, 2, 3)):
    inner = [dft4([z[4 * n1 + n2] for n1 in range(4)], sign) for n2 in range(4)]
    out = {}
    for k1 in range(4):
        column = [croot(inner[n2][k1], n2 * k1, sign) for n2 in range(4)]
        for k2, value in dft4(column, sign, keep).items():
            out[k1 + 4 * k2] = value
    return out


def sincos(x):
    n = jnp.round(x * np.float32(2.0 / math.pi))
    r = x - n * np.float32(1.5703125)
    r = r - n * np.float32(4.837512969970703125e-4)
    r = r - n * np.float32(7.54978995489188216e-8)
    q = n.astype(jnp.int32)
    r2 = r * r
    s = np.float32(-1.9515295891e-4) * r2 + np.float32(8.3321608736e-3)
    s = s * r2 + np.float32(-1.6666654611e-1)
    s = s * r2 * r + r
    c = np.float32(2.443315711809948e-5) * r2 + np.float32(-1.388731625493765e-3)
    c = c * r2 + np.float32(4.166664568298827e-2)
    c = c * r2 * r2 - np.float32(0.5) * r2 + np.float32(1.0)
    odd = (q & 1) == 1
    sine = jnp.where(odd, c, s)
    cosine = jnp.where(odd, s, c)
    sine = jnp.where((q & 2) == 2, -sine, sine)
    cosine = jnp.where(((q + 1) & 2) == 2, -cosine, cosine)
    return sine, cosine


def rotate_chunk(x_ref, q_ref, sel_ref, strength, tt, channels_total, fibres, slots, write):
    real, imag = x_ref[tt, 0], x_ref[tt, 1]
    power = real * real + imag * imag
    power = power[:slots] + power[slots:]
    if fibres == 1:
        total = q_ref[0, pl.ds(tt, 1), :]
    else:
        total = sel_ref[0] * q_ref[0, pl.ds(tt, 1), :]
        for f in range(1, fibres):
            total = total + sel_ref[f] * q_ref[f, pl.ds(tt, 1), :]
    phase = strength * (2.0 * total - power) * np.float32(1.0 / channels_total)
    sine, cosine = sincos(phase)
    sine = jnp.concatenate([sine, sine], axis=0)
    cosine = jnp.concatenate([cosine, cosine], axis=0)
    write(real * cosine - imag * sine, real * sine + imag * cosine)


def split_store(a_ref, base, column, value):
    high = value.astype(jnp.bfloat16)
    low = (value - high.astype(jnp.float32)).astype(jnp.bfloat16)
    rows = value.shape[0]
    a_ref[base : base + rows, column : column + FB] = high
    a_ref[base : base + rows, 2 * FB + column : 3 * FB + column] = low


def step_kernel(
    *refs, rotate, hold, fetch, leave, channels_total, fibres_in, fibres_out, slots
):
    refs = list(refs)
    x_ref = refs.pop(0)
    if rotate:
        q_ref, selin_ref, strength_ref = refs[:3]
        refs = refs[3:]
    selout_ref, fc_ref, fs_ref, tw_ref, wf_ref, wi_ref, u_out = refs[:7]
    refs = refs[7:]
    p_ref = refs.pop(0)
    rest_ref = refs.pop(0) if hold else None
    xs_ref = refs.pop(0) if rotate else x_ref
    u_ref, out_sems = (refs.pop(0), refs.pop(0)) if leave else (u_out, None)
    from_ref, in_sems = x_ref, None
    if fetch:
        x_ref, in_sems = refs.pop(0), refs.pop(0)
    lanes = refs
    chunks = x_ref.shape[0]
    held = u_ref.shape[2]
    groups = held // SUB
    half = slots // SUB

    if rotate:

        def turn(tt, carry):
            def write(real, imag):
                xs_ref[tt, 0] = real[:held]
                xs_ref[tt, 1] = imag[:held]
                if hold:
                    rest_ref[tt, 0] = real[held:]
                    rest_ref[tt, 1] = imag[held:]

            rotate_chunk(
                x_ref, q_ref, selin_ref, strength_ref[...], tt, channels_total, fibres_in, slots,
                write,
            )
            return carry

        if fetch:
            copies = []
            pieces = in_sems.shape[0]
            length = chunks // pieces
            for i in range(pieces):
                at = pl.ds(i * length, length)
                copies.append(
                    pltpu.make_async_copy(from_ref.at[at], x_ref.at[at], in_sems.at[i])
                )
                copies[-1].start()
            for i, copy in enumerate(copies):
                copy.wait()
                lax.fori_loop(i * length, (i + 1) * length, turn, 0, unroll=STEP)
        else:
            lax.fori_loop(0, chunks, turn, 0, unroll=STEP)

    def gather(j, a_ref, g):
        places = []
        for a in range(FA):
            at = j * STEP + (a - LEAD)
            at = jnp.where(at < 0, at + chunks, at)
            places.append(jnp.where(at >= chunks, at - chunks, at))
        rows = slice(g * SUB, (g + 1) * SUB)
        z = [(xs_ref[at, 0, rows, :], xs_ref[at, 1, rows, :]) for at in places]
        y = dft16(z, -1)
        for i in range(FA // 2):
            pair = []
            for k in (2 * i, 2 * i + 1):
                real, imag = y[k]
                if k:
                    c, s = tw_ref[0, k], tw_ref[1, k]
                    real, imag = real * c + imag * s, imag * c - real * s
                pair.append((real, imag))
            store_pair(a_ref, (g * FA + 2 * i) * SUB, pair)

    def shape(a_ref, z_ref, g):
        rows = slice((g % half) * SUB, (g % half + 1) * SUB)
        for i in range(FA // 2):
            pair = []
            for k in (2 * i, 2 * i + 1):
                at = (g * FA + k) * SUB
                real, imag = z_ref[at : at + SUB, :FB], z_ref[at : at + SUB, FB:]
                c, s = fc_ref[k, rows, :], fs_ref[k, rows, :]
                pair.append((real * c - imag * s, real * s + imag * c))
            store_pair(a_ref, (g * FA + 2 * i) * SUB, pair)

    def spread(j, z_ref, g):
        rows = slice(g * SUB, (g + 1) * SUB)
        z = []
        for k in range(FA):
            at = (g * FA + k) * SUB
            real, imag = z_ref[at : at + SUB, :FB], z_ref[at : at + SUB, FB:]
            if k:
                c, s = tw_ref[0, k], tw_ref[1, k]
                real, imag = real * c - imag * s, real * s + imag * c
            z.append((real, imag))
        y = dft16(z, 1, keep=(1, 2))
        for k in range(STEP):
            real, imag = y[LEAD + k]
            u_ref[j * STEP + k, 0, rows, :] = real
            u_ref[j * STEP + k, 1, rows, :] = imag

    def add_up(j):
        for k in range(STEP):
            tt = j * STEP + k
            power = None
            for p in range(held // slots):
                rows = slice(p * slots, (p + 1) * slots)
                real, imag = u_ref[tt, 0, rows, :], u_ref[tt, 1, rows, :]
                mine = real * real + imag * imag
                power = mine if power is None else power + mine
            for f in range(fibres_out):
                mine = power if fibres_out == 1 else power * selout_ref[f]
                p_ref[f, pl.ds(tt, 1), :] = jnp.sum(mine, axis=0, keepdims=True)

    count = len(lanes) // 4
    size = FA * SUB

    def blocks(n, carry):
        stage = [lanes[4 * i : 4 * i + 4] for i in range(count)]

        def times(a_ref, w_ref, z_ref, g):
            at = slice(g * size, (g + 1) * size)
            z_ref[at, :] = product(a_ref[at, :], w_ref)

        units = [(i, g) for i in range(count) for g in range(groups)]

        def unit(turn, stages_back):
            at = turn - stages_back * LAG
            return units[at] if 0 <= at < len(units) else None

        for turn in range(len(units) + 4 * LAG):
            if now := unit(turn, 4):
                i, g = now
                spread(n * count + i, stage[i][3], g)
                if g == groups - 1:
                    add_up(n * count + i)
            if now := unit(turn, 3):
                i, g = now
                times(stage[i][2], wi_ref, stage[i][3], g)
            if now := unit(turn, 2):
                i, g = now
                shape(stage[i][2], stage[i][1], g)
            if now := unit(turn, 1):
                i, g = now
                times(stage[i][0], wf_ref, stage[i][1], g)
            if now := unit(turn, 0):
                i, g = now
                gather(n * count + i, stage[i][0], g)
        return carry

    turns = chunks // STEP // count

    def leaving(n):
        at = pl.ds(n * count * STEP, count * STEP)
        return pltpu.make_async_copy(u_ref.at[at], u_out.at[at], out_sems.at[n])

    def blocks_out(n, carry):
        blocks(n, carry)
        leaving(n).start()
        return carry

    if leave:
        lax.fori_loop(0, turns, blocks_out, 0)
        for n in range(turns):
            leaving(n).wait()
    else:
        lax.fori_loop(0, turns, blocks, 0)


def product(operand, w_ref):
    width = 2 * FB
    high, low = operand[:, :width], operand[:, width:]
    matrix_high, matrix_low = w_ref[:width, :], w_ref[width:, :]
    return (
        jnp.dot(high, matrix_high, preferred_element_type=jnp.float32)
        + jnp.dot(high, matrix_low, preferred_element_type=jnp.float32)
        + jnp.dot(low, matrix_high, preferred_element_type=jnp.float32)
    )


def store_pair(a_ref, base, pair):
    for part in range(2):
        split_store(a_ref, base, part * FB, jnp.concatenate([pair[0][part], pair[1][part]], axis=0))


def step_scratch(rows, count):
    operand = pltpu.VMEM((FA * rows, 4 * FB), jnp.bfloat16)
    product = pltpu.VMEM((FA * rows, 2 * FB), jnp.float32)
    return [operand, product, operand, product] * count


def pack_kernel(count_ref, x_hbm, o_hbm, x_ref, o_ref, sems, *, units, slots, channels):
    rows = 2 * slots
    span = o_ref.shape[1] // rows
    strips = sems.shape[1]
    length, devices = x_ref.shape[0] // strips, o_ref.shape[0] // strips
    base = lax.axis_index("wave") * channels

    def copy_in(i):
        at = pl.ds(i * length, length)
        return pltpu.make_async_copy(x_hbm.at[at], x_ref.at[at], sems.at[0, i])

    def copy_out(i):
        at = pl.ds(i * devices, devices)
        return pltpu.make_async_copy(o_ref.at[at], o_hbm.at[at], sems.at[1, i])

    for i in range(strips):
        copy_in(i).start()
    for i in range(strips):
        copy_in(i).wait()
        for g in range(i * devices, (i + 1) * devices):
            if units < slots:
                o_ref[g] = jnp.zeros(o_ref.shape[1:], jnp.float32)
            for u in range(units):
                unit = g * units + u
                lit = base + unit % channels < count_ref[unit // channels]
                for p in range(2):
                    at = (unit * 2 + p) * span
                    value = jnp.where(lit, x_ref[at : at + span, :], 0.0)
                    o_ref[g, pl.ds(p * slots + u, span, stride=rows), :] = value
        copy_out(i).start()
    for i in range(strips):
        copy_out(i).wait()


def send_kernel(item_ref, count_ref, x_ref, *refs, units, slots):
    *out_refs, held_ref, sems = refs
    capacity, near = held_ref.shape[1], held_ref.shape[2] // (2 * BLK)
    several = math.gcd(capacity, 4)
    copies = []
    for s, out_ref in enumerate(out_refs):
        o_ref = held_ref.at[s]

        def body(m, carry, s=s, o_ref=o_ref):
            for k in range(several):
                n = m * several + k
                for c in range(BLK):
                    channel = item_ref[s * capacity + n] * BLK + c
                    g = channel // units
                    u = channel - g * units
                    for part in range(2):
                        at = (c * 2 + part) * near
                        o_ref[n, at : at + near, :] = x_ref[
                            g, pl.ds(part * slots + u, near, stride=2 * slots), :
                        ]
            return carry

        lax.fori_loop(0, (count_ref[s] + several - 1) // several, body, 0)
        copies.append(pltpu.make_async_copy(o_ref, out_ref, sems.at[s]))
        copies[-1].start()
    for copy in copies:
        copy.wait()


def place_kernel(from_ref, strength_ref, q_ref, *refs, channels_total, sources):
    in_refs, (o_hbm, o_ref, held_ref, sems, out_sems) = refs[: 2 * sources], refs[2 * sources :]
    capacity, near = in_refs[0].shape[0], in_refs[0].shape[1] // (2 * BLK)
    copies = []
    for p in range(2):
        for s in range(sources):
            copies.append(
                pltpu.make_async_copy(
                    in_refs[p * sources + s],
                    held_ref.at[p, pl.ds(s * capacity, capacity)],
                    sems.at[p, s],
                )
            )
    for copy in copies:
        copy.start()
    for copy in copies:
        copy.wait()
    copies = []
    fibres = q_ref.shape[0]
    group_blocks = o_ref.shape[0] // fibres
    for f in range(fibres):
        total = 2.0 * q_ref[f]
        strength = strength_ref[f]

        def body(b, carry, f=f, total=total, strength=strength):
            n = f * group_blocks + b
            source = from_ref[n]
            for c in range(BLK):
                parts = []
                power = None
                for p in range(2):
                    at = c * 2 * near
                    real = held_ref[p, source, at : at + near, :]
                    imag = held_ref[p, source, at + near : at + 2 * near, :]
                    parts.append((real, imag))
                    mine = real * real + imag * imag
                    power = mine if power is None else power + mine
                phase = strength * (total - power) * np.float32(1.0 / channels_total)
                sine, cosine = sincos(phase)
                for p, (real, imag) in enumerate(parts):
                    at = (c * 2 + p) * 2 * near
                    o_ref[n, pl.ds(at, near, stride=2), :] = real * cosine - imag * sine
                    o_ref[n, pl.ds(at + 1, near, stride=2), :] = real * sine + imag * cosine
            return carry

        lax.fori_loop(0, group_blocks, body, 0, unroll=4)
        at = pl.ds(f * group_blocks, group_blocks)
        copies.append(pltpu.make_async_copy(o_ref.at[at], o_hbm.at[at], out_sems.at[f]))
        copies[-1].start()
    for copy in copies:
        copy.wait()


def params(*shapes):
    return pltpu.CompilerParams(
        vmem_limit_bytes=SPARE + sum(4 * math.prod(shape) for shape in shapes)
    )


def cost(flops, moved):
    return pl.CostEstimate(flops=int(flops), bytes_accessed=int(moved), transcendentals=0)


def in_vmem():
    return pl.BlockSpec(memory_space=pltpu.VMEM)


def in_smem():
    return pl.BlockSpec(memory_space=pltpu.SMEM)


def summed(values, rounds):
    size = lax.axis_size("wave") * lax.axis_size("tm")
    for bits in rounds:
        masks = [0]
        for bit in bits:
            masks += [mask | bit for mask in masks]
        others = [
            lax.ppermute(values, ("wave", "tm"), [(i, i ^ mask) for i in range(size)])
            for mask in masks[1:]
        ]
        for other in others:
            values = values + other
    return values


def route_tables(route_fibre, route_slot, groups, my_group, capacity):
    fibres = route_slot.shape[0]
    group_blocks = route_slot.shape[1] // groups
    sends = fibres * group_blocks

    def by_group(table):
        return table.reshape(fibres, groups, group_blocks).transpose(1, 0, 2).reshape(groups, sends)

    slot_all, fibre_all = by_group(route_slot), by_group(route_fibre)
    target_all = slot_all // group_blocks
    landing_all = fibre_all * group_blocks + slot_all % group_blocks
    position = jnp.arange(sends)
    earlier = (target_all[:, :, None] == target_all[:, None, :]) & (
        position[None, None, :] < position[None, :, None]
    )
    arrival_all = jnp.sum(earlier.astype(jnp.int32), axis=2)
    my_target = lax.dynamic_index_in_dim(target_all, my_group, 0, keepdims=False)
    my_arrival = lax.dynamic_index_in_dim(arrival_all, my_group, 0, keepdims=False)
    partner = my_target ^ my_group
    slot_index = partner * capacity + my_arrival
    matches = slot_index[None, :] == jnp.arange(groups * capacity)[:, None]
    source_item = jnp.sum(jnp.where(matches, position[None, :], 0), axis=1)
    counts = jnp.sum((partner[None, :] == jnp.arange(groups)[:, None]).astype(jnp.int32), axis=1)
    mine = target_all == my_group
    receive_slot = (jnp.arange(groups) ^ my_group)[:, None] * capacity + arrival_all
    hits = mine[:, :, None] & (landing_all[:, :, None] == position[None, None, :])
    take_from = jnp.sum(jnp.where(hits, receive_slot[:, :, None], 0), axis=(0, 1))
    return source_item.astype(jnp.int32), counts, take_from.astype(jnp.int32)


def time_parts(values, bits):
    times = lax.axis_size("tm")
    count = times.bit_length() - 1
    masks = [0]
    for b in bits:
        masks += [mask | (1 << b) for mask in masks]
    kept = None
    for mask in masks:
        part = values
        for b in bits:
            side = ((lax.axis_index("tm") ^ mask) >> b) & 1
            part = lax.dynamic_index_in_dim(part, side, count - b)
        if mask:
            part = lax.ppermute(part, "tm", [(i, i ^ mask) for i in range(times)])
        kept = part if kept is None else kept + part
    return kept


def local(field, lit_count, route_fibre, route_slot, dispersion, nonlinearity):
    fibres, channels, samples = field.shape[0], field.shape[1], field.shape[-1]
    groups, times = lax.axis_size("wave"), lax.axis_size("tm")
    my_group, my_time = lax.axis_index("wave"), lax.axis_index("tm")
    channels_total = groups * channels
    units = fibres * channels // times
    slots = -(-units // SUB) * SUB
    rows = 2 * slots
    near = samples // FB
    chunks = times * near
    same_fibre = channels % units == 0
    group_blocks = channels // BLK
    sends = fibres * group_blocks
    capacity = 2 * sends // groups

    unit = my_time * units + jnp.minimum(jnp.arange(slots), units - 1)
    in_fibre = unit // channels
    in_channel = my_group * channels + unit % channels
    in_block = in_channel // BLK
    out_fibre = route_fibre[in_fibre, in_block]
    out_channel = route_slot[in_fibre, in_block] * BLK + in_channel % BLK
    real_slot = jnp.arange(slots) < units

    def wide(values):
        return jnp.broadcast_to(values.astype(jnp.float32)[..., None], values.shape + (FB,))

    def selection(fibre):
        chosen = (fibre[None, :] == jnp.arange(fibres)[:, None]) & real_slot[None, :]
        return wide(chosen)

    spans = []
    for span, (fibre, channel) in enumerate(((in_fibre, in_channel), (out_fibre, out_channel))):
        spread, strength = dispersion[span][fibre], nonlinearity[span][fibre]
        fc, fs = filter_tables(spread, channel, channels_total)
        spans.append((fc, fs, wide(strength), selection(fibre)))
    source_item, counts, take_from = route_tables(route_fibre, route_slot, groups, my_group, capacity)

    wave_bits = [times << b for b in range(groups.bit_length() - 1)]
    time_bits = [1 << b for b in range(times.bit_length() - 1)]
    wave_rounds = [(bit,) for bit in wave_bits]
    all_rounds = [(bit,) for bit in wave_bits + time_bits]
    shared = channels // units if same_fibre else 0
    fibre_bits = wave_bits + time_bits[: max(shared.bit_length() - 1, 0)]
    fibre_rounds = [tuple(fibre_bits[:1])]
    fibre_rounds += [tuple(fibre_bits[i : i + 2]) for i in range(1, len(fibre_bits), 2)]

    def natural_rows(values):
        split = values.reshape(fibres, channels, 2, 2, near, FB)
        return split.transpose(0, 1, 2, 4, 3, 5).reshape(-1, FB)

    strips = math.gcd(times, 4)
    in_hbm = pl.BlockSpec(memory_space=pltpu.HBM)
    natural = pltpu.with_memory_space_constraint(natural_rows(field), pltpu.HBM)
    shape = (times, 2 * near * rows, FB)
    packed = pl.pallas_call(
        functools.partial(pack_kernel, units=units, slots=slots, channels=channels),
        out_shape=pltpu.HBM(shape, jnp.float32),
        in_specs=[in_smem(), in_hbm],
        out_specs=in_hbm,
        scratch_shapes=[
            pltpu.VMEM(natural.shape, jnp.float32),
            pltpu.VMEM(shape, jnp.float32),
            pltpu.SemaphoreType.DMA((2, strips)),
        ],
        compiler_params=params(field.shape, shape),
        name="pack",
    )(lit_count, natural)
    wave_form = lax.all_to_all(packed, "tm", split_axis=0, concat_axis=0, tiled=True)
    wave_form = wave_form.reshape(chunks, 2, rows, FB)

    twist = jnp.asarray(twist_table())
    forward, inverse = (jnp.asarray(table) for table in matrix_tables())
    def dispersed(x, step, total, q_fibres, fibres_out, hold):
        fc, fs, _, select = spans[step // HALF]
        rotate = total is not None
        operands = [x]
        if rotate:
            operands += [total, spans[(step - 1) // HALF][3], spans[(step - 1) // HALF][2]]
        operands += [select, fc, fs, twist, forward, inverse]
        held = slots if hold else x.shape[2]
        shape = (chunks, 2, held, FB)
        leave, fetch = not rotate or hold, step == 1
        wave = (pltpu.HBM if leave else jax.ShapeDtypeStruct)(shape, jnp.float32)
        outs = [wave, jax.ShapeDtypeStruct((fibres_out, chunks, FB), jnp.float32)]
        outs += [pltpu.HBM(shape, jnp.float32)] if hold else []
        specs_in = [in_vmem()] * len(operands)
        specs_out = [in_vmem()] * len(outs)
        unroll = math.gcd(UNROLL, chunks // STEP)
        scratch = [pltpu.VMEM(shape, jnp.float32)] if rotate else []
        if leave:
            specs_out[0] = pl.BlockSpec(memory_space=pltpu.HBM)
            turns = chunks // STEP // unroll
            scratch += [pltpu.VMEM(shape, jnp.float32), pltpu.SemaphoreType.DMA((turns,))]
        if fetch:
            specs_in[0] = pl.BlockSpec(memory_space=pltpu.HBM)
            operands[0] = pltpu.with_memory_space_constraint(x, pltpu.HBM)
            scratch += [
                pltpu.VMEM(x.shape, jnp.float32),
                pltpu.SemaphoreType.DMA((math.gcd(4, chunks // STEP),)),
            ]
        scratch += step_scratch(held, unroll)
        return pl.pallas_call(
            functools.partial(
                step_kernel, rotate=rotate, hold=hold, fetch=fetch, leave=leave,
                channels_total=channels_total, fibres_in=q_fibres, fibres_out=fibres_out,
                slots=slots,
            ),
            out_shape=tuple(outs),
            in_specs=specs_in,
            out_specs=tuple(specs_out),
            scratch_shapes=scratch,
            compiler_params=params(*[x.shape] * 5, *[ref.shape for ref in scratch]),
            cost_estimate=cost(chunks * held * FB * 6400, 4 * x.size * 4),
            name="step",
        )(*operands)

    total, q_fibres = None, 0
    for step in range(2 * HALF - 1):
        fibres_out = 1 if (step < HALF and same_fibre) else fibres
        wave_form, partial = dispersed(wave_form, step, total, q_fibres, fibres_out, False)
        if fibres_out == 1:
            total = summed(partial, fibre_rounds)
        else:
            cut = fibres_out // 2
            there, back = all_rounds, all_rounds[:1] + all_rounds[:0:-1]
            total = jnp.concatenate(
                [summed(partial[:cut], there), summed(partial[cut:], back)], axis=0
            )
        q_fibres = fibres_out

    last = 2 * HALF - 1

    def to_times(values):
        values = values.reshape(times, 2 * near * slots, FB)
        return lax.all_to_all(values, "tm", split_axis=0, concat_axis=0, tiled=True)

    def prepared(values):
        block = pltpu.HBM((capacity, BLK * 2 * near, FB), jnp.float32)
        return pl.pallas_call(
            functools.partial(send_kernel, units=units, slots=slots),
            out_shape=(block,) * groups,
            in_specs=[in_smem(), in_smem(), in_vmem()],
            out_specs=(pl.BlockSpec(memory_space=pltpu.HBM),) * groups,
            scratch_shapes=[
                pltpu.VMEM((groups,) + block.shape, jnp.float32),
                pltpu.SemaphoreType.DMA((groups,)),
            ],
            compiler_params=params(values.shape, (groups,) + block.shape),
            cost_estimate=cost(0, 4 * 4 * values.size),
            name="send",
        )(source_item, counts, values)

    def to_groups(outgoing):
        moved = [pltpu.with_memory_space_constraint(outgoing[0], pltpu.HBM)]
        for s in range(1, groups):
            moved.append(lax.ppermute(outgoing[s], "wave", [(i, i ^ s) for i in range(groups)]))
        return moved

    first, partial, rest = dispersed(wave_form, last, total, q_fibres, fibres, True)
    second, more = dispersed(rest, last, None, 0, fibres, False)
    bits = list(range(times.bit_length() - 1))
    partial = summed(partial + more, wave_rounds)
    partial = partial.reshape([fibres] + [2] * len(bits) + [near, FB])
    partial = time_parts(partial, bits[:1])
    first, partial = lax.optimization_barrier((to_times(first), partial))
    first = prepared(first)
    first, second = lax.optimization_barrier((first, second))
    second, *first = lax.optimization_barrier((to_times(second), *to_groups(first)))
    blocks = first + to_groups(prepared(second))
    for i in range(1, len(bits), 2):
        partial = time_parts(partial, bits[i : i + 2])
    own_total = partial.reshape(fibres, near, FB)
    strength = jnp.broadcast_to(nonlinearity[1][:, None, None], (fibres, near, FB))
    placed = pl.pallas_call(
        functools.partial(place_kernel, channels_total=channels_total, sources=groups),
        out_shape=pltpu.HBM((sends, BLK * 4 * near, FB), jnp.float32),
        in_specs=[in_smem(), in_vmem(), in_vmem()]
        + [pl.BlockSpec(memory_space=pl.ANY)] * (2 * groups),
        out_specs=in_hbm,
        scratch_shapes=[
            pltpu.VMEM((sends, BLK * 4 * near, FB), jnp.float32),
            pltpu.VMEM((2, groups * capacity, BLK * 2 * near, FB), jnp.float32),
            pltpu.SemaphoreType.DMA((2, groups)),
            pltpu.SemaphoreType.DMA((fibres,)),
        ],
        compiler_params=params(field.shape, field.shape, (2, groups * capacity, BLK * 2 * near, FB)),
        cost_estimate=cost(0, 4 * 4 * field.size),
        name="place",
    )(take_from, strength, own_total, *blocks)
    result = placed.reshape(fibres, channels, 2, near, 2, FB).transpose(0, 1, 2, 4, 3, 5)
    return result.reshape(fibres, channels, 2, 2, samples)


def solution(mesh):
    return jax.shard_map(
        local,
        mesh=mesh,
        in_specs=(P(None, "wave", None, None, "tm"), P(), P(), P(), P(), P()),
        out_specs=P(None, "wave", None, None, "tm"),
        check_vma=False,
    )
```

```python
import functools
import math

import jax
import jax.numpy as jnp
import numpy as np
from jax import lax
from jax.experimental import pallas as pl
from jax.experimental.pallas import tpu as pltpu
from jax.sharding import PartitionSpec as P

BLK = 2
FA = 16
FB = 128
NFFT = FA * FB
HALF = 2
MARGIN = 512
VALID = 1024
LEAD = MARGIN // FB
STEP = VALID // FB
SUB = 8
UNROLL = 4
LAG = 1
SPARE = 6 * 1024 * 1024


def split_bf16(values):
    high = values.astype(jnp.bfloat16)
    low = (values - high.astype(np.float64)).astype(jnp.bfloat16)
    return high, low


def matrix_tables():
    index = np.arange(FB)
    angle = 2.0 * np.pi * (np.outer(index, index) % FB) / FB
    cos, sin = np.cos(angle), np.sin(angle)
    forward = np.block([[cos, -sin], [sin, cos]])
    inverse = np.block([[cos, sin], [-sin, cos]])
    tables = []
    for matrix in (forward, inverse):
        high, low = split_bf16(matrix)
        tables.append(np.concatenate([high, low], axis=0))
    return tables


def twist_table():
    angle = 2.0 * np.pi * np.outer(np.arange(FA), np.arange(FB)) / NFFT
    table = np.stack([np.cos(angle), np.sin(angle)]).astype(np.float32)
    return np.ascontiguousarray(np.broadcast_to(table[:, :, None, :], (2, FA, SUB, FB)))


def filter_tables(spread, channel, channels_total):
    index = np.arange(FA)[:, None] + FA * np.arange(FB)[None, :]
    signed = np.where(index < NFFT // 2, index, index - NFFT).astype(np.float32)
    omega = jnp.asarray(signed) * (2.0 * math.pi / NFFT)
    offsets = (math.pi / 2.0) * (2.0 * channel.astype(jnp.float32) + 1.0 - channels_total)
    offsets = offsets / channels_total
    theta = spread[None, :, None] * (
        omega[:, None, :] ** 2 + 2.0 * omega[:, None, :] * offsets[None, :, None]
    )
    scale = 1.0 / NFFT
    return jnp.cos(theta) * scale, jnp.sin(theta) * scale


def cadd(a, b):
    return (a[0] + b[0], a[1] + b[1])


def csub(a, b):
    return (a[0] - b[0], a[1] - b[1])


def cturn(a, sign):
    return (-a[1], a[0]) if sign > 0 else (a[1], -a[0])


def croot(a, m, sign):
    m %= FA
    if m == 0:
        return a
    if m == 4:
        return cturn(a, sign)
    if m in (2, 6):
        h = np.float32(math.sqrt(0.5))
        c = h if m == 2 else -h
        s = h * sign
        if m == 2:
            if sign > 0:
                return ((a[0] - a[1]) * h, (a[0] + a[1]) * h)
            return ((a[0] + a[1]) * h, (a[1] - a[0]) * h)
        if sign > 0:
            return ((a[0] + a[1]) * (-h), (a[0] - a[1]) * h)
        return ((a[1] - a[0]) * h, (a[0] + a[1]) * (-h))
    c = np.float32(math.cos(2.0 * math.pi * m / FA))
    s = np.float32(sign * math.sin(2.0 * math.pi * m / FA))
    return (a[0] * c - a[1] * s, a[0] * s + a[1] * c)


def dft4(z, sign, keep=(0, 1, 2, 3)):
    even, odd = cadd(z[0], z[2]), cadd(z[1], z[3])
    out = {}
    if 0 in keep:
        out[0] = cadd(even, odd)
    if 2 in keep:
        out[2] = csub(even, odd)
    if 1 in keep or 3 in keep:
        base, turn = csub(z[0], z[2]), cturn(csub(z[1], z[3]), sign)
        if 1 in keep:
            out[1] = cadd(base, turn)
        if 3 in keep:
            out[3] = csub(base, turn)
    return out


def dft16(z, sign, keep=(0, 1, 2, 3)):
    inner = [dft4([z[4 * n1 + n2] for n1 in range(4)], sign) for n2 in range(4)]
    out = {}
    for k1 in range(4):
        column = [croot(inner[n2][k1], n2 * k1, sign) for n2 in range(4)]
        for k2, value in dft4(column, sign, keep).items():
            out[k1 + 4 * k2] = value
    return out


def sincos(x):
    n = jnp.round(x * np.float32(2.0 / math.pi))
    r = x - n * np.float32(1.5703125)
    r = r - n * np.float32(4.837512969970703125e-4)
    r = r - n * np.float32(7.54978995489188216e-8)
    q = n.astype(jnp.int32)
    r2 = r * r
    s = np.float32(-1.9515295891e-4) * r2 + np.float32(8.3321608736e-3)
    s = s * r2 + np.float32(-1.6666654611e-1)
    s = s * r2 * r + r
    c = np.float32(2.443315711809948e-5) * r2 + np.float32(-1.388731625493765e-3)
    c = c * r2 + np.float32(4.166664568298827e-2)
    c = c * r2 * r2 - np.float32(0.5) * r2 + np.float32(1.0)
    odd = (q & 1) == 1
    sine = jnp.where(odd, c, s)
    cosine = jnp.where(odd, s, c)
    sine = jnp.where((q & 2) == 2, -sine, sine)
    cosine = jnp.where(((q + 1) & 2) == 2, -cosine, cosine)
    return sine, cosine


def rotate_chunk(x_ref, q_ref, sel_ref, strength, tt, channels_total, fibres, slots, write):
    real, imag = x_ref[tt, 0], x_ref[tt, 1]
    power = real * real + imag * imag
    power = power[:slots] + power[slots:]
    if fibres == 1:
        total = q_ref[0, pl.ds(tt, 1), :]
    else:
        total = sel_ref[0] * q_ref[0, pl.ds(tt, 1), :]
        for f in range(1, fibres):
            total = total + sel_ref[f] * q_ref[f, pl.ds(tt, 1), :]
    phase = strength * (2.0 * total - power) * np.float32(1.0 / channels_total)
    sine, cosine = sincos(phase)
    sine = jnp.concatenate([sine, sine], axis=0)
    cosine = jnp.concatenate([cosine, cosine], axis=0)
    write(real * cosine - imag * sine, real * sine + imag * cosine)


def split_store(a_ref, base, column, value):
    high = value.astype(jnp.bfloat16)
    low = (value - high.astype(jnp.float32)).astype(jnp.bfloat16)
    rows = value.shape[0]
    a_ref[base : base + rows, column : column + FB] = high
    a_ref[base : base + rows, 2 * FB + column : 3 * FB + column] = low


def step_kernel(
    *refs, rotate, hold, fetch, leave, channels_total, fibres_in, fibres_out, slots
):
    refs = list(refs)
    x_ref = refs.pop(0)
    if rotate:
        q_ref, selin_ref, strength_ref = refs[:3]
        refs = refs[3:]
    selout_ref, fc_ref, fs_ref, tw_ref, wf_ref, wi_ref, u_out = refs[:7]
    refs = refs[7:]
    p_ref = refs.pop(0)
    rest_ref = refs.pop(0) if hold else None
    xs_ref = refs.pop(0) if rotate else x_ref
    u_ref, out_sems = (refs.pop(0), refs.pop(0)) if leave else (u_out, None)
    from_ref, in_sems = x_ref, None
    if fetch:
        x_ref, in_sems = refs.pop(0), refs.pop(0)
    lanes = refs
    chunks = x_ref.shape[0]
    held = u_ref.shape[2]
    groups = held // SUB
    half = slots // SUB

    if rotate:

        def turn(tt, carry):
            def write(real, imag):
                xs_ref[tt, 0] = real[:held]
                xs_ref[tt, 1] = imag[:held]
                if hold:
                    rest_ref[tt, 0] = real[held:]
                    rest_ref[tt, 1] = imag[held:]

            rotate_chunk(
                x_ref, q_ref, selin_ref, strength_ref[...], tt, channels_total, fibres_in, slots,
                write,
            )
            return carry

        if fetch:
            copies = []
            pieces = in_sems.shape[0]
            length = chunks // pieces
            for i in range(pieces):
                at = pl.ds(i * length, length)
                copies.append(
                    pltpu.make_async_copy(from_ref.at[at], x_ref.at[at], in_sems.at[i])
                )
                copies[-1].start()
            for i, copy in enumerate(copies):
                copy.wait()
                lax.fori_loop(i * length, (i + 1) * length, turn, 0, unroll=STEP)
        else:
            lax.fori_loop(0, chunks, turn, 0, unroll=STEP)

    def gather(j, a_ref, g):
        places = []
        for a in range(FA):
            at = j * STEP + (a - LEAD)
            at = jnp.where(at < 0, at + chunks, at)
            places.append(jnp.where(at >= chunks, at - chunks, at))
        rows = slice(g * SUB, (g + 1) * SUB)
        z = [(xs_ref[at, 0, rows, :], xs_ref[at, 1, rows, :]) for at in places]
        y = dft16(z, -1)
        for i in range(FA // 2):
            pair = []
            for k in (2 * i, 2 * i + 1):
                real, imag = y[k]
                if k:
                    c, s = tw_ref[0, k], tw_ref[1, k]
                    real, imag = real * c + imag * s, imag * c - real * s
                pair.append((real, imag))
            store_pair(a_ref, (g * FA + 2 * i) * SUB, pair)

    def shape(a_ref, z_ref, g):
        rows = slice((g % half) * SUB, (g % half + 1) * SUB)
        for i in range(FA // 2):
            pair = []
            for k in (2 * i, 2 * i + 1):
                at = (g * FA + k) * SUB
                real, imag = z_ref[at : at + SUB, :FB], z_ref[at : at + SUB, FB:]
                c, s = fc_ref[k, rows, :], fs_ref[k, rows, :]
                pair.append((real * c - imag * s, real * s + imag * c))
            store_pair(a_ref, (g * FA + 2 * i) * SUB, pair)

    def spread(j, z_ref, g):
        rows = slice(g * SUB, (g + 1) * SUB)
        z = []
        for k in range(FA):
            at = (g * FA + k) * SUB
            real, imag = z_ref[at : at + SUB, :FB], z_ref[at : at + SUB, FB:]
            if k:
                c, s = tw_ref[0, k], tw_ref[1, k]
                real, imag = real * c - imag * s, real * s + imag * c
            z.append((real, imag))
        y = dft16(z, 1, keep=(1, 2))
        for k in range(STEP):
            real, imag = y[LEAD + k]
            u_ref[j * STEP + k, 0, rows, :] = real
            u_ref[j * STEP + k, 1, rows, :] = imag

    def add_up(j):
        for k in range(STEP):
            tt = j * STEP + k
            power = None
            for p in range(held // slots):
                rows = slice(p * slots, (p + 1) * slots)
                real, imag = u_ref[tt, 0, rows, :], u_ref[tt, 1, rows, :]
                mine = real * real + imag * imag
                power = mine if power is None else power + mine
            for f in range(fibres_out):
                mine = power if fibres_out == 1 else power * selout_ref[f]
                p_ref[f, pl.ds(tt, 1), :] = jnp.sum(mine, axis=0, keepdims=True)

    count = len(lanes) // 4
    size = FA * SUB

    def blocks(n, carry):
        stage = [lanes[4 * i : 4 * i + 4] for i in range(count)]

        def times(a_ref, w_ref, z_ref, g):
            at = slice(g * size, (g + 1) * size)
            z_ref[at, :] = product(a_ref[at, :], w_ref)

        units = [(i, g) for i in range(count) for g in range(groups)]

        def unit(turn, stages_back):
            at = turn - stages_back * LAG
            return units[at] if 0 <= at < len(units) else None

        for turn in range(len(units) + 4 * LAG):
            if now := unit(turn, 4):
                i, g = now
                spread(n * count + i, stage[i][3], g)
                if g == groups - 1:
                    add_up(n * count + i)
            if now := unit(turn, 3):
                i, g = now
                times(stage[i][2], wi_ref, stage[i][3], g)
            if now := unit(turn, 2):
                i, g = now
                shape(stage[i][2], stage[i][1], g)
            if now := unit(turn, 1):
                i, g = now
                times(stage[i][0], wf_ref, stage[i][1], g)
            if now := unit(turn, 0):
                i, g = now
                gather(n * count + i, stage[i][0], g)
        return carry

    turns = chunks // STEP // count

    def leaving(n):
        at = pl.ds(n * count * STEP, count * STEP)
        return pltpu.make_async_copy(u_ref.at[at], u_out.at[at], out_sems.at[n])

    def blocks_out(n, carry):
        blocks(n, carry)
        leaving(n).start()
        return carry

    if leave:
        lax.fori_loop(0, turns, blocks_out, 0)
        for n in range(turns):
            leaving(n).wait()
    else:
        lax.fori_loop(0, turns, blocks, 0)


def product(operand, w_ref):
    width = 2 * FB
    high, low = operand[:, :width], operand[:, width:]
    matrix_high, matrix_low = w_ref[:width, :], w_ref[width:, :]
    return (
        jnp.dot(high, matrix_high, preferred_element_type=jnp.float32)
        + jnp.dot(high, matrix_low, preferred_element_type=jnp.float32)
        + jnp.dot(low, matrix_high, preferred_element_type=jnp.float32)
    )


def store_pair(a_ref, base, pair):
    for part in range(2):
        split_store(a_ref, base, part * FB, jnp.concatenate([pair[0][part], pair[1][part]], axis=0))


def step_scratch(rows, count):
    operand = pltpu.VMEM((FA * rows, 4 * FB), jnp.bfloat16)
    product = pltpu.VMEM((FA * rows, 2 * FB), jnp.float32)
    return [operand, product, operand, product] * count


def pack_kernel(count_ref, x_hbm, o_hbm, x_ref, o_ref, sems, *, units, slots, channels):
    rows = 2 * slots
    span = o_ref.shape[1] // rows
    strips = sems.shape[1]
    length, devices = x_ref.shape[0] // strips, o_ref.shape[0] // strips
    base = lax.axis_index("wave") * channels

    def copy_in(i):
        at = pl.ds(i * length, length)
        return pltpu.make_async_copy(x_hbm.at[at], x_ref.at[at], sems.at[0, i])

    def copy_out(i):
        at = pl.ds(i * devices, devices)
        return pltpu.make_async_copy(o_ref.at[at], o_hbm.at[at], sems.at[1, i])

    for i in range(strips):
        copy_in(i).start()
    for i in range(strips):
        copy_in(i).wait()
        for g in range(i * devices, (i + 1) * devices):
            for p in range(2):
                values = [jnp.zeros((span, FB), jnp.float32)] * slots
                for u in range(units):
                    unit = g * units + u
                    lit = base + unit % channels < count_ref[unit // channels]
                    at = (unit * 2 + p) * span
                    values[u] = jnp.where(lit, x_ref[at : at + span, :], 0.0)
                turned = jnp.swapaxes(jnp.stack(values), 0, 1)
                for r in range(span):
                    at = r * rows + p * slots
                    o_ref[g, at : at + slots, :] = turned[r]
        copy_out(i).start()
    for i in range(strips):
        copy_out(i).wait()


def send_kernel(item_ref, count_ref, x_ref, *refs, units, slots):
    *out_refs, held_ref, turned_ref, sems = refs
    capacity, near = held_ref.shape[1], held_ref.shape[2] // (2 * BLK)
    for g in range(x_ref.shape[0]):
        for part in range(2):
            rows = [x_ref[g, (2 * k + part) * slots : (2 * k + part + 1) * slots, :] for k in range(near)]
            turned_ref[g, :, part] = jnp.swapaxes(jnp.stack(rows), 0, 1)
    several = math.gcd(capacity, 4)
    copies = []
    for s, out_ref in enumerate(out_refs):
        o_ref = held_ref.at[s]

        def body(m, carry, s=s, o_ref=o_ref):
            for k in range(several):
                n = m * several + k
                for c in range(BLK):
                    channel = item_ref[s * capacity + n] * BLK + c
                    g = channel // units
                    u = channel - g * units
                    for part in range(2):
                        at = (c * 2 + part) * near
                        o_ref[n, at : at + near, :] = turned_ref[g, u, part]
            return carry

        lax.fori_loop(0, (count_ref[s] + several - 1) // several, body, 0)
        copies.append(pltpu.make_async_copy(o_ref, out_ref, sems.at[s]))
        copies[-1].start()
    for copy in copies:
        copy.wait()


def place_kernel(from_ref, strength_ref, q_ref, *refs, channels_total, sources):
    in_refs, (o_hbm, o_ref, held_ref, sems, out_sems) = refs[: 2 * sources], refs[2 * sources :]
    capacity, near = in_refs[0].shape[0], in_refs[0].shape[1] // (2 * BLK)
    copies = []
    for p in range(2):
        for s in range(sources):
            copies.append(
                pltpu.make_async_copy(
                    in_refs[p * sources + s],
                    held_ref.at[p, pl.ds(s * capacity, capacity)],
                    sems.at[p, s],
                )
            )
    for copy in copies:
        copy.start()
    for copy in copies:
        copy.wait()
    copies = []
    fibres = q_ref.shape[0]
    group_blocks = o_ref.shape[0] // fibres
    for f in range(fibres):
        total = 2.0 * q_ref[f]
        strength = strength_ref[f]

        def body(b, carry, f=f, total=total, strength=strength):
            n = f * group_blocks + b
            source = from_ref[n]
            for c in range(BLK):
                parts = []
                power = None
                for p in range(2):
                    at = c * 2 * near
                    real = held_ref[p, source, at : at + near, :]
                    imag = held_ref[p, source, at + near : at + 2 * near, :]
                    parts.append((real, imag))
                    mine = real * real + imag * imag
                    power = mine if power is None else power + mine
                phase = strength * (total - power) * np.float32(1.0 / channels_total)
                sine, cosine = sincos(phase)
                for p, (real, imag) in enumerate(parts):
                    at = (c * 2 + p) * 2 * near
                    o_ref[n, pl.ds(at, near, stride=2), :] = real * cosine - imag * sine
                    o_ref[n, pl.ds(at + 1, near, stride=2), :] = real * sine + imag * cosine
            return carry

        lax.fori_loop(0, group_blocks, body, 0, unroll=4)
        at = pl.ds(f * group_blocks, group_blocks)
        copies.append(pltpu.make_async_copy(o_ref.at[at], o_hbm.at[at], out_sems.at[f]))
        copies[-1].start()
    for copy in copies:
        copy.wait()


def params(*shapes):
    return pltpu.CompilerParams(
        vmem_limit_bytes=SPARE + sum(4 * math.prod(shape) for shape in shapes)
    )


def cost(flops, moved):
    return pl.CostEstimate(flops=int(flops), bytes_accessed=int(moved), transcendentals=0)


def in_vmem():
    return pl.BlockSpec(memory_space=pltpu.VMEM)


def in_smem():
    return pl.BlockSpec(memory_space=pltpu.SMEM)


def summed(values, rounds):
    size = lax.axis_size("wave") * lax.axis_size("tm")
    for bits in rounds:
        masks = [0]
        for bit in bits:
            masks += [mask | bit for mask in masks]
        others = [
            lax.ppermute(values, ("wave", "tm"), [(i, i ^ mask) for i in range(size)])
            for mask in masks[1:]
        ]
        for other in others:
            values = values + other
    return values


def route_tables(route_fibre, route_slot, groups, my_group, capacity):
    fibres = route_slot.shape[0]
    group_blocks = route_slot.shape[1] // groups
    sends = fibres * group_blocks

    def by_group(table):
        return table.reshape(fibres, groups, group_blocks).transpose(1, 0, 2).reshape(groups, sends)

    slot_all, fibre_all = by_group(route_slot), by_group(route_fibre)
    target_all = slot_all // group_blocks
    landing_all = fibre_all * group_blocks + slot_all % group_blocks
    position = jnp.arange(sends)
    earlier = (target_all[:, :, None] == target_all[:, None, :]) & (
        position[None, None, :] < position[None, :, None]
    )
    arrival_all = jnp.sum(earlier.astype(jnp.int32), axis=2)
    my_target = lax.dynamic_index_in_dim(target_all, my_group, 0, keepdims=False)
    my_arrival = lax.dynamic_index_in_dim(arrival_all, my_group, 0, keepdims=False)
    partner = my_target ^ my_group
    slot_index = partner * capacity + my_arrival
    matches = slot_index[None, :] == jnp.arange(groups * capacity)[:, None]
    source_item = jnp.sum(jnp.where(matches, position[None, :], 0), axis=1)
    counts = jnp.sum((partner[None, :] == jnp.arange(groups)[:, None]).astype(jnp.int32), axis=1)
    mine = target_all == my_group
    receive_slot = (jnp.arange(groups) ^ my_group)[:, None] * capacity + arrival_all
    hits = mine[:, :, None] & (landing_all[:, :, None] == position[None, None, :])
    take_from = jnp.sum(jnp.where(hits, receive_slot[:, :, None], 0), axis=(0, 1))
    return source_item.astype(jnp.int32), counts, take_from.astype(jnp.int32)


def time_parts(values, bits):
    times = lax.axis_size("tm")
    count = times.bit_length() - 1
    masks = [0]
    for b in bits:
        masks += [mask | (1 << b) for mask in masks]
    kept = None
    for mask in masks:
        part = values
        for b in bits:
            side = ((lax.axis_index("tm") ^ mask) >> b) & 1
            part = lax.dynamic_index_in_dim(part, side, count - b)
        if mask:
            part = lax.ppermute(part, "tm", [(i, i ^ mask) for i in range(times)])
        kept = part if kept is None else kept + part
    return kept


def local(field, lit_count, route_fibre, route_slot, dispersion, nonlinearity):
    fibres, channels, samples = field.shape[0], field.shape[1], field.shape[-1]
    groups, times = lax.axis_size("wave"), lax.axis_size("tm")
    my_group, my_time = lax.axis_index("wave"), lax.axis_index("tm")
    channels_total = groups * channels
    units = fibres * channels // times
    slots = -(-units // SUB) * SUB
    rows = 2 * slots
    near = samples // FB
    chunks = times * near
    same_fibre = channels % units == 0
    group_blocks = channels // BLK
    sends = fibres * group_blocks
    capacity = 2 * sends // groups

    unit = my_time * units + jnp.minimum(jnp.arange(slots), units - 1)
    in_fibre = unit // channels
    in_channel = my_group * channels + unit % channels
    in_block = in_channel // BLK
    out_fibre = route_fibre[in_fibre, in_block]
    out_channel = route_slot[in_fibre, in_block] * BLK + in_channel % BLK
    real_slot = jnp.arange(slots) < units

    def wide(values):
        return jnp.broadcast_to(values.astype(jnp.float32)[..., None], values.shape + (FB,))

    def selection(fibre):
        chosen = (fibre[None, :] == jnp.arange(fibres)[:, None]) & real_slot[None, :]
        return wide(chosen)

    spans = []
    for span, (fibre, channel) in enumerate(((in_fibre, in_channel), (out_fibre, out_channel))):
        spread, strength = dispersion[span][fibre], nonlinearity[span][fibre]
        fc, fs = filter_tables(spread, channel, channels_total)
        spans.append((fc, fs, wide(strength), selection(fibre)))
    source_item, counts, take_from = route_tables(route_fibre, route_slot, groups, my_group, capacity)

    wave_bits = [times << b for b in range(groups.bit_length() - 1)]
    time_bits = [1 << b for b in range(times.bit_length() - 1)]
    wave_rounds = [(bit,) for bit in wave_bits]
    all_rounds = [(bit,) for bit in wave_bits + time_bits]
    shared = channels // units if same_fibre else 0
    fibre_bits = wave_bits + time_bits[: max(shared.bit_length() - 1, 0)]
    fibre_rounds = [tuple(fibre_bits[:1])]
    fibre_rounds += [tuple(fibre_bits[i : i + 2]) for i in range(1, len(fibre_bits), 2)]

    def natural_rows(values):
        split = values.reshape(fibres, channels, 2, 2, near, FB)
        return split.transpose(0, 1, 2, 4, 3, 5).reshape(-1, FB)

    strips = math.gcd(times, 4)
    in_hbm = pl.BlockSpec(memory_space=pltpu.HBM)
    natural = pltpu.with_memory_space_constraint(natural_rows(field), pltpu.HBM)
    shape = (times, 2 * near * rows, FB)
    packed = pl.pallas_call(
        functools.partial(pack_kernel, units=units, slots=slots, channels=channels),
        out_shape=pltpu.HBM(shape, jnp.float32),
        in_specs=[in_smem(), in_hbm],
        out_specs=in_hbm,
        scratch_shapes=[
            pltpu.VMEM(natural.shape, jnp.float32),
            pltpu.VMEM(shape, jnp.float32),
            pltpu.SemaphoreType.DMA((2, strips)),
        ],
        compiler_params=params(field.shape, shape),
        name="pack",
    )(lit_count, natural)
    wave_form = lax.all_to_all(packed, "tm", split_axis=0, concat_axis=0, tiled=True)
    wave_form = wave_form.reshape(chunks, 2, rows, FB)

    twist = jnp.asarray(twist_table())
    forward, inverse = (jnp.asarray(table) for table in matrix_tables())
    def dispersed(x, step, total, q_fibres, fibres_out, hold):
        fc, fs, _, select = spans[step // HALF]
        rotate = total is not None
        operands = [x]
        if rotate:
            operands += [total, spans[(step - 1) // HALF][3], spans[(step - 1) // HALF][2]]
        operands += [select, fc, fs, twist, forward, inverse]
        held = slots if hold else x.shape[2]
        shape = (chunks, 2, held, FB)
        leave, fetch = not rotate or hold, step == 1
        wave = (pltpu.HBM if leave else jax.ShapeDtypeStruct)(shape, jnp.float32)
        outs = [wave, jax.ShapeDtypeStruct((fibres_out, chunks, FB), jnp.float32)]
        outs += [pltpu.HBM(shape, jnp.float32)] if hold else []
        specs_in = [in_vmem()] * len(operands)
        specs_out = [in_vmem()] * len(outs)
        unroll = math.gcd(UNROLL, chunks // STEP)
        scratch = [pltpu.VMEM(shape, jnp.float32)] if rotate else []
        if leave:
            specs_out[0] = pl.BlockSpec(memory_space=pltpu.HBM)
            turns = chunks // STEP // unroll
            scratch += [pltpu.VMEM(shape, jnp.float32), pltpu.SemaphoreType.DMA((turns,))]
        if fetch:
            specs_in[0] = pl.BlockSpec(memory_space=pltpu.HBM)
            operands[0] = pltpu.with_memory_space_constraint(x, pltpu.HBM)
            scratch += [
                pltpu.VMEM(x.shape, jnp.float32),
                pltpu.SemaphoreType.DMA((math.gcd(4, chunks // STEP),)),
            ]
        scratch += step_scratch(held, unroll)
        return pl.pallas_call(
            functools.partial(
                step_kernel, rotate=rotate, hold=hold, fetch=fetch, leave=leave,
                channels_total=channels_total, fibres_in=q_fibres, fibres_out=fibres_out,
                slots=slots,
            ),
            out_shape=tuple(outs),
            in_specs=specs_in,
            out_specs=tuple(specs_out),
            scratch_shapes=scratch,
            compiler_params=params(*[x.shape] * 5, *[ref.shape for ref in scratch]),
            cost_estimate=cost(chunks * held * FB * 6400, 4 * x.size * 4),
            name="step",
        )(*operands)

    total, q_fibres = None, 0
    for step in range(2 * HALF - 1):
        fibres_out = 1 if (step < HALF and same_fibre) else fibres
        wave_form, partial = dispersed(wave_form, step, total, q_fibres, fibres_out, False)
        if fibres_out == 1:
            total = summed(partial, fibre_rounds)
        else:
            cut = fibres_out // 2
            there = all_rounds[:1] + all_rounds[2:] + all_rounds[1:2]
            back = all_rounds[:1] + all_rounds[:0:-1]
            total = jnp.concatenate(
                [summed(partial[:cut], there), summed(partial[cut:], back)], axis=0
            )
        q_fibres = fibres_out

    last = 2 * HALF - 1

    def to_times(values):
        values = values.reshape(times, 2 * near * slots, FB)
        return lax.all_to_all(values, "tm", split_axis=0, concat_axis=0, tiled=True)

    def prepared(values):
        block = pltpu.HBM((capacity, BLK * 2 * near, FB), jnp.float32)
        return pl.pallas_call(
            functools.partial(send_kernel, units=units, slots=slots),
            out_shape=(block,) * groups,
            in_specs=[in_smem(), in_smem(), in_vmem()],
            out_specs=(pl.BlockSpec(memory_space=pltpu.HBM),) * groups,
            scratch_shapes=[
                pltpu.VMEM((groups,) + block.shape, jnp.float32),
                pltpu.VMEM((times, slots, 2, near, FB), jnp.float32),
                pltpu.SemaphoreType.DMA((groups,)),
            ],
            compiler_params=params(values.shape, values.shape, (groups,) + block.shape),
            cost_estimate=cost(0, 4 * 4 * values.size),
            name="send",
        )(source_item, counts, values)

    def to_groups(outgoing):
        moved = [pltpu.with_memory_space_constraint(outgoing[0], pltpu.HBM)]
        for s in range(1, groups):
            moved.append(lax.ppermute(outgoing[s], "wave", [(i, i ^ s) for i in range(groups)]))
        return moved

    first, partial, rest = dispersed(wave_form, last, total, q_fibres, fibres, True)
    second, more = dispersed(rest, last, None, 0, fibres, False)
    bits = list(range(times.bit_length() - 1))
    partial = summed(partial + more, wave_rounds)
    partial = partial.reshape([fibres] + [2] * len(bits) + [near, FB])
    partial = time_parts(partial, bits[:1])
    first, partial = lax.optimization_barrier((to_times(first), partial))
    first = prepared(first)
    first, second = lax.optimization_barrier((first, second))
    second, *first = lax.optimization_barrier((to_times(second), *to_groups(first)))
    blocks = first + to_groups(prepared(second))
    for i in range(1, len(bits), 2):
        partial = time_parts(partial, bits[i : i + 2])
    own_total = partial.reshape(fibres, near, FB)
    strength = jnp.broadcast_to(nonlinearity[1][:, None, None], (fibres, near, FB))
    placed = pl.pallas_call(
        functools.partial(place_kernel, channels_total=channels_total, sources=groups),
        out_shape=pltpu.HBM((sends, BLK * 4 * near, FB), jnp.float32),
        in_specs=[in_smem(), in_vmem(), in_vmem()]
        + [pl.BlockSpec(memory_space=pl.ANY)] * (2 * groups),
        out_specs=in_hbm,
        scratch_shapes=[
            pltpu.VMEM((sends, BLK * 4 * near, FB), jnp.float32),
            pltpu.VMEM((2, groups * capacity, BLK * 2 * near, FB), jnp.float32),
            pltpu.SemaphoreType.DMA((2, groups)),
            pltpu.SemaphoreType.DMA((fibres,)),
        ],
        compiler_params=params(field.shape, field.shape, (2, groups * capacity, BLK * 2 * near, FB)),
        cost_estimate=cost(0, 4 * 4 * field.size),
        name="place",
    )(take_from, strength, own_total, *blocks)
    result = placed.reshape(fibres, channels, 2, near, 2, FB).transpose(0, 1, 2, 4, 3, 5)
    return result.reshape(fibres, channels, 2, 2, samples)


def solution(mesh):
    return jax.shard_map(
        local,
        mesh=mesh,
        in_specs=(P(None, "wave", None, None, "tm"), P(), P(), P(), P(), P()),
        out_specs=P(None, "wave", None, None, "tm"),
        check_vma=False,
    )
```

```python
import functools
import math

import jax
import jax.numpy as jnp
import numpy as np
from jax import lax
from jax.experimental import pallas as pl
from jax.experimental.pallas import tpu as pltpu
from jax.sharding import PartitionSpec as P

BLK = 2
FA = 16
FB = 128
NFFT = FA * FB
HALF = 2
MARGIN = 512
VALID = 1024
LEAD = MARGIN // FB
STEP = VALID // FB
SUB = 8
UNROLL = 4
LAG = 1
SPARE = 6 * 1024 * 1024


def split_bf16(values):
    high = values.astype(jnp.bfloat16)
    low = (values - high.astype(np.float64)).astype(jnp.bfloat16)
    return high, low


def matrix_tables():
    index = np.arange(FB)
    angle = 2.0 * np.pi * (np.outer(index, index) % FB) / FB
    cos, sin = np.cos(angle), np.sin(angle)
    forward = np.block([[cos, -sin], [sin, cos]])
    inverse = np.block([[cos, sin], [-sin, cos]])
    tables = []
    for matrix in (forward, inverse):
        high, low = split_bf16(matrix)
        tables.append(np.concatenate([high, low], axis=0))
    return tables


def twist_table():
    angle = 2.0 * np.pi * np.outer(np.arange(FA), np.arange(FB)) / NFFT
    table = np.stack([np.cos(angle), np.sin(angle)]).astype(np.float32)
    return np.ascontiguousarray(np.broadcast_to(table[:, :, None, :], (2, FA, SUB, FB)))


def filter_tables(spread, channel, channels_total):
    index = np.arange(FA)[:, None] + FA * np.arange(FB)[None, :]
    signed = np.where(index < NFFT // 2, index, index - NFFT).astype(np.float32)
    omega = jnp.asarray(signed) * (2.0 * math.pi / NFFT)
    offsets = (math.pi / 2.0) * (2.0 * channel.astype(jnp.float32) + 1.0 - channels_total)
    offsets = offsets / channels_total
    theta = spread[None, :, None] * (
        omega[:, None, :] ** 2 + 2.0 * omega[:, None, :] * offsets[None, :, None]
    )
    scale = 1.0 / NFFT
    return jnp.cos(theta) * scale, jnp.sin(theta) * scale


def cadd(a, b):
    return (a[0] + b[0], a[1] + b[1])


def csub(a, b):
    return (a[0] - b[0], a[1] - b[1])


def cturn(a, sign):
    return (-a[1], a[0]) if sign > 0 else (a[1], -a[0])


def croot(a, m, sign):
    m %= FA
    if m == 0:
        return a
    if m == 4:
        return cturn(a, sign)
    if m in (2, 6):
        h = np.float32(math.sqrt(0.5))
        c = h if m == 2 else -h
        s = h * sign
        if m == 2:
            if sign > 0:
                return ((a[0] - a[1]) * h, (a[0] + a[1]) * h)
            return ((a[0] + a[1]) * h, (a[1] - a[0]) * h)
        if sign > 0:
            return ((a[0] + a[1]) * (-h), (a[0] - a[1]) * h)
        return ((a[1] - a[0]) * h, (a[0] + a[1]) * (-h))
    c = np.float32(math.cos(2.0 * math.pi * m / FA))
    s = np.float32(sign * math.sin(2.0 * math.pi * m / FA))
    return (a[0] * c - a[1] * s, a[0] * s + a[1] * c)


def dft4(z, sign, keep=(0, 1, 2, 3)):
    even, odd = cadd(z[0], z[2]), cadd(z[1], z[3])
    out = {}
    if 0 in keep:
        out[0] = cadd(even, odd)
    if 2 in keep:
        out[2] = csub(even, odd)
    if 1 in keep or 3 in keep:
        base, turn = csub(z[0], z[2]), cturn(csub(z[1], z[3]), sign)
        if 1 in keep:
            out[1] = cadd(base, turn)
        if 3 in keep:
            out[3] = csub(base, turn)
    return out


def dft16(z, sign, keep=(0, 1, 2, 3)):
    inner = [dft4([z[4 * n1 + n2] for n1 in range(4)], sign) for n2 in range(4)]
    out = {}
    for k1 in range(4):
        column = [croot(inner[n2][k1], n2 * k1, sign) for n2 in range(4)]
        for k2, value in dft4(column, sign, keep).items():
            out[k1 + 4 * k2] = value
    return out


def sincos(x):
    n = jnp.round(x * np.float32(2.0 / math.pi))
    r = x - n * np.float32(1.5703125)
    r = r - n * np.float32(4.837512969970703125e-4)
    r = r - n * np.float32(7.54978995489188216e-8)
    q = n.astype(jnp.int32)
    r2 = r * r
    s = np.float32(-1.9515295891e-4) * r2 + np.float32(8.3321608736e-3)
    s = s * r2 + np.float32(-1.6666654611e-1)
    s = s * r2 * r + r
    c = np.float32(2.443315711809948e-5) * r2 + np.float32(-1.388731625493765e-3)
    c = c * r2 + np.float32(4.166664568298827e-2)
    c = c * r2 * r2 - np.float32(0.5) * r2 + np.float32(1.0)
    odd = (q & 1) == 1
    sine = jnp.where(odd, c, s)
    cosine = jnp.where(odd, s, c)
    sine = jnp.where((q & 2) == 2, -sine, sine)
    cosine = jnp.where(((q + 1) & 2) == 2, -cosine, cosine)
    return sine, cosine


def rotate_chunk(x_ref, q_ref, sel_ref, strength, tt, channels_total, fibres, slots, write):
    real, imag = x_ref[tt, 0], x_ref[tt, 1]
    power = real * real + imag * imag
    power = power[:slots] + power[slots:]
    if fibres == 1:
        total = q_ref[0, pl.ds(tt, 1), :]
    else:
        total = sel_ref[0] * q_ref[0, pl.ds(tt, 1), :]
        for f in range(1, fibres):
            total = total + sel_ref[f] * q_ref[f, pl.ds(tt, 1), :]
    phase = strength * (2.0 * total - power) * np.float32(1.0 / channels_total)
    sine, cosine = sincos(phase)
    sine = jnp.concatenate([sine, sine], axis=0)
    cosine = jnp.concatenate([cosine, cosine], axis=0)
    write(real * cosine - imag * sine, real * sine + imag * cosine)


def split_store(a_ref, base, column, value):
    high = value.astype(jnp.bfloat16)
    low = (value - high.astype(jnp.float32)).astype(jnp.bfloat16)
    rows = value.shape[0]
    a_ref[base : base + rows, column : column + FB] = high
    a_ref[base : base + rows, 2 * FB + column : 3 * FB + column] = low


def step_kernel(
    *refs, rotate, hold, fetch, leave, channels_total, fibres_in, fibres_out, slots
):
    refs = list(refs)
    x_ref = refs.pop(0)
    if rotate:
        q_ref, selin_ref, strength_ref = refs[:3]
        refs = refs[3:]
    selout_ref, fc_ref, fs_ref, tw_ref, wf_ref, wi_ref, u_out = refs[:7]
    refs = refs[7:]
    p_ref = refs.pop(0)
    rest_ref = refs.pop(0) if hold else None
    xs_ref = refs.pop(0) if rotate else x_ref
    u_ref, out_sems = (refs.pop(0), refs.pop(0)) if leave else (u_out, None)
    from_ref, in_sems = x_ref, None
    if fetch:
        x_ref, in_sems = refs.pop(0), refs.pop(0)
    lanes = refs
    chunks = x_ref.shape[0]
    held = u_ref.shape[2]
    groups = held // SUB
    half = slots // SUB

    if rotate:

        def turn(tt, carry):
            def write(real, imag):
                xs_ref[tt, 0] = real[:held]
                xs_ref[tt, 1] = imag[:held]
                if hold:
                    rest_ref[tt, 0] = real[held:]
                    rest_ref[tt, 1] = imag[held:]

            rotate_chunk(
                x_ref, q_ref, selin_ref, strength_ref[...], tt, channels_total, fibres_in, slots,
                write,
            )
            return carry

        if fetch:
            copies = []
            pieces = in_sems.shape[0]
            length = chunks // pieces
            for i in range(pieces):
                at = pl.ds(i * length, length)
                copies.append(
                    pltpu.make_async_copy(from_ref.at[at], x_ref.at[at], in_sems.at[i])
                )
                copies[-1].start()
            for i, copy in enumerate(copies):
                copy.wait()
                lax.fori_loop(i * length, (i + 1) * length, turn, 0, unroll=STEP)
        else:
            lax.fori_loop(0, chunks, turn, 0, unroll=STEP)

    def gather(j, a_ref, g):
        places = []
        for a in range(FA):
            at = j * STEP + (a - LEAD)
            at = jnp.where(at < 0, at + chunks, at)
            places.append(jnp.where(at >= chunks, at - chunks, at))
        rows = slice(g * SUB, (g + 1) * SUB)
        z = [(xs_ref[at, 0, rows, :], xs_ref[at, 1, rows, :]) for at in places]
        y = dft16(z, -1)
        for i in range(FA // 2):
            pair = []
            for k in (2 * i, 2 * i + 1):
                real, imag = y[k]
                if k:
                    c, s = tw_ref[0, k], tw_ref[1, k]
                    real, imag = real * c + imag * s, imag * c - real * s
                pair.append((real, imag))
            store_pair(a_ref, (g * FA + 2 * i) * SUB, pair)

    def shape(a_ref, z_ref, g):
        rows = slice((g % half) * SUB, (g % half + 1) * SUB)
        for i in range(FA // 2):
            pair = []
            for k in (2 * i, 2 * i + 1):
                at = (g * FA + k) * SUB
                real, imag = z_ref[at : at + SUB, :FB], z_ref[at : at + SUB, FB:]
                c, s = fc_ref[k, rows, :], fs_ref[k, rows, :]
                pair.append((real * c - imag * s, real * s + imag * c))
            store_pair(a_ref, (g * FA + 2 * i) * SUB, pair)

    def spread(j, z_ref, g):
        rows = slice(g * SUB, (g + 1) * SUB)
        z = []
        for k in range(FA):
            at = (g * FA + k) * SUB
            real, imag = z_ref[at : at + SUB, :FB], z_ref[at : at + SUB, FB:]
            if k:
                c, s = tw_ref[0, k], tw_ref[1, k]
                real, imag = real * c - imag * s, real * s + imag * c
            z.append((real, imag))
        y = dft16(z, 1, keep=(1, 2))
        for k in range(STEP):
            real, imag = y[LEAD + k]
            u_ref[j * STEP + k, 0, rows, :] = real
            u_ref[j * STEP + k, 1, rows, :] = imag

    def add_up(j):
        for k in range(STEP):
            tt = j * STEP + k
            power = None
            for p in range(held // slots):
                rows = slice(p * slots, (p + 1) * slots)
                real, imag = u_ref[tt, 0, rows, :], u_ref[tt, 1, rows, :]
                mine = real * real + imag * imag
                power = mine if power is None else power + mine
            for f in range(fibres_out):
                mine = power if fibres_out == 1 else power * selout_ref[f]
                p_ref[f, pl.ds(tt, 1), :] = jnp.sum(mine, axis=0, keepdims=True)

    count = len(lanes) // 4
    size = FA * SUB

    def blocks(n, carry):
        stage = [lanes[4 * i : 4 * i + 4] for i in range(count)]

        def times(a_ref, w_ref, z_ref, g):
            at = slice(g * size, (g + 1) * size)
            z_ref[at, :] = product(a_ref[at, :], w_ref)

        units = [(i, g) for i in range(count) for g in range(groups)]

        def unit(turn, stages_back):
            at = turn - stages_back * LAG
            return units[at] if 0 <= at < len(units) else None

        for turn in range(len(units) + 4 * LAG):
            if now := unit(turn, 4):
                i, g = now
                spread(n * count + i, stage[i][3], g)
                if g == groups - 1:
                    add_up(n * count + i)
            if now := unit(turn, 3):
                i, g = now
                times(stage[i][2], wi_ref, stage[i][3], g)
            if now := unit(turn, 2):
                i, g = now
                shape(stage[i][2], stage[i][1], g)
            if now := unit(turn, 1):
                i, g = now
                times(stage[i][0], wf_ref, stage[i][1], g)
            if now := unit(turn, 0):
                i, g = now
                gather(n * count + i, stage[i][0], g)
        return carry

    turns = chunks // STEP // count

    def leaving(n):
        at = pl.ds(n * count * STEP, count * STEP)
        return pltpu.make_async_copy(u_ref.at[at], u_out.at[at], out_sems.at[n])

    def blocks_out(n, carry):
        blocks(n, carry)
        leaving(n).start()
        return carry

    if leave:
        lax.fori_loop(0, turns, blocks_out, 0)
        for n in range(turns):
            leaving(n).wait()
    else:
        lax.fori_loop(0, turns, blocks, 0)


def product(operand, w_ref):
    width = 2 * FB
    high, low = operand[:, :width], operand[:, width:]
    matrix_high, matrix_low = w_ref[:width, :], w_ref[width:, :]
    return (
        jnp.dot(high, matrix_high, preferred_element_type=jnp.float32)
        + jnp.dot(high, matrix_low, preferred_element_type=jnp.float32)
        + jnp.dot(low, matrix_high, preferred_element_type=jnp.float32)
    )


def store_pair(a_ref, base, pair):
    for part in range(2):
        split_store(a_ref, base, part * FB, jnp.concatenate([pair[0][part], pair[1][part]], axis=0))


def step_scratch(rows, count):
    operand = pltpu.VMEM((FA * rows, 4 * FB), jnp.bfloat16)
    product = pltpu.VMEM((FA * rows, 2 * FB), jnp.float32)
    return [operand, product, operand, product] * count


def pack_kernel(count_ref, x_hbm, o_hbm, x_ref, o_ref, sems, *, units, slots, channels):
    rows = 2 * slots
    span = o_ref.shape[1] // rows
    strips = sems.shape[1]
    length, devices = x_ref.shape[0] // strips, o_ref.shape[0] // strips
    base = lax.axis_index("wave") * channels

    def copy_in(i):
        at = pl.ds(i * length, length)
        return pltpu.make_async_copy(x_hbm.at[at], x_ref.at[at], sems.at[0, i])

    def copy_out(i):
        at = pl.ds(i * devices, devices)
        return pltpu.make_async_copy(o_ref.at[at], o_hbm.at[at], sems.at[1, i])

    for i in range(strips):
        copy_in(i).start()
    for i in range(strips):
        copy_in(i).wait()
        for g in range(i * devices, (i + 1) * devices):
            for p in range(2):
                values = [jnp.zeros((span, FB), jnp.float32)] * slots
                for u in range(units):
                    unit = g * units + u
                    lit = base + unit % channels < count_ref[unit // channels]
                    at = (unit * 2 + p) * span
                    values[u] = jnp.where(lit, x_ref[at : at + span, :], 0.0)
                turned = jnp.swapaxes(jnp.stack(values), 0, 1)
                for r in range(span):
                    at = r * rows + p * slots
                    o_ref[g, at : at + slots, :] = turned[r]
        copy_out(i).start()
    for i in range(strips):
        copy_out(i).wait()


def send_kernel(item_ref, count_ref, x_ref, *refs, units, slots):
    *out_refs, held_ref, turned_ref, sems = refs
    capacity, near = held_ref.shape[1], held_ref.shape[2] // (2 * BLK)
    for g in range(x_ref.shape[0]):
        for part in range(2):
            rows = [x_ref[g, (2 * k + part) * slots : (2 * k + part + 1) * slots, :] for k in range(near)]
            turned_ref[g, :, part] = jnp.swapaxes(jnp.stack(rows), 0, 1)
    several = math.gcd(capacity, 4)
    copies = []
    for s, out_ref in enumerate(out_refs):
        o_ref = held_ref.at[s]

        def body(m, carry, s=s, o_ref=o_ref):
            for k in range(several):
                n = m * several + k
                for c in range(BLK):
                    channel = item_ref[s * capacity + n] * BLK + c
                    g = channel // units
                    u = channel - g * units
                    for part in range(2):
                        at = (c * 2 + part) * near
                        o_ref[n, at : at + near, :] = turned_ref[g, u, part]
            return carry

        lax.fori_loop(0, (count_ref[s] + several - 1) // several, body, 0)
        copies.append(pltpu.make_async_copy(o_ref, out_ref, sems.at[s]))
        copies[-1].start()
    for copy in copies:
        copy.wait()


def place_kernel(from_ref, strength_ref, q_ref, *refs, channels_total, sources):
    in_refs, (o_hbm, o_ref, held_ref, sems, out_sems) = refs[: 2 * sources], refs[2 * sources :]
    capacity, near = in_refs[0].shape[0], in_refs[0].shape[1] // (2 * BLK)
    copies = []
    for p in range(2):
        for s in range(sources):
            copies.append(
                pltpu.make_async_copy(
                    in_refs[p * sources + s],
                    held_ref.at[p, pl.ds(s * capacity, capacity)],
                    sems.at[p, s],
                )
            )
    for copy in copies:
        copy.start()
    for copy in copies:
        copy.wait()
    copies = []
    fibres = q_ref.shape[0]
    group_blocks = o_ref.shape[0] // fibres
    for f in range(fibres):
        total = 2.0 * q_ref[f]
        strength = strength_ref[f]

        def body(b, carry, f=f, total=total, strength=strength):
            n = f * group_blocks + b
            source = from_ref[n]
            for c in range(BLK):
                parts = []
                power = None
                for p in range(2):
                    at = c * 2 * near
                    real = held_ref[p, source, at : at + near, :]
                    imag = held_ref[p, source, at + near : at + 2 * near, :]
                    parts.append((real, imag))
                    mine = real * real + imag * imag
                    power = mine if power is None else power + mine
                phase = strength * (total - power) * np.float32(1.0 / channels_total)
                sine, cosine = sincos(phase)
                for p, (real, imag) in enumerate(parts):
                    at = (c * 2 + p) * 2 * near
                    turned = jnp.stack([real * cosine - imag * sine, real * sine + imag * cosine])
                    o_ref[n, at : at + 2 * near, :] = jnp.swapaxes(turned, 0, 1).reshape(2 * near, FB)
            return carry

        lax.fori_loop(0, group_blocks, body, 0, unroll=4)
        at = pl.ds(f * group_blocks, group_blocks)
        copies.append(pltpu.make_async_copy(o_ref.at[at], o_hbm.at[at], out_sems.at[f]))
        copies[-1].start()
    for copy in copies:
        copy.wait()


def params(*shapes):
    return pltpu.CompilerParams(
        vmem_limit_bytes=SPARE + sum(4 * math.prod(shape) for shape in shapes)
    )


def cost(flops, moved):
    return pl.CostEstimate(flops=int(flops), bytes_accessed=int(moved), transcendentals=0)


def in_vmem():
    return pl.BlockSpec(memory_space=pltpu.VMEM)


def in_smem():
    return pl.BlockSpec(memory_space=pltpu.SMEM)


def summed(values, rounds):
    size = lax.axis_size("wave") * lax.axis_size("tm")
    for bits in rounds:
        masks = [0]
        for bit in bits:
            masks += [mask | bit for mask in masks]
        others = [
            lax.ppermute(values, ("wave", "tm"), [(i, i ^ mask) for i in range(size)])
            for mask in masks[1:]
        ]
        for other in others:
            values = values + other
    return values


def route_tables(route_fibre, route_slot, groups, my_group, capacity):
    fibres = route_slot.shape[0]
    group_blocks = route_slot.shape[1] // groups
    sends = fibres * group_blocks

    def by_group(table):
        return table.reshape(fibres, groups, group_blocks).transpose(1, 0, 2).reshape(groups, sends)

    slot_all, fibre_all = by_group(route_slot), by_group(route_fibre)
    target_all = slot_all // group_blocks
    landing_all = fibre_all * group_blocks + slot_all % group_blocks
    position = jnp.arange(sends)
    earlier = (target_all[:, :, None] == target_all[:, None, :]) & (
        position[None, None, :] < position[None, :, None]
    )
    arrival_all = jnp.sum(earlier.astype(jnp.int32), axis=2)
    my_target = lax.dynamic_index_in_dim(target_all, my_group, 0, keepdims=False)
    my_arrival = lax.dynamic_index_in_dim(arrival_all, my_group, 0, keepdims=False)
    partner = my_target ^ my_group
    slot_index = partner * capacity + my_arrival
    matches = slot_index[None, :] == jnp.arange(groups * capacity)[:, None]
    source_item = jnp.sum(jnp.where(matches, position[None, :], 0), axis=1)
    counts = jnp.sum((partner[None, :] == jnp.arange(groups)[:, None]).astype(jnp.int32), axis=1)
    mine = target_all == my_group
    receive_slot = (jnp.arange(groups) ^ my_group)[:, None] * capacity + arrival_all
    hits = mine[:, :, None] & (landing_all[:, :, None] == position[None, None, :])
    take_from = jnp.sum(jnp.where(hits, receive_slot[:, :, None], 0), axis=(0, 1))
    return source_item.astype(jnp.int32), counts, take_from.astype(jnp.int32)


def time_parts(values, bits):
    times = lax.axis_size("tm")
    count = times.bit_length() - 1
    masks = [0]
    for b in bits:
        masks += [mask | (1 << b) for mask in masks]
    kept = None
    for mask in masks:
        part = values
        for b in bits:
            side = ((lax.axis_index("tm") ^ mask) >> b) & 1
            part = lax.dynamic_index_in_dim(part, side, count - b)
        if mask:
            part = lax.ppermute(part, "tm", [(i, i ^ mask) for i in range(times)])
        kept = part if kept is None else kept + part
    return kept


def local(field, lit_count, route_fibre, route_slot, dispersion, nonlinearity):
    fibres, channels, samples = field.shape[0], field.shape[1], field.shape[-1]
    groups, times = lax.axis_size("wave"), lax.axis_size("tm")
    my_group, my_time = lax.axis_index("wave"), lax.axis_index("tm")
    channels_total = groups * channels
    units = fibres * channels // times
    slots = -(-units // SUB) * SUB
    rows = 2 * slots
    near = samples // FB
    chunks = times * near
    same_fibre = channels % units == 0
    group_blocks = channels // BLK
    sends = fibres * group_blocks
    capacity = 2 * sends // groups

    unit = my_time * units + jnp.minimum(jnp.arange(slots), units - 1)
    in_fibre = unit // channels
    in_channel = my_group * channels + unit % channels
    in_block = in_channel // BLK
    out_fibre = route_fibre[in_fibre, in_block]
    out_channel = route_slot[in_fibre, in_block] * BLK + in_channel % BLK
    real_slot = jnp.arange(slots) < units

    def wide(values):
        return jnp.broadcast_to(values.astype(jnp.float32)[..., None], values.shape + (FB,))

    def selection(fibre):
        chosen = (fibre[None, :] == jnp.arange(fibres)[:, None]) & real_slot[None, :]
        return wide(chosen)

    spans = []
    for span, (fibre, channel) in enumerate(((in_fibre, in_channel), (out_fibre, out_channel))):
        spread, strength = dispersion[span][fibre], nonlinearity[span][fibre]
        fc, fs = filter_tables(spread, channel, channels_total)
        spans.append((fc, fs, wide(strength), selection(fibre)))
    source_item, counts, take_from = route_tables(route_fibre, route_slot, groups, my_group, capacity)

    wave_bits = [times << b for b in range(groups.bit_length() - 1)]
    time_bits = [1 << b for b in range(times.bit_length() - 1)]
    wave_rounds = [(bit,) for bit in wave_bits]
    all_rounds = [(bit,) for bit in wave_bits + time_bits]
    shared = channels // units if same_fibre else 0
    fibre_bits = wave_bits + time_bits[: max(shared.bit_length() - 1, 0)]
    fibre_rounds = [tuple(fibre_bits[:1])]
    fibre_rounds += [tuple(fibre_bits[i : i + 2]) for i in range(1, len(fibre_bits), 2)]

    def natural_rows(values):
        split = values.reshape(fibres, channels, 2, 2, near, FB)
        return split.transpose(0, 1, 2, 4, 3, 5).reshape(-1, FB)

    strips = math.gcd(times, 4)
    in_hbm = pl.BlockSpec(memory_space=pltpu.HBM)
    natural = pltpu.with_memory_space_constraint(natural_rows(field), pltpu.HBM)
    shape = (times, 2 * near * rows, FB)
    packed = pl.pallas_call(
        functools.partial(pack_kernel, units=units, slots=slots, channels=channels),
        out_shape=pltpu.HBM(shape, jnp.float32),
        in_specs=[in_smem(), in_hbm],
        out_specs=in_hbm,
        scratch_shapes=[
            pltpu.VMEM(natural.shape, jnp.float32),
            pltpu.VMEM(shape, jnp.float32),
            pltpu.SemaphoreType.DMA((2, strips)),
        ],
        compiler_params=params(field.shape, shape),
        name="pack",
    )(lit_count, natural)
    wave_form = lax.all_to_all(packed, "tm", split_axis=0, concat_axis=0, tiled=True)
    wave_form = wave_form.reshape(chunks, 2, rows, FB)

    twist = jnp.asarray(twist_table())
    forward, inverse = (jnp.asarray(table) for table in matrix_tables())
    def dispersed(x, step, total, q_fibres, fibres_out, hold):
        fc, fs, _, select = spans[step // HALF]
        rotate = total is not None
        operands = [x]
        if rotate:
            operands += [total, spans[(step - 1) // HALF][3], spans[(step - 1) // HALF][2]]
        operands += [select, fc, fs, twist, forward, inverse]
        held = slots if hold else x.shape[2]
        shape = (chunks, 2, held, FB)
        leave, fetch = not rotate or hold, step == 1
        wave = (pltpu.HBM if leave else jax.ShapeDtypeStruct)(shape, jnp.float32)
        outs = [wave, jax.ShapeDtypeStruct((fibres_out, chunks, FB), jnp.float32)]
        outs += [pltpu.HBM(shape, jnp.float32)] if hold else []
        specs_in = [in_vmem()] * len(operands)
        specs_out = [in_vmem()] * len(outs)
        unroll = math.gcd(UNROLL, chunks // STEP)
        scratch = [pltpu.VMEM(shape, jnp.float32)] if rotate else []
        if leave:
            specs_out[0] = pl.BlockSpec(memory_space=pltpu.HBM)
            turns = chunks // STEP // unroll
            scratch += [pltpu.VMEM(shape, jnp.float32), pltpu.SemaphoreType.DMA((turns,))]
        if fetch:
            specs_in[0] = pl.BlockSpec(memory_space=pltpu.HBM)
            operands[0] = pltpu.with_memory_space_constraint(x, pltpu.HBM)
            scratch += [
                pltpu.VMEM(x.shape, jnp.float32),
                pltpu.SemaphoreType.DMA((math.gcd(4, chunks // STEP),)),
            ]
        scratch += step_scratch(held, unroll)
        return pl.pallas_call(
            functools.partial(
                step_kernel, rotate=rotate, hold=hold, fetch=fetch, leave=leave,
                channels_total=channels_total, fibres_in=q_fibres, fibres_out=fibres_out,
                slots=slots,
            ),
            out_shape=tuple(outs),
            in_specs=specs_in,
            out_specs=tuple(specs_out),
            scratch_shapes=scratch,
            compiler_params=params(*[x.shape] * 5, *[ref.shape for ref in scratch]),
            cost_estimate=cost(chunks * held * FB * 6400, 4 * x.size * 4),
            name="step",
        )(*operands)

    total, q_fibres = None, 0
    for step in range(2 * HALF - 1):
        fibres_out = 1 if (step < HALF and same_fibre) else fibres
        wave_form, partial = dispersed(wave_form, step, total, q_fibres, fibres_out, False)
        if fibres_out == 1:
            total = summed(partial, fibre_rounds)
        else:
            cut = fibres_out // 2
            there = all_rounds[:1] + all_rounds[2:] + all_rounds[1:2]
            back = all_rounds[:1] + all_rounds[:0:-1]
            total = jnp.concatenate(
                [summed(partial[:cut], there), summed(partial[cut:], back)], axis=0
            )
        q_fibres = fibres_out

    last = 2 * HALF - 1

    def to_times(values):
        values = values.reshape(times, 2 * near * slots, FB)
        return lax.all_to_all(values, "tm", split_axis=0, concat_axis=0, tiled=True)

    def prepared(values):
        block = pltpu.HBM((capacity, BLK * 2 * near, FB), jnp.float32)
        return pl.pallas_call(
            functools.partial(send_kernel, units=units, slots=slots),
            out_shape=(block,) * groups,
            in_specs=[in_smem(), in_smem(), in_vmem()],
            out_specs=(pl.BlockSpec(memory_space=pltpu.HBM),) * groups,
            scratch_shapes=[
                pltpu.VMEM((groups,) + block.shape, jnp.float32),
                pltpu.VMEM((times, slots, 2, near, FB), jnp.float32),
                pltpu.SemaphoreType.DMA((groups,)),
            ],
            compiler_params=params(values.shape, values.shape, (groups,) + block.shape),
            cost_estimate=cost(0, 4 * 4 * values.size),
            name="send",
        )(source_item, counts, values)

    def to_groups(outgoing):
        moved = [pltpu.with_memory_space_constraint(outgoing[0], pltpu.HBM)]
        for s in range(1, groups):
            moved.append(lax.ppermute(outgoing[s], "wave", [(i, i ^ s) for i in range(groups)]))
        return moved

    first, partial, rest = dispersed(wave_form, last, total, q_fibres, fibres, True)
    second, more = dispersed(rest, last, None, 0, fibres, False)
    bits = list(range(times.bit_length() - 1))
    partial = summed(partial + more, wave_rounds)
    partial = partial.reshape([fibres] + [2] * len(bits) + [near, FB])
    partial = time_parts(partial, bits[:1])
    first, partial = lax.optimization_barrier((to_times(first), partial))
    first = prepared(first)
    first, second = lax.optimization_barrier((first, second))
    second, *first = lax.optimization_barrier((to_times(second), *to_groups(first)))
    blocks = first + to_groups(prepared(second))
    for i in range(1, len(bits), 2):
        partial = time_parts(partial, bits[i : i + 2])
    own_total = partial.reshape(fibres, near, FB)
    strength = jnp.broadcast_to(nonlinearity[1][:, None, None], (fibres, near, FB))
    placed = pl.pallas_call(
        functools.partial(place_kernel, channels_total=channels_total, sources=groups),
        out_shape=pltpu.HBM((sends, BLK * 4 * near, FB), jnp.float32),
        in_specs=[in_smem(), in_vmem(), in_vmem()]
        + [pl.BlockSpec(memory_space=pl.ANY)] * (2 * groups),
        out_specs=in_hbm,
        scratch_shapes=[
            pltpu.VMEM((sends, BLK * 4 * near, FB), jnp.float32),
            pltpu.VMEM((2, groups * capacity, BLK * 2 * near, FB), jnp.float32),
            pltpu.SemaphoreType.DMA((2, groups)),
            pltpu.SemaphoreType.DMA((fibres,)),
        ],
        compiler_params=params(field.shape, field.shape, (2, groups * capacity, BLK * 2 * near, FB)),
        cost_estimate=cost(0, 4 * 4 * field.size),
        name="place",
    )(take_from, strength, own_total, *blocks)
    result = placed.reshape(fibres, channels, 2, near, 2, FB).transpose(0, 1, 2, 4, 3, 5)
    return result.reshape(fibres, channels, 2, 2, samples)


def solution(mesh):
    return jax.shard_map(
        local,
        mesh=mesh,
        in_specs=(P(None, "wave", None, None, "tm"), P(), P(), P(), P(), P()),
        out_specs=P(None, "wave", None, None, "tm"),
        check_vma=False,
    )
```
